32 devices in a mesh: dp: 8 (over z, core), fsdp: 4 (over y, x).
Axes of the slice: x: 2, y: 2, z: 4, core: 2. Of those that a mesh axis runs over, the one named last changes fastest.
Arguments:
- media: bfloat16 [64, 256, 1536], P(('dp', 'fsdp')), may hold values from -6 to 6
- latents: bfloat16 [64, 64, 1536], P(('dp', 'fsdp')), may hold values from -6 to 6
- upstream: bfloat16 [64, 64, 1536], P(('dp', 'fsdp')), may hold values from -6 to 6
- time_index: int32 [64], P(('dp', 'fsdp')), may hold values from 0 to 7
- live_count: int32 [32], P(('dp', 'fsdp')), may hold values from 0 to 2, as said below
- time_table: bfloat16 [8, 1536], P(None, ('dp', 'fsdp')), may hold values from -5 to 5
- media_gain: bfloat16 [1536], P(('dp', 'fsdp')), may hold values from 0.099609375 to 1.8984375
- media_bias: bfloat16 [1536], P(('dp', 'fsdp')), may hold values from -3 to 3
- latent_gain: bfloat16 [1536], P(('dp', 'fsdp')), may hold values from 0.099609375 to 1.8984375
- latent_bias: bfloat16 [1536], P(('dp', 'fsdp')), may hold values from -3 to 3
- ff_gain: bfloat16 [1536], P(('dp', 'fsdp')), may hold values from 0.099609375 to 1.8984375
- ff_bias: bfloat16 [1536], P(('dp', 'fsdp')), may hold values from -3 to 3
- w_query: bfloat16 [1536, 1536], P(('dp', 'fsdp')), may hold values from -0.15625 to 0.15625
- w_keyval: bfloat16 [1536, 3072], P(('dp', 'fsdp')), may hold values from -0.15625 to 0.15625
- w_out: bfloat16 [1536, 1536], P(('dp', 'fsdp')), may hold values from -0.625 to 0.625
- w_up: bfloat16 [1536, 6144], P(('dp', 'fsdp')), may hold values from -0.15625 to 0.15625
- w_down: bfloat16 [6144, 1536], P(('dp', 'fsdp')), may hold values from -0.078125 to 0.078125
Outputs:
- latents_out: bfloat16 [64, 64, 1536], P(('dp', 'fsdp'))
- media_grad: float32 [64, 256, 1536], P(('dp', 'fsdp'))
- latent_grad: float32 [64, 64, 1536], P(('dp', 'fsdp'))
- table_grad: float32 [8, 1536], P(None, ('dp', 'fsdp'))
- media_gain_grad: float32 [1536], P(('dp', 'fsdp'))
- media_bias_grad: float32 [1536], P(('dp', 'fsdp'))
- latent_gain_grad: float32 [1536], P(('dp', 'fsdp'))
- latent_bias_grad: float32 [1536], P(('dp', 'fsdp'))
- ff_gain_grad: float32 [1536], P(('dp', 'fsdp'))
- ff_bias_grad: float32 [1536], P(('dp', 'fsdp'))
- w_query_grad: float32 [1536, 1536], P(('dp', 'fsdp'))
- w_keyval_grad: float32 [1536, 3072], P(('dp', 'fsdp'))
- w_out_grad: float32 [1536, 1536], P(('dp', 'fsdp'))
- w_up_grad: float32 [1536, 6144], P(('dp', 'fsdp'))
- w_down_grad: float32 [6144, 1536], P(('dp', 'fsdp'))
The draws below stay inside these ranges and needn't reach their ends.
Inputs may be any that keep to these rules, and one draw needn't show every extreme that they name: live_count[i] images are live on device i, the devices ordered dp first; the counts sum to 32; a quarter of the devices hold 2 live images and another quarter none.
All inputs are finite; a program needn't handle non-finite values.
Results may differ from the reference program's by a relative error of at most 0.012.
Values may be sent and summed in bfloat16 or wider, within the bound.
No kernel may reach another device: no remote copies, remote signals or barrier semaphores. Data moves between devices by JAX's collectives and lax.ppermute only.
A program may use at most 320 MiB of HBM per device.

```python
import math
import jax
import jax.numpy as jnp
from jax import lax

D = 1536
HEADS = 16
HEAD = 96
FF = 6144
LATENTS = 64
PATCHES = 256
TMAX = 8
IMG_DEV = 1
CAP = 2
DEVICE_COUNT = 32
SLOTS = 64


def draw_live_count(key, part):
    key = jax.random.fold_in(key, 7)
    order = jax.random.permutation(key, DEVICE_COUNT)
    quarter = DEVICE_COUNT // 4
    ranks = jnp.arange(DEVICE_COUNT)
    by_rank = jnp.where(ranks < quarter, 2 * IMG_DEV, jnp.where(ranks < 2 * quarter, 0, IMG_DEV))
    counts = jnp.zeros((DEVICE_COUNT,), jnp.int32).at[order].set(by_rank.astype(jnp.int32))
    return counts


def set_ends(values, stream_key, smallest, top_value):
    longest = values.shape.index(max(values.shape))
    spots = []
    for shift in (0, 1):
        where = [jax.random.randint(jax.random.fold_in(stream_key, axis), (), 0, length) for axis, length in enumerate(values.shape)]
        where[longest] = (where[longest] + shift) % values.shape[longest]
        spots.append(tuple(where))
    return values.at[spots[0]].set(smallest).at[spots[1]].set(top_value)


def strengthened(drawn, stream_key, source, target, parts, factor):
    def block_of(position):
        return (jnp.arange(drawn.shape[position]) // (drawn.shape[position] // parts)).reshape((-1,) + (1,) * (drawn.ndim - 1 - position))

    near = jax.random.permutation(stream_key, parts)[block_of(target)]
    other_side = (block_of(target) + parts // 2) % parts
    return jnp.where((block_of(source) == near) | (block_of(source) == other_side), factor * drawn, drawn)


def shard_levels(own_key, shape, split, smallest, high):
    factor_of, own = 1.0, jax.random.fold_in(own_key, 6)
    for position, blocks in split:
        steps = jnp.exp(jax.random.uniform(jax.random.fold_in(own, position), (blocks,), jnp.float32, smallest / len(split), high / len(split)))
        factor_of = factor_of * jnp.repeat(steps, shape[position] // blocks).reshape([-1 if axis == position else 1 for axis in range(len(shape))])
    return factor_of


def scatter_about(key, dims, deviation, limit, shards=(), held_as=jnp.bfloat16):
    values = deviation * jax.random.normal(key, dims, jnp.float32)
    if shards:
        values = values * shard_levels(key, dims, shards, -0.22, 0.18)
    return jnp.clip(values, -limit, limit).astype(held_as)


def noise_with(key, extent, deviation, most, shards, heavy, held_as=jnp.bfloat16):
    values = deviation * jax.random.normal(key, extent, jnp.float32)
    if shards:
        values = values * shard_levels(key, extent, shards, -0.22, 0.18)
    return jnp.clip(strengthened(values, jax.random.fold_in(key, 3), *heavy), -most, most).astype(held_as)


def setup_inputs(seed: int = 0) -> dict:
    key_of = jax.random.split(jax.random.key(seed), 18)
    return {
        "media": noise_with(key_of[0], (SLOTS, PATCHES, D), 1.0, 6.0, ((0, 32),), (0, 2, 32, 2.75)),
        "latents": scatter_about(key_of[1], (SLOTS, LATENTS, D), 1.0, 6.0, ((0, 32),)),
        "upstream": scatter_about(key_of[2], (SLOTS, LATENTS, D), 1.0, 6.0, ((0, 32),)),
        "time_index": set_ends(jax.random.randint(key_of[3], (SLOTS,), 0, TMAX), jax.random.fold_in(key_of[3], 1), 0, TMAX - 1).astype(jnp.int32),
        "live_count": draw_live_count(jax.random.fold_in(key_of[17], 71), 0),
        "time_table": scatter_about(key_of[5], (TMAX, D), 1.0, 5.0, ((1, 32),)),
        "media_gain": jnp.clip(1.0 + 0.18 * jax.random.normal(key_of[6], (D,), jnp.float32), 0.099609375, 1.8984375).astype(jnp.bfloat16),
        "media_bias": scatter_about(key_of[7], (D,), 0.5, 3.0, ((0, 32),)),
        "latent_gain": jnp.clip(1.0 + 0.18 * jax.random.normal(key_of[8], (D,), jnp.float32), 0.099609375, 1.8984375).astype(jnp.bfloat16),
        "latent_bias": scatter_about(key_of[9], (D,), 0.5, 3.0, ((0, 32),)),
        "ff_gain": jnp.clip(1.0 + 0.18 * jax.random.normal(key_of[10], (D,), jnp.float32), 0.099609375, 1.8984375).astype(jnp.bfloat16),
        "ff_bias": scatter_about(key_of[11], (D,), 0.5, 3.0, ((0, 32),)),
        "w_query": scatter_about(key_of[12], (D, D), D ** -0.5, 0.15625, ((0, 32),)),
        "w_keyval": scatter_about(key_of[13], (D, 2 * D), D ** -0.5, 0.15625, ((0, 32),)),
        "w_out": scatter_about(key_of[14], (D, D), (D // 16) ** -0.5, 0.625, ((0, 32),)),
        "w_up": scatter_about(key_of[15], (D, FF), D ** -0.5, 0.15625, ((0, 32),)),
        "w_down": scatter_about(key_of[16], (FF, D), FF ** -0.5, 0.078125, ((0, 32),)),
    }


@jax.custom_vjp
def low(v):
    return lax.optimization_barrier(v.astype(jnp.bfloat16)).astype(jnp.float32)

@jax.custom_vjp
def low_back(v):
    return v

def low_keep(v):
    return (low(v), None)

def low_pass(kept, grad):
    return (grad,)

def back_keep(v):
    return (v, None)

def back_low(kept, grad):
    return (low(grad),)
low.defvjp(low_keep, low_pass)
low_back.defvjp(back_keep, back_low)
norm_eps = 1e-05
highest = lax.Precision.HIGHEST

def norm_rows(inputs, gain, shift):
    row_mean = lax.optimization_barrier(jnp.mean(inputs, axis=-1, keepdims=True))
    centered = inputs - row_mean
    variance = lax.optimization_barrier(jnp.mean(centered * centered, axis=-1, keepdims=True))
    return centered * lax.rsqrt(variance + norm_eps) * gain + shift

def project(left, right):
    return jnp.einsum('crd,de->cre', left, right, precision=highest)

def layer_forward(params, media_in, latents_in, one_hot):
    time_table, media_gain, media_bias, latent_gain, latent_bias, ff_gain, ff_bias, w_query, w_keyval, w_out, w_up, w_down = params
    images, patches, model_width = media_in.shape
    lat_rows = latents_in.shape[1]
    key_rows = patches + lat_rows
    scale = 1.0 / math.sqrt(HEAD)
    time_rows = jnp.dot(one_hot, time_table, precision=highest)
    media_norm = low(norm_rows(media_in + time_rows[:, None, :], media_gain, media_bias))
    latent_norm = low(norm_rows(latents_in, latent_gain, latent_bias))
    query_rows = low_back(low(project(latent_norm, w_query)))
    sources = jnp.concatenate([media_norm, latent_norm], axis=1)
    keyval = low_back(low(project(sources, w_keyval)))
    key_heads = keyval[:, :, :model_width].reshape(images, key_rows, HEADS, HEAD)
    value_heads = keyval[:, :, model_width:].reshape(images, key_rows, HEADS, HEAD)
    query_heads = query_rows.reshape(images, lat_rows, HEADS, HEAD)
    scores = low_back(jnp.einsum('cqhe,ckhe->chqk', query_heads, key_heads, precision=highest) * scale)
    row_top = lax.optimization_barrier(jnp.max(scores, axis=-1, keepdims=True))
    exps = jnp.exp(scores - row_top)
    attention = exps / lax.optimization_barrier(jnp.sum(exps, axis=-1, keepdims=True))
    mixed_rows = jnp.einsum('chqk,ckhe->cqhe', low(attention), value_heads, precision=highest)
    mixed_rows = low_back(low(mixed_rows.reshape(images, lat_rows, model_width)))
    middle = latents_in + low_back(project(mixed_rows, w_out))
    ffn_input = low(norm_rows(middle, ff_gain, ff_bias))
    pre_act = low_back(project(ffn_input, w_up))
    hidden = low(jax.nn.gelu(pre_act, approximate=False))
    return middle + low_back(project(hidden, w_down))

def reference(media, latents, upstream, time_index, live_count, time_table, media_gain, media_bias, latent_gain, latent_bias, ff_gain, ff_bias, w_query, w_keyval, w_out, w_up, w_down):
    params = tuple((weight.astype(jnp.float32) for weight in (time_table, media_gain, media_bias, latent_gain, latent_bias, ff_gain, ff_bias, w_query, w_keyval, w_out, w_up, w_down)))
    slot_count = media.shape[0]
    places = jnp.arange(slot_count) % CAP
    owners = jnp.repeat(live_count, CAP)
    alive = (places < owners).astype(jnp.float32)
    one_hot = (time_index[:, None] == jnp.arange(TMAX)[None, :]).astype(jnp.float32)
    group_size = math.gcd(slot_count, 16)
    block_count = slot_count // group_size

    def blocked(array):
        return array.reshape((block_count, group_size) + array.shape[1:])

    def block_step(totals, block):
        media_blk, latent_blk, upstream_blk, hot_blk, alive_blk = block

        def forward(weights, media_in, latents_in):
            return layer_forward(weights, media_in, latents_in, hot_blk)
        result, pullback = jax.vjp(forward, params, media_blk, latent_blk)
        live_mask = alive_blk[:, None, None]
        gradients, media_part, latent_part = pullback(upstream_blk * live_mask)
        totals = jax.tree.map(jnp.add, totals, gradients)
        return (totals, ((result * live_mask).astype(jnp.bfloat16), media_part, latent_part))
    initial = jax.tree.map(jnp.zeros_like, params)
    totals, outputs = lax.scan(block_step, initial, (blocked(media.astype(jnp.float32)), blocked(latents.astype(jnp.float32)), blocked(upstream.astype(jnp.float32)), blocked(one_hot), blocked(alive)))
    latents_out = outputs[0].reshape(latents.shape)
    media_grad = outputs[1].reshape(media.shape)
    latent_grad = outputs[2].reshape(latents.shape)
    return (latents_out, media_grad, latent_grad, totals[0], totals[1], totals[2], totals[3], totals[4], totals[5], totals[6], totals[7], totals[8], totals[9], totals[10], totals[11])
```

```python
import functools
import math

import jax
import jax.numpy as jnp
from jax import lax
from jax.sharding import PartitionSpec as P

HEAD = 96
AXES = ("dp", "fsdp")
LOW = jnp.bfloat16
WIDE = jnp.float32
HIGHEST = lax.Precision.HIGHEST
NORM_EPS = 1e-05


def norm_rows(inputs, gain, shift):
    row_mean = jnp.mean(inputs, axis=-1, keepdims=True)
    centered = inputs - row_mean
    variance = jnp.mean(centered * centered, axis=-1, keepdims=True)
    return centered * lax.rsqrt(variance + NORM_EPS) * gain + shift


def exact_gelu(inputs):
    return jax.nn.gelu(inputs, approximate=False)


def dot(left, right, contract):
    return lax.dot_general(left, right, (contract, ((), ())), preferred_element_type=WIDE)


def rows_by(left, right):
    return dot(left, right, ((left.ndim - 1,), (0,)))


def rows_back(left, right):
    return dot(left, right, ((left.ndim - 1,), (1,)))


def outer(left, right):
    return dot(left, right, ((0,), (0,)))


class Wires:
    def __init__(self, mesh):
        self.deep = mesh.shape["dp"] // 2
        self.flat = mesh.shape["fsdp"]
        self.count = 2 * self.deep * self.flat
        places = [
            (z, c, f) for z in range(self.deep) for c in range(2) for f in range(self.flat)
        ]

        def number(z, c, f):
            return (z * 2 + c) * self.flat + f

        def moves(target):
            return [(number(*place), number(*target(*place))) for place in places]

        self.bits = [1 << k for k in range(self.flat.bit_length() - 1)]
        self.swap = moves(lambda z, c, f: (z, 1 - c, f))
        self.rise = moves(lambda z, c, f: ((z + 1) % self.deep, c, f))
        self.cross = {
            mask: moves(lambda z, c, f, mask=mask: (z, c, f ^ mask)) for mask in range(1, self.flat)
        }

    def place(self):
        outer_at = lax.axis_index("dp")
        self.z, self.c = outer_at // 2, outer_at % 2
        self.f = lax.axis_index("fsdp")

    def send(self, block, moves):
        return lax.ppermute(block, AXES, moves)

    def plane(self, step):
        return lax.rem(self.z + self.deep - step, self.deep)

    def bit(self, mask):
        return (self.f // mask) % 2


def at(array, index, axis):
    return lax.dynamic_index_in_dim(array, index, axis, keepdims=False)


def put(array, block, where):
    shape = []
    left = list(block.shape)
    for entry in where:
        shape.append(left.pop(0) if entry is None else 1)
    block = block.reshape(tuple(shape) + tuple(left))
    start = [0 if entry is None else entry for entry in where] + [0] * len(left)
    return lax.dynamic_update_slice(array, block, start)


def pair(mine, other, side, axis):
    return jnp.where(
        side == 0, jnp.stack([mine, other], axis=axis), jnp.stack([other, mine], axis=axis)
    )


def gather_plane(wires, block, rising, store):
    bits = wires.bits if rising else wires.bits[::-1]
    current = block
    for done, mask in enumerate(bits):
        arrived = wires.send(current, wires.cross[mask])
        side = wires.bit(mask)
        if done == len(bits) - 1:
            free = [None] * done
            for half, at_side in ((current, side), (arrived, 1 - side)):
                store(half, [at_side, *free] if rising else [*free, at_side])
        else:
            current = pair(current, arrived, side, 0 if rising else done)


def scatter_plane(wires, partial, rising):
    bits = list(wires.bits)
    order = bits if rising else bits[::-1]
    current, axes = partial, bits[::-1]
    for mask in order:
        axis = axes.index(mask)
        side = wires.bit(mask)
        leave = at(current, 1 - side, axis).astype(LOW)
        arrived = wires.send(leave, wires.cross[mask])
        current = at(current, side, axis).astype(WIDE) + arrived.astype(WIDE)
        axes.pop(axis)
    return current


def spread_rows(wires, block):
    parts = []
    for half, order in ((block[0], wires.bits), (block[1], wires.bits[::-1])):
        current = half[None]
        for mask in order:
            arrived = wires.send(current, wires.cross[mask])
            axis_new = jnp.stack([current, arrived], axis=1 if order is wires.bits else 0)
            current = (
                jnp.concatenate([current, arrived], axis=0)
                if order is wires.bits
                else axis_new.swapaxes(0, 1).reshape((-1,) + half.shape)
            )
        parts.append(current)
    own = jnp.stack(parts, axis=1)
    other = wires.send(own, wires.swap)
    return jnp.stack([own, other], axis=0)


def collect_rows(wires, partial):
    arrived = wires.send(partial[1].astype(LOW), wires.swap)
    both = partial[0] + arrived.astype(WIDE)
    halves = []
    for half, order in ((both[:, 0], wires.bits[::-1]), (both[:, 1], wires.bits)):
        shape = half.shape[1:]
        current = half.reshape((2,) * len(wires.bits) + shape)
        axes = wires.bits[::-1]
        for mask in order:
            axis = axes.index(mask)
            leave = lax.index_in_dim(current, 1, axis, keepdims=False).astype(LOW)
            arrived = wires.send(leave, wires.cross[mask])
            current = lax.index_in_dim(current, 0, axis, keepdims=False) + arrived.astype(WIDE)
            axes = [a for a in axes if a != mask]
        halves.append(current)
    return jnp.stack(halves, axis=0)


def gather_planes(wires, block):
    current = block
    for step in range(wires.deep):
        if step:
            current = wires.send(current, wires.rise)
        yield current, wires.plane(step)


def scatter_planes(wires, term):
    total = term(wires.plane(1)).astype(WIDE)
    for step in range(1, wires.deep):
        arrived = wires.send(total.astype(LOW), wires.rise)
        total = term(wires.plane(1 + step)).astype(WIDE) + arrived.astype(WIDE)
    return total


def on_device(
    wires,
    media,
    latents,
    upstream,
    time_index,
    live_count,
    time_table,
    media_gain,
    media_bias,
    latent_gain,
    latent_bias,
    ff_gain,
    ff_bias,
    w_query,
    w_keyval,
    w_out,
    w_up,
    w_down,
):
    wires.place()
    deep, flat, count = wires.deep, wires.flat, wires.count
    images, patches, model_width = media.shape
    lat_rows = latents.shape[1]
    key_rows = patches + lat_rows
    scale = 1.0 / math.sqrt(HEAD)
    table_rows, shard = time_table.shape
    group = model_width // (2 * deep)
    half_width = model_width // 2
    heads = half_width // HEAD
    bit_dims = (2,) * len(wires.bits)
    slots = 2 * images

    columns = jnp.concatenate([w_query, w_keyval], axis=1).reshape(shard, 3 * deep, 2, group)
    qkv_mine = at(columns, wires.c, 2).reshape(shard, 3 * half_width)
    qkv_other = at(columns, 1 - wires.c, 2).reshape(shard, 3 * half_width)
    qkv_arrived = wires.send(qkv_other, wires.swap)
    qkv_block = pair(qkv_mine, qkv_arrived, wires.c, 0)
    qkv_full = jnp.zeros((deep, 2) + bit_dims + (shard, 3 * half_width), LOW)
    box = [qkv_full]
    for block, plane in gather_planes(wires, qkv_block):
        for core in range(2):

            def store(half, where, core=core, plane=plane):
                box[0] = put(box[0], half, [plane, core, *where])

            gather_plane(wires, block[core], core == 0, store)
    qkv_full = box[0].reshape(model_width, 3 * half_width)
    query_full, keyval_full = qkv_full[:, :half_width], qkv_full[:, half_width:]

    smalls = jnp.concatenate(
        [time_table]
        + [
            v[None]
            for v in (media_gain, media_bias, latent_gain, latent_bias, ff_gain, ff_bias)
        ],
        axis=0,
    )
    smalls = jnp.broadcast_to(smalls[None], (count,) + smalls.shape)
    smalls = lax.all_to_all(smalls, AXES, 0, 0, tiled=True)
    smalls = smalls.transpose(1, 0, 2).reshape(-1, model_width).astype(WIDE)
    table_full = smalls[:table_rows]
    (
        media_gain_full,
        media_bias_full,
        latent_gain_full,
        latent_bias_full,
        ff_gain_full,
        ff_bias_full,
    ) = [smalls[table_rows + k] for k in range(6)]

    alive = (jnp.arange(images) < live_count[0]).astype(WIDE)
    live_mask = alive[:, None, None]
    one_hot = (time_index[:, None] == jnp.arange(table_rows)[None, :]).astype(WIDE)
    time_rows = jnp.dot(one_hot, table_full, precision=HIGHEST)
    media_in = media.astype(WIDE) + time_rows[:, None, :]
    media_normed, media_norm_back = jax.vjp(norm_rows, media_in, media_gain_full, media_bias_full)
    latents_wide = latents.astype(WIDE)
    latent_normed, latent_norm_back = jax.vjp(
        norm_rows, latents_wide, latent_gain_full, latent_bias_full
    )
    own_sources = jnp.concatenate([media_normed.astype(LOW), latent_normed.astype(LOW)], axis=1)
    sources = jnp.concatenate([own_sources, wires.send(own_sources, wires.swap)], axis=0)
    latent_norm = sources[:, patches:, :]

    down_full = jnp.zeros((deep,) + w_down.shape, LOW)
    for block, plane in gather_planes(wires, w_down):
        down_full = put(down_full, block, [plane])
    hidden_units = deep * w_down.shape[0]
    down_full = down_full.reshape(hidden_units, model_width)
    unit = w_down.shape[0]
    up_shards = w_up.reshape(shard, deep, 2, flat, unit)
    up_mine = at(up_shards, wires.c, 2)
    up_other = wires.send(at(up_shards, 1 - wires.c, 2), wires.swap)
    up_pair = pair(up_mine, up_other, wires.c, 0)
    up_block = jnp.zeros((2, flat, shard, hidden_units), LOW)
    for mask in range(flat):
        target = wires.f ^ mask
        part = at(up_pair, target, 3).reshape(2, shard, hidden_units)
        if mask:
            part = wires.send(part, wires.cross[mask])
        up_block = put(up_block, part, [None, target])
    up_full = jnp.zeros((deep, 2 * flat * shard, hidden_units), LOW)
    up_block = up_block.reshape(2 * flat * shard, hidden_units)
    for block, plane in gather_planes(wires, up_block):
        up_full = put(up_full, block, [plane])
    up_full = up_full.reshape(model_width, hidden_units)

    out_full = jnp.zeros((deep,) + bit_dims + (shard, model_width), LOW)
    out_column = jnp.zeros((deep, shard, model_width), LOW)
    for block, plane in gather_planes(wires, w_out):
        out_column = put(out_column, block, [plane])
    out_box = [jnp.zeros(bit_dims + (deep, 2, shard, half_width), LOW)]
    for side in range(2):

        def store_out(half, where, side=side):
            out_box[0] = put(out_box[0], half, [*where, None, side])

        gather_plane(
            wires, out_column[:, :, side * half_width : (side + 1) * half_width], side == 0, store_out
        )
    out_full = (
        out_box[0]
        .reshape(flat, deep, 2, shard, half_width)
        .transpose(1, 0, 3, 2, 4)
        .reshape(half_width, model_width)
    )

    query_rows = rows_by(latent_norm, query_full).astype(LOW)
    keyval = rows_by(sources, keyval_full).astype(LOW)
    key_heads = keyval[:, :, :half_width].reshape(slots, key_rows, heads, HEAD)
    value_heads = keyval[:, :, half_width:].reshape(slots, key_rows, heads, HEAD)
    query_heads = query_rows.reshape(slots, lat_rows, heads, HEAD)
    raw = jnp.einsum("cqhe,ckhe->ckhq", query_heads, key_heads, preferred_element_type=WIDE)
    scores = (raw * scale).reshape(slots, key_rows, heads * lat_rows)
    row_top = jnp.max(scores, axis=1, keepdims=True)
    exps = jnp.exp(scores - row_top)
    attention = exps / jnp.sum(exps, axis=1, keepdims=True)
    attention_low = attention.reshape(slots, key_rows, heads, lat_rows).astype(LOW)
    mixed = jnp.einsum("ckhq,ckhe->cqhe", attention_low, value_heads, preferred_element_type=WIDE)
    mixed = mixed.reshape(slots, lat_rows, half_width).astype(LOW)
    branch = rows_by(mixed, out_full)
    branch = branch[:images] + wires.send(branch[images:], wires.swap)
    middle = latents_wide + branch

    ffn_normed, ffn_norm_back = jax.vjp(norm_rows, middle, ff_gain_full, ff_bias_full)
    d_out = upstream.astype(WIDE) * live_mask
    plane_shape = (2, flat, images, lat_rows, model_width)
    d_out_rows = spread_rows(wires, d_out.astype(LOW)).reshape(-1, model_width)
    ffn_rows = spread_rows(wires, ffn_normed.astype(LOW)).reshape(-1, model_width)
    pre_act = rows_by(ffn_rows, up_full)
    activated, gelu_back = jax.vjp(exact_gelu, pre_act)
    hidden = activated.astype(LOW)
    d_hidden = rows_back(d_out_rows, down_full)
    (d_pre,) = gelu_back(d_hidden)
    d_pre_low = d_pre.astype(LOW)
    d_ffn_input = collect_rows(wires, rows_back(d_pre_low, up_full).reshape(plane_shape))
    d_middle_norm, ff_gain_grad, ff_bias_grad = ffn_norm_back(d_ffn_input)
    d_middle = d_out + d_middle_norm
    result = middle + collect_rows(wires, rows_by(hidden, down_full).reshape(plane_shape))
    latents_out = (result * live_mask).astype(LOW)

    down_partial = outer(hidden, d_out_rows).astype(LOW).reshape(deep, unit, model_width)
    w_down_grad = scatter_planes(wires, lambda plane: at(down_partial, plane, 0))
    up_partial = outer(ffn_rows, d_pre_low).astype(LOW)
    up_partial = up_partial.reshape(deep, 2, flat, shard, hidden_units)
    up_sum = scatter_planes(wires, lambda plane: at(up_partial, plane, 0)).astype(LOW)
    up_grad = jnp.zeros((2, shard, deep, flat, unit), LOW)
    for mask in range(flat):
        target = wires.f ^ mask
        part = at(up_sum, target, 1).reshape(2, shard, deep, unit)
        if mask:
            part = wires.send(part, wires.cross[mask])
        up_grad = put(up_grad, part, [None, None, None, target])
    up_mine = at(up_grad, wires.c, 0)
    up_other = wires.send(at(up_grad, 1 - wires.c, 0), wires.swap)
    w_up_grad = pair(up_mine, up_other, wires.c, 2).reshape(w_up.shape).astype(WIDE)

    own_branch = d_middle.astype(LOW)
    d_branch = jnp.concatenate([own_branch, wires.send(own_branch, wires.swap)], axis=0)
    d_mixed = rows_back(d_branch, out_full).astype(LOW)
    out_partial = outer(mixed.reshape(-1, half_width), d_branch.reshape(-1, model_width))
    out_partial = out_partial.astype(LOW).reshape((deep,) + bit_dims + (shard, model_width))
    d_mixed_heads = d_mixed.reshape(slots, lat_rows, heads, HEAD)
    d_attention = jnp.einsum(
        "cqhe,ckhe->ckhq", d_mixed_heads, value_heads, preferred_element_type=WIDE
    )
    d_attention = d_attention.reshape(slots, key_rows, heads * lat_rows)
    d_values = jnp.einsum(
        "ckhq,cqhe->ckhe", attention_low, d_mixed_heads, preferred_element_type=WIDE
    )
    row_delta = jnp.sum(attention * d_attention, axis=1, keepdims=True)
    d_scores = (attention * (d_attention - row_delta)).reshape(slots, key_rows, heads, lat_rows)
    d_scores = d_scores.astype(LOW)
    d_query = jnp.einsum("ckhq,ckhe->cqhe", d_scores, key_heads, preferred_element_type=WIDE)
    d_query = (d_query * scale).reshape(slots, lat_rows, half_width).astype(LOW)
    d_keys = jnp.einsum("ckhq,cqhe->ckhe", d_scores, query_heads, preferred_element_type=WIDE)
    d_keyval = jnp.concatenate(
        [
            (d_keys * scale).reshape(slots, key_rows, half_width),
            d_values.reshape(slots, key_rows, half_width),
        ],
        axis=2,
    ).astype(LOW)

    query_partial = outer(latent_norm.reshape(-1, model_width), d_query.reshape(-1, half_width))
    keyval_partial = outer(sources.reshape(-1, model_width), d_keyval.reshape(-1, model_width))
    qkv_partial = jnp.concatenate([query_partial.astype(LOW), keyval_partial.astype(LOW)], axis=1)
    qkv_partial = qkv_partial.reshape((deep, 2) + bit_dims + (shard, 3 * half_width))

    def qkv_term(plane):
        block = at(qkv_partial, plane, 0)
        return jnp.stack([scatter_plane(wires, block[core], core == 0) for core in range(2)])

    qkv_sum = scatter_planes(wires, qkv_term)
    qkv_own = at(qkv_sum, wires.c, 0)
    qkv_far = wires.send(at(qkv_sum, 1 - wires.c, 0), wires.swap)
    halves = [part.reshape(shard, 3 * deep, group) for part in (qkv_own, qkv_far)]
    qkv_grad = pair(halves[0], halves[1], wires.c, 2).reshape(shard, 3 * model_width)
    w_query_grad, w_keyval_grad = qkv_grad[:, :model_width], qkv_grad[:, model_width:]

    def out_term(side):
        return scatter_plane(
            wires,
            jnp.moveaxis(out_partial, 0, len(bit_dims))[
                ..., side * half_width : (side + 1) * half_width
            ],
            side == 0,
        )

    out_sums = jnp.concatenate([out_term(side) for side in range(2)], axis=-1)
    w_out_grad = scatter_planes(wires, lambda plane: at(out_sums, plane, 0))

    d_sources = rows_back(d_keyval, keyval_full)
    d_latent_part = rows_back(d_query, query_full) + d_sources[:, patches:, :]
    d_sources = jnp.concatenate([d_sources[:, :patches, :], d_latent_part], axis=1)
    d_sources = d_sources[:images] + wires.send(d_sources[images:], wires.swap)
    d_latent_in, latent_gain_grad, latent_bias_grad = latent_norm_back(d_sources[:, patches:, :])
    media_grad, media_gain_grad, media_bias_grad = media_norm_back(d_sources[:, :patches, :])
    latent_grad = d_middle + d_latent_in
    table_part = jnp.dot(one_hot.T, jnp.sum(media_grad, axis=1), precision=HIGHEST)

    small_grads = jnp.concatenate(
        [table_part]
        + [
            v[None]
            for v in (
                media_gain_grad,
                media_bias_grad,
                latent_gain_grad,
                latent_bias_grad,
                ff_gain_grad,
                ff_bias_grad,
            )
        ],
        axis=0,
    )
    small_grads = small_grads.reshape(-1, count, shard).transpose(1, 0, 2)
    small_grads = lax.all_to_all(small_grads, AXES, 0, 0, tiled=True)
    small_grads = jnp.sum(small_grads, axis=0)
    return (
        latents_out,
        media_grad,
        latent_grad,
        small_grads[:table_rows],
        *[small_grads[table_rows + k] for k in range(6)],
        w_query_grad,
        w_keyval_grad,
        w_out_grad,
        w_up_grad,
        w_down_grad,
    )


def solution(mesh):
    lead = P(AXES)
    table = P(None, AXES)
    return jax.shard_map(
        functools.partial(on_device, Wires(mesh)),
        mesh=mesh,
        in_specs=(lead,) * 5 + (table,) + (lead,) * 11,
        out_specs=(lead,) * 3 + (table,) + (lead,) * 11,
        check_vma=False,
    )
```

```python
import functools
import math

import jax
import jax.numpy as jnp
from jax import lax
from jax.experimental import pallas as pl
from jax.experimental.pallas import tpu as pltpu
from jax.sharding import PartitionSpec as P

HEAD = 96
PACK = 4
AXES = ("dp", "fsdp")
LOW = jnp.bfloat16
WIDE = jnp.float32
HIGHEST = lax.Precision.HIGHEST
NORM_EPS = 1e-05


def norm_rows(inputs, gain, shift):
    row_mean = jnp.mean(inputs, axis=-1, keepdims=True)
    centered = inputs - row_mean
    variance = jnp.mean(centered * centered, axis=-1, keepdims=True)
    return centered * lax.rsqrt(variance + NORM_EPS) * gain + shift


def exact_gelu(inputs):
    return jax.nn.gelu(inputs, approximate=False)


def dot(left, right, contract):
    return lax.dot_general(left, right, (contract, ((), ())), preferred_element_type=WIDE)


def rows_by(left, right):
    return dot(left, right, ((left.ndim - 1,), (0,)))


def rows_back(left, right):
    return dot(left, right, ((left.ndim - 1,), (1,)))


def outer(left, right):
    return dot(left, right, ((0,), (0,)))


class Wires:
    def __init__(self, mesh):
        self.deep = mesh.shape["dp"] // 2
        self.flat = mesh.shape["fsdp"]
        self.count = 2 * self.deep * self.flat
        places = [
            (z, c, f) for z in range(self.deep) for c in range(2) for f in range(self.flat)
        ]

        def number(z, c, f):
            return (z * 2 + c) * self.flat + f

        def moves(target):
            return [(number(*place), number(*target(*place))) for place in places]

        self.bits = [1 << k for k in range(self.flat.bit_length() - 1)]
        self.masks = list(range(1, self.flat))
        self.moves = {
            "core": moves(lambda z, c, f: (z, 1 - c, f)),
        }
        self.moves["rise"] = moves(lambda z, c, f: ((z + 1) % self.deep, c, f))
        self.columns = [
            [number(z, c, f) for z in range(self.deep)] for c in range(2) for f in range(self.flat)
        ]
        self.planes = [
            [number(z, c, f) for c in range(2) for f in range(self.flat)] for z in range(self.deep)
        ]
        for mask in self.masks:
            self.moves[mask] = moves(lambda z, c, f, mask=mask: (z, c, f ^ mask))

    def place(self):
        outer_at = lax.axis_index("dp")
        self.z, self.c = outer_at // 2, outer_at % 2
        self.f = lax.axis_index("fsdp")
        self.queues = {}

    def send(self, block, kind, *ahead):
        if ahead:
            block = after(block, *ahead)
        return lax.ppermute(block, AXES, self.moves[kind])

    def swap_blocks(self, blocks, groups):
        return lax.all_to_all(blocks, AXES, 0, 0, tiled=True, axis_index_groups=groups)

    def plane(self, step):
        return lax.rem(self.z + 2 * self.deep - step, self.deep)


def after(block, *others):
    return lax.optimization_barrier((block, *others))[0]


def at(array, index, axis):
    return lax.dynamic_index_in_dim(array, index, axis, keepdims=False)


def pair(mine, other, side, axis):
    return jnp.where(
        side == 0, jnp.stack([mine, other], axis=axis), jnp.stack([other, mine], axis=axis)
    )


def pick(array, side, axis):
    return jnp.where(
        side == 0,
        lax.index_in_dim(array, 0, axis, keepdims=False),
        lax.index_in_dim(array, 1, axis, keepdims=False),
    )


def corner(mask):
    return mask & -mask, 1 << (mask.bit_length() - 1)


def gather_rows(wires, block, take, guest, hooks):
    rings, gathered, before, guests = [block], [], (), {0: guest}
    single = [mask for mask in wires.masks if not mask & (mask - 1)]
    multiple = sorted((m for m in wires.masks if m & (m - 1)), key=lambda m: bin(m).count("1"))
    steps = []
    for step in range(wires.deep + 1):
        now = []
        before = (*before, *(hooks[step](guests) if step in hooks else ()))
        if step < wires.deep:
            if step + 1 < wires.deep:
                rings.append(wires.send(rings[step], "rise", *before))
                now.append(rings[-1])
            mine = take(rings[step])
            got = {0: mine}
            for mask in single:
                got[mask] = wires.send(mine, mask, *before)
                now.append(got[mask])
            gathered.append(got)
        for mask in single if step == 0 else multiple if step == wires.deep - 1 else ():
            guests[mask] = wires.send(guest, mask, *before)
            if step == 0:
                now.append(guests[mask])
        if step:
            got = gathered[step - 1]
            for mask in multiple:
                low, high = corner(mask)
                got[mask] = (
                    wires.send(got[mask ^ high][0], high, *before),
                    wires.send(got[mask ^ low][1], low, *before),
                )
                now += got[mask]
        before = now
        steps.append(now)
    return rings, gathered, guests, steps


def scatter_rows(wires, part, pulls):
    single = [mask for mask in wires.masks if not mask & (mask - 1)]
    multiple = sorted((m for m in wires.masks if m & (m - 1)), key=lambda m: -bin(m).count("1"))
    extra = [{} for _ in range(wires.deep)]
    before, total = [None], None
    for step in range(wires.deep + 2):
        now = []
        ahead = (*(before if step else ()), *(pulls[step](before[-1]) if step in pulls else ()))

        def term(block, mask, half=None):
            mine = part(block, mask)
            if half is not None:
                mine = mine[half]
            more = extra[block].get((mask, half), [])
            return sum([m.astype(WIDE) for m in more], mine).astype(LOW)

        block = step - 2
        if 0 <= block:
            total = (
                sum([m.astype(WIDE) for m in extra[block][0, None]], part(block, 0).astype(WIDE))
                + (0.0 if total is None else total)
            )
            if block == wires.deep - 1:
                return total
            arrived = wires.send(total.astype(LOW), "rise", *ahead)
            now.append(arrived)
            total = arrived.astype(WIDE)
        block = step - 1
        if 0 <= block < wires.deep:
            for mask in single:
                halves = [term(block, mask, half) for half in range(2)]
                arrived = wires.send(jnp.stack(halves), mask, *ahead)
                extra[block].setdefault((0, None), []).append(arrived)
                now.append(arrived)
        if step < wires.deep:
            for mask in multiple:
                low, high = corner(mask)
                for half, bit in ((0, high), (1, low)):
                    arrived = wires.send(term(step, mask, half), bit, *ahead)
                    extra[step].setdefault((mask ^ bit, half), []).append(arrived)
                    now.append(arrived)
        before = now


def spread_plane(wires, block, *ahead):
    got = {0: block}
    for mask in reversed(wires.masks):
        got[mask] = wires.send(block, mask, *ahead)
    return got


def sum_plane(wires, part, *ahead):
    arrived = [wires.send(part(mask).astype(LOW), mask, *ahead) for mask in reversed(wires.masks)]
    return sum([block.astype(WIDE) for block in arrived], part(0).astype(WIDE)), arrived


def lay(places, pieces, count):
    entry = pieces[0].shape[1:]
    views = [(k, i) for k, piece in enumerate(pieces) for i in range(piece.shape[0])]
    number = len(views)

    def kernel(places_ref, *refs):
        out_ref, held, sems = refs[-3:]
        loads = [
            pltpu.make_async_copy(refs[k].at[i], held.at[n], sems.at[0, n])
            for n, (k, i) in enumerate(views)
        ]
        stores = [
            pltpu.make_async_copy(held.at[n], out_ref.at[places_ref[n]], sems.at[1, n])
            for n in range(number)
        ]
        for load in loads:
            load.start()
        for load, store in zip(loads, stores, strict=True):
            load.wait()
            store.start()
        for store in stores:
            store.wait()

    anywhere = pl.BlockSpec(memory_space=pl.ANY)
    return pl.pallas_call(
        kernel,
        out_shape=jax.ShapeDtypeStruct((count,) + entry, pieces[0].dtype),
        in_specs=[pl.BlockSpec(memory_space=pltpu.SMEM)] + [anywhere] * len(pieces),
        out_specs=anywhere,
        scratch_shapes=[
            pltpu.VMEM((number,) + entry, pieces[0].dtype),
            pltpu.SemaphoreType.DMA((2, number)),
        ],
        compiler_params=pltpu.CompilerParams(vmem_limit_bytes=16 * 2**20),
    )(jnp.stack(places).astype(jnp.int32), *pieces)


def whole_tiles(rows):
    return rows % 16 == 0


def joined(places, pieces):
    shard = pieces[0].shape[-2]
    if whole_tiles(shard):
        return places, pieces
    rows = [row for piece in pieces for row in (piece if piece.ndim == 3 else (piece,))]
    full = jnp.zeros((len(rows), *rows[0].shape), rows[0].dtype)
    for place, row in zip(places, rows, strict=True):
        full = lax.dynamic_update_index_in_dim(full, row, place, 0)
    return [jnp.zeros((), jnp.int32)], [full.reshape(1, len(rows) * shard, -1)]


def on_chip(kernel, out_shape, side, *operands):
    whole = pl.BlockSpec(memory_space=pltpu.VMEM)
    return pl.pallas_call(
        kernel,
        out_shape=out_shape,
        in_specs=[pl.BlockSpec(memory_space=pltpu.SMEM)] + [whole] * len(operands),
        out_specs=jax.tree.map(lambda _: whole, out_shape),
    )(side.reshape(1).astype(jnp.int32), *operands)


def deal_columns(side, arrays, group):
    shard = arrays[0].shape[0]
    width = sum(array.shape[1] for array in arrays) // 2
    if not whole_tiles(shard):
        both = jnp.concatenate(arrays, axis=1).reshape(shard, -1, 2, group)
        return tuple(pick(both, s, 2).reshape(shard, width) for s in (side, 1 - side))

    def kernel(side_ref, *refs):
        *in_refs, own_ref, other_ref = refs
        first = side_ref[0] == 0
        base = 0
        for ref in in_refs:
            block = ref[...]
            count = block.shape[1] // (2 * group)
            hands = [
                jnp.concatenate(
                    [block[:, (2 * j + s) * group : (2 * j + s + 1) * group] for j in range(count)],
                    axis=1,
                )
                for s in range(2)
            ]
            own_ref[:, base : base + count * group] = jnp.where(first, hands[0], hands[1])
            other_ref[:, base : base + count * group] = jnp.where(first, hands[1], hands[0])
            base += count * group

    shape = jax.ShapeDtypeStruct((shard, width), arrays[0].dtype)
    return on_chip(kernel, (shape, shape), side, *arrays)


def join_columns(side, own, other, widths, group):
    shard = own.shape[0]
    if not whole_tiles(shard):
        halves = [part.reshape(shard, -1, group) for part in (own, other)]
        both = pair(halves[0], halves[1], side, 2).reshape(shard, -1)
        return tuple(jnp.split(both, [widths[0]], axis=1))

    def kernel(side_ref, own_ref, other_ref, *out_refs):
        first = side_ref[0] == 0
        hands = (
            jnp.where(first, own_ref[...], other_ref[...]),
            jnp.where(first, other_ref[...], own_ref[...]),
        )
        base = 0
        for ref in out_refs:
            parts = []
            for j in range(ref.shape[1] // (2 * group)):
                columns = slice(base + j * group, base + (j + 1) * group)
                parts += [hand[:, columns] for hand in hands]
            ref[...] = jnp.concatenate(parts, axis=1)
            base += ref.shape[1] // 2

    shapes = tuple(jax.ShapeDtypeStruct((own.shape[0], width), own.dtype) for width in widths)
    return on_chip(kernel, shapes, side, own, other)


def split_units(array, ways, unit):
    shard, width = array.shape
    deep = width // (ways * unit)
    if not whole_tiles(shard):
        blocks = array.reshape(shard, deep, ways, unit).transpose(2, 0, 1, 3)
        return blocks.reshape(ways, shard, deep * unit)

    def kernel(_, in_ref, out_ref):
        block = in_ref[...]
        for way in range(ways):
            parts = [
                block[:, (z * ways + way) * unit : (z * ways + way + 1) * unit] for z in range(deep)
            ]
            out_ref[way] = jnp.concatenate(parts, axis=1)

    shape = jax.ShapeDtypeStruct((ways, shard, deep * unit), array.dtype)
    return on_chip(kernel, shape, jnp.zeros((), jnp.int32), array)


def merge_units(blocks, unit):
    ways, shard, part = blocks.shape
    deep = part // unit
    if not whole_tiles(shard):
        blocks = blocks.reshape(ways, shard, deep, unit).transpose(1, 2, 0, 3)
        return blocks.reshape(shard, -1).astype(WIDE)

    def kernel(_, in_ref, out_ref):
        parts = []
        for z in range(deep):
            for way in range(ways):
                parts.append(in_ref[way][:, z * unit : (z + 1) * unit].astype(WIDE))
        out_ref[...] = jnp.concatenate(parts, axis=1)

    shape = jax.ShapeDtypeStruct((shard, deep * ways * unit), WIDE)
    return on_chip(kernel, shape, jnp.zeros((), jnp.int32), blocks)


def tile_heads(rows, mask):
    return jnp.concatenate([rows] * PACK, axis=0) * mask


def untile_heads(rows, mask):
    kept = rows * mask
    size = rows.shape[0] // PACK
    return sum(kept[k * size : (k + 1) * size] for k in range(PACK))


def head_mask(rows, dtype):
    row = lax.broadcasted_iota(jnp.int32, (PACK * rows, PACK * HEAD), 0) // rows
    column = lax.broadcasted_iota(jnp.int32, (PACK * rows, PACK * HEAD), 1) // HEAD
    return (row == column).astype(WIDE).astype(dtype)


def attend(places, pieces, own, far, patches, half_width):
    images, key_rows, model_width = own.shape
    slots = 2 * images
    lat_rows = key_rows - patches
    width = 3 * half_width
    places, pieces = joined(places, pieces)
    chunk = PACK * HEAD
    groups = half_width // chunk
    scale = 1.0 / math.sqrt(HEAD)
    shard = pieces[0].shape[-2]
    views = []
    for k, piece in enumerate(pieces):
        views += [(k, None)] if piece.ndim == 2 else [(k, core) for core in range(piece.shape[0])]

    def kernel(places_ref, *refs):
        piece_refs = refs[: len(pieces)]
        (
            own_ref,
            far_ref,
            full_ref,
            query_ref,
            keyval_ref,
            probs_ref,
            mixed_ref,
            w_ref,
            sems,
        ) = refs[len(pieces) :]
        slot = pl.program_id(0)

        def save():
            return pltpu.make_async_copy(w_ref, full_ref, sems.at[len(views)])

        @pl.when(slot == 0)
        def _():
            loads = []
            for i, (k, core) in enumerate(views):
                source = piece_refs[k] if core is None else piece_refs[k].at[core]
                start = pl.multiple_of(places_ref[i] * shard, shard)
                loads.append(
                    pltpu.make_async_copy(source, w_ref.at[pl.ds(start, shard)], sems.at[i])
                )
            for load in loads:
                load.start()
            for load in loads:
                load.wait()
            save().start()

        x = jnp.where(slot < images, own_ref[0], far_ref[0])
        mask_low, mask_wide = head_mask(lat_rows, LOW), head_mask(lat_rows, WIDE)

        def project(rows, part):
            w = w_ref[:, part * chunk : (part + 1) * chunk]
            return jnp.dot(rows, w, preferred_element_type=WIDE).astype(LOW)

        for part in range(groups):
            columns = slice(part * chunk, (part + 1) * chunk)
            query = project(x[patches:], part)
            query_ref[0, :, columns] = query
            k = project(x, groups + part)
            keyval_ref[0, :, columns] = k
            v = project(x, 2 * groups + part)
            keyval_ref[0, :, half_width + part * chunk : half_width + (part + 1) * chunk] = v
            s = dot(tile_heads(query, mask_low), k, ((1,), (1,)))
            e = jnp.exp((s - jnp.max(s, axis=1, keepdims=True)) * scale)
            p = e * (1.0 / jnp.sum(e, axis=1, keepdims=True))
            probs_ref[0, part] = p
            m = jnp.dot(p.astype(LOW), v, preferred_element_type=WIDE)
            mixed_ref[0, :, columns] = untile_heads(m, mask_wide).astype(LOW)

        @pl.when(slot == slots - 1)
        def _():
            save().wait()

    anywhere = pl.BlockSpec(memory_space=pl.ANY)

    def slotted(*block):
        return pl.BlockSpec((1, *block), lambda i: (i,) + (0,) * len(block))

    return pl.pallas_call(
        kernel,
        grid=(slots,),
        out_shape=(
            jax.ShapeDtypeStruct((model_width, width), LOW),
            jax.ShapeDtypeStruct((slots, lat_rows, half_width), LOW),
            jax.ShapeDtypeStruct((slots, key_rows, 2 * half_width), LOW),
            jax.ShapeDtypeStruct((slots, groups, PACK * lat_rows, key_rows), WIDE),
            jax.ShapeDtypeStruct((slots, lat_rows, half_width), LOW),
        ),
        in_specs=[pl.BlockSpec(memory_space=pltpu.SMEM)]
        + [anywhere] * len(pieces)
        + [
            pl.BlockSpec((1, key_rows, model_width), lambda i: (jnp.minimum(i, images - 1), 0, 0)),
            pl.BlockSpec((1, key_rows, model_width), lambda i: (jnp.maximum(i - images, 0), 0, 0)),
        ],
        out_specs=(
            anywhere,
            slotted(lat_rows, half_width),
            slotted(key_rows, 2 * half_width),
            slotted(groups, PACK * lat_rows, key_rows),
            slotted(lat_rows, half_width),
        ),
        scratch_shapes=[
            pltpu.VMEM((model_width, width), LOW),
            pltpu.SemaphoreType.DMA((len(views) + 1,)),
        ],
        compiler_params=pltpu.CompilerParams(vmem_limit_bytes=40 * 2**20),
        cost_estimate=pl.CostEstimate(
            flops=2 * slots * key_rows * model_width * width,
            bytes_accessed=4 * model_width * width,
            transcendentals=0,
        ),
    )(jnp.stack(places).astype(jnp.int32), *pieces, own, far)


def project_out(places, pieces, mixed, model_width):
    slots, lat_rows, half_width = mixed.shape
    places, pieces = joined(places, pieces)
    shard = pieces[0].shape[-2]
    views = [(k, i) for k, piece in enumerate(pieces) for i in range(piece.shape[0])]
    chunk = PACK * HEAD

    def kernel(places_ref, *refs):
        piece_refs = refs[: len(pieces)]
        mixed_ref, full_ref, branch_ref, w_ref, sems = refs[len(pieces) :]
        loads = []
        for i, (k, entry) in enumerate(views):
            start = pl.multiple_of(places_ref[i] * shard, shard)
            loads.append(
                pltpu.make_async_copy(
                    piece_refs[k].at[entry], w_ref.at[pl.ds(start, shard)], sems.at[i]
                )
            )
        for load in loads:
            load.start()
        for load in loads:
            load.wait()
        save = pltpu.make_async_copy(w_ref, full_ref, sems.at[len(views)])
        save.start()
        rows = mixed_ref[...].reshape(slots * lat_rows, half_width)
        for part in range(model_width // chunk):
            columns = slice(part * chunk, (part + 1) * chunk)
            branch_ref[:, columns] = jnp.dot(
                rows, w_ref[:, columns], preferred_element_type=WIDE
            )
        save.wait()

    anywhere = pl.BlockSpec(memory_space=pl.ANY)
    whole = pl.BlockSpec(memory_space=pltpu.VMEM)
    full, branch = pl.pallas_call(
        kernel,
        out_shape=(
            jax.ShapeDtypeStruct((half_width, model_width), LOW),
            jax.ShapeDtypeStruct((slots * lat_rows, model_width), WIDE),
        ),
        in_specs=[pl.BlockSpec(memory_space=pltpu.SMEM)] + [anywhere] * len(pieces) + [whole],
        out_specs=(anywhere, whole),
        scratch_shapes=[
            pltpu.VMEM((half_width, model_width), LOW),
            pltpu.SemaphoreType.DMA((len(views) + 1,)),
        ],
        compiler_params=pltpu.CompilerParams(vmem_limit_bytes=16 * 2**20),
    )(jnp.stack(places).astype(jnp.int32), *pieces, mixed)
    return full, branch.reshape(slots, lat_rows, model_width)


def normal_parts(x):
    density = jnp.exp(-0.5 * x * x)
    t = 1.0 / (1.0 + (0.3275911 * math.sqrt(0.5)) * jnp.abs(x))
    series = t * (
        0.254829592
        + t * (-0.284496736 + t * (1.421413741 + t * (-1.453152027 + t * 1.061405429)))
    )
    upper = 0.5 * series * density
    return jnp.where(x < 0, upper, 1.0 - upper), density * (1.0 / math.sqrt(2 * math.pi))


def fold_up(block, folds):
    return jnp.concatenate(jnp.split(block, folds, axis=-2), axis=-1)


def unfold_up(block, folds):
    return jnp.concatenate(jnp.split(block, folds, axis=-1), axis=-2)


def ffn_rows_back(ffn_blocks, xs, d_outs, unit):
    deep = ffn_blocks.shape[0]
    hidden_units = deep * unit
    rows, model_width = xs[0].shape
    folds = model_width // hidden_units
    block = 128
    direct = whole_tiles(unit) and hidden_units % 128 == 0
    if direct:
        weights = (ffn_blocks,)
    else:
        weights = (
            unfold_up(ffn_blocks[:, unit:], folds).reshape(model_width, hidden_units),
            ffn_blocks[:, :unit].reshape(hidden_units, model_width),
        )

    def copies(weight_refs, up_ref, down_ref, sems):
        if not direct:
            moves = list(zip(weight_refs, (up_ref, down_ref), strict=True))
        else:
            (ffn_ref,) = weight_refs
            moves = []
            for z in range(deep):
                moves.append((ffn_ref.at[z, pl.ds(0, unit)], down_ref.at[pl.ds(z * unit, unit)]))
                for fold in range(folds):
                    moves.append(
                        (
                            ffn_ref.at[z, pl.ds(unit, unit), pl.ds(fold * hidden_units, hidden_units)],
                            up_ref.at[pl.ds((folds * z + fold) * unit, unit)],
                        )
                    )
        return [pltpu.make_async_copy(*move, sems.at[i]) for i, move in enumerate(moves)]

    def kernel(x0, x1, d0, d1, *refs):
        weight_refs, (hidden0, hidden1, pre0, pre1, in0, in1, up_ref, down_ref, sems) = (
            refs[: len(weights)],
            refs[len(weights) :],
        )

        @pl.when(pl.program_id(0) == 0)
        def _():
            loads = copies(weight_refs, up_ref, down_ref, sems)
            for load in loads:
                load.start()
            for load in loads:
                load.wait()

        x = jnp.concatenate([x0[...], x1[...]])
        d_out = jnp.concatenate([d0[...], d1[...]])
        pre = jnp.dot(x, up_ref[...], preferred_element_type=WIDE)
        d_hidden = dot(d_out, down_ref[...], ((1,), (1,)))
        below, density = normal_parts(pre)
        hidden = (pre * below).astype(LOW)
        d_pre = (d_hidden * (below + pre * density)).astype(LOW)
        d_input = dot(d_pre, up_ref[...], ((1,), (1,)))
        for side, (hidden_ref, pre_ref, in_ref) in enumerate(
            ((hidden0, pre0, in0), (hidden1, pre1, in1))
        ):
            mine = slice(side * block, (side + 1) * block)
            hidden_ref[...] = hidden[mine]
            pre_ref[...] = d_pre[mine]
            in_ref[...] = d_input[mine].astype(in_ref.dtype)

    wide = pl.BlockSpec((block, model_width), lambda i: (i, 0))
    narrow = pl.BlockSpec((block, hidden_units), lambda i: (i, 0))
    low = jax.ShapeDtypeStruct((rows, hidden_units), LOW)
    return pl.pallas_call(
        kernel,
        grid=(rows // block,),
        out_shape=(
            low,
            low,
            low,
            low,
            jax.ShapeDtypeStruct((rows, model_width), WIDE),
            jax.ShapeDtypeStruct((rows, model_width), LOW),
        ),
        in_specs=[wide] * 4 + [pl.BlockSpec(memory_space=pl.ANY)] * len(weights),
        out_specs=(narrow,) * 4 + (wide,) * 2,
        scratch_shapes=[
            pltpu.VMEM((model_width, hidden_units), LOW),
            pltpu.VMEM((hidden_units, model_width), LOW),
            pltpu.SemaphoreType.DMA(((folds + 1) * deep,)),
        ],
        compiler_params=pltpu.CompilerParams(vmem_limit_bytes=32 * 2**20),
        cost_estimate=pl.CostEstimate(
            flops=12 * rows * hidden_units * model_width,
            bytes_accessed=8 * rows * model_width,
            transcendentals=0,
        ),
    )(*xs, *d_outs, *weights)


def attend_back(d_mixed, query, keyval, probs):
    slots, lat_rows, half_width = query.shape
    key_rows = keyval.shape[1]
    patches = key_rows - lat_rows
    chunk = PACK * HEAD
    groups = half_width // chunk
    scale = 1.0 / math.sqrt(HEAD)

    def kernel(d_ref, query_ref, keyval_ref, probs_ref, out_ref):
        mask_low, mask_wide = head_mask(lat_rows, LOW), head_mask(lat_rows, WIDE)
        out_ref[0, :patches, :half_width] = jnp.zeros((patches, half_width), LOW)
        for part in range(groups):
            columns = slice(part * chunk, (part + 1) * chunk)
            q = tile_heads(query_ref[0, :, columns], mask_low)
            d = tile_heads(d_ref[0, :, columns], mask_low)
            k = keyval_ref[0, :, columns]
            v = keyval_ref[0, :, half_width + part * chunk : half_width + (part + 1) * chunk]
            p = probs_ref[0, part]
            d_probs = dot(d, v, ((1,), (1,)))
            d_value = dot(p.astype(LOW), d, ((0,), (0,)))
            delta = jnp.sum(p * d_probs, axis=1, keepdims=True)
            d_scores = (p * (d_probs - delta)).astype(LOW)
            d_query = untile_heads(jnp.dot(d_scores, k, preferred_element_type=WIDE), mask_wide)
            d_key = dot(d_scores, q, ((0,), (0,)))
            out_ref[0, patches:, columns] = (d_query * scale).astype(LOW)
            out_ref[0, :, half_width + part * chunk : half_width + (part + 1) * chunk] = (
                d_key * scale
            ).astype(LOW)
            out_ref[0, :, 2 * half_width + part * chunk : 2 * half_width + (part + 1) * chunk] = (
                d_value.astype(LOW)
            )

    def slotted(*block):
        return pl.BlockSpec((1, *block), lambda i: (i,) + (0,) * len(block))

    return pl.pallas_call(
        kernel,
        grid=(slots,),
        out_shape=jax.ShapeDtypeStruct((slots, key_rows, 3 * half_width), LOW),
        in_specs=[
            slotted(lat_rows, half_width),
            slotted(lat_rows, half_width),
            slotted(key_rows, 2 * half_width),
            slotted(groups, PACK * lat_rows, key_rows),
        ],
        out_specs=slotted(key_rows, 3 * half_width),
        compiler_params=pltpu.CompilerParams(vmem_limit_bytes=32 * 2**20),
        cost_estimate=pl.CostEstimate(
            flops=16 * slots * groups * PACK * lat_rows * key_rows * chunk,
            bytes_accessed=10 * slots * key_rows * half_width,
            transcendentals=0,
        ),
    )(d_mixed, query, keyval, probs)


def on_device(
    wires,
    media,
    latents,
    upstream,
    time_index,
    live_count,
    time_table,
    media_gain,
    media_bias,
    latent_gain,
    latent_bias,
    ff_gain,
    ff_bias,
    w_query,
    w_keyval,
    w_out,
    w_up,
    w_down,
):
    wires.place()
    deep, flat, count = wires.deep, wires.flat, wires.count
    images, patches, model_width = media.shape
    lat_rows = latents.shape[1]
    key_rows = patches + lat_rows
    table_rows, shard = time_table.shape
    group = model_width // (2 * deep)
    half_width = model_width // 2
    slots = 2 * images

    qkv_mine, qkv_other = deal_columns(wires.c, (w_query, w_keyval), group)
    qkv_arrived = wires.send(qkv_other, "core")
    qkv_block = pair(qkv_mine, qkv_arrived, wires.c, 0)

    unit = w_down.shape[0]
    hidden_units = deep * unit
    tall, wide = 2 * shard, 3 * half_width
    ring_block = jnp.concatenate(
        [qkv_block.reshape(tall, wide), jnp.pad(w_out, ((0, 0), (0, wide - model_width)))]
    )
    made = {}

    def norms(guests):
        smalls = jnp.concatenate(
            [time_table]
            + [
                v[None]
                for v in (media_gain, media_bias, latent_gain, latent_bias, ff_gain, ff_bias)
            ],
            axis=0,
        )
        smalls = jnp.broadcast_to(smalls[None], (count,) + smalls.shape)
        smalls = lax.all_to_all(after(smalls, guests[wires.bits[0]]), AXES, 0, 0, tiled=True)
        smalls = smalls.transpose(1, 0, 2).reshape(-1, model_width).astype(WIDE)
        table_full = smalls[:table_rows]
        (
            media_gain_full,
            media_bias_full,
            latent_gain_full,
            latent_bias_full,
            ff_gain_full,
            ff_bias_full,
        ) = [smalls[table_rows + k] for k in range(6)]

        alive = (jnp.arange(images) < live_count[0]).astype(WIDE)
        live_mask = alive[:, None, None]
        one_hot = (time_index[:, None] == jnp.arange(table_rows)[None, :]).astype(WIDE)
        time_rows = jnp.dot(one_hot, table_full, precision=HIGHEST)
        media_in = media.astype(WIDE) + time_rows[:, None, :]
        media_normed, media_norm_back = jax.vjp(norm_rows, media_in, media_gain_full, media_bias_full)
        latents_wide = after(latents, smalls).astype(WIDE)
        latent_normed, latent_norm_back = jax.vjp(
            norm_rows, latents_wide, latent_gain_full, latent_bias_full
        )
        own_sources = jnp.concatenate([media_normed.astype(LOW), latent_normed.astype(LOW)], axis=1)
        made.update(
            ff_gain_full=ff_gain_full,
            ff_bias_full=ff_bias_full,
            live_mask=live_mask,
            one_hot=one_hot,
            media_norm_back=media_norm_back,
            latent_norm_back=latent_norm_back,
            latents_wide=latents_wide,
            own_sources=own_sources,
        )
        return (own_sources,)

    d_out_low = after(upstream, qkv_other) * (jnp.arange(images) < live_count[0]).astype(LOW)[:, None, None]
    rings, gathered, d_out_got, steps = gather_rows(
        wires, ring_block, lambda block: block[:tall].reshape(2, shard, wide), d_out_low, {1: norms}
    )
    own_sources, latents_wide, live_mask, one_hot = (
        made[name] for name in ("own_sources", "latents_wide", "live_mask", "one_hot")
    )
    places, pieces = [], []
    for step, got in enumerate(gathered):
        for mask, part in got.items():
            pieces += part if isinstance(part, tuple) else [part]
            for core in range(2):
                places.append((wires.plane(step) * 2 + core) * flat + (wires.f ^ mask))
    out_column = [ring[tall:, :model_width] for ring in rings]

    up_block = wires.swap_blocks(
        split_units(after(w_up, gathered[0][wires.bits[0]]), 2 * flat, unit), wires.planes
    )
    folds = model_width // hidden_units
    ffn_block = jnp.concatenate([w_down, fold_up(up_block.reshape(-1, hidden_units), folds)])

    ffn_blocks = jnp.broadcast_to(ffn_block[None], (deep, *ffn_block.shape))
    ffn_blocks = after(ffn_blocks, rings[-1])
    ffn_blocks = wires.swap_blocks(ffn_blocks, wires.columns)

    out_places, out_pieces = [], []
    for mask, part in spread_plane(wires, jnp.stack(out_column), *steps[-2]).items():
        out_pieces.append(part)
        for step in range(deep):
            out_places.append(wires.plane(step) * flat + (wires.f ^ mask))

    far_sources = wires.send(own_sources, "core", rings[-1])

    qkv_full, query, keyval, probs, mixed = attend(
        places,
        pieces,
        own_sources,
        far_sources,
        patches,
        half_width,
    )
    out_full, branch = project_out(
        out_places, out_pieces, after(mixed, *d_out_got.values()), model_width
    )
    branch = branch[:images] + wires.send(branch[images:], "core")
    middle = latents_wide + branch

    ffn_normed, ffn_norm_back = jax.vjp(norm_rows, middle, made["ff_gain_full"], made["ff_bias_full"])
    d_out = upstream.astype(WIDE) * live_mask

    def swapped(blocks, *ahead):
        mine = jnp.stack(blocks)
        far = wires.send(mine, "core", *ahead)
        return mine.reshape(-1, model_width), far.reshape(-1, model_width)

    ffn_low = ffn_normed.astype(LOW)
    ffn_got = spread_plane(wires, ffn_low)
    d_out_got = {mask: after(part, ffn_low) for mask, part in d_out_got.items()}
    d_out_chunks = [swapped([d_out_got[0]]), swapped([d_out_got[mask] for mask in wires.masks])]
    ffn_chunks = [swapped([ffn_low])]
    near = ffn_rows_back(ffn_blocks, ffn_chunks[0], d_out_chunks[0], unit)
    ffn_chunks.append(swapped([ffn_got[mask] for mask in wires.masks], near[0]))
    far = ffn_rows_back(ffn_blocks, ffn_chunks[1], d_out_chunks[1], unit)
    block_shape = (images, lat_rows, model_width)

    def collect_core(near, far, *ahead):
        far_whole = far[0] + wires.send(far[1].astype(LOW), "core", *ahead).astype(WIDE)
        far_whole = far_whole.reshape(len(wires.masks), *block_shape)
        near_whole = near[0] + wires.send(near[1].astype(LOW), "core", *ahead).astype(WIDE)
        return {0: near_whole.reshape(block_shape)} | dict(zip(wires.masks, far_whole, strict=True))

    d_sums = collect_core(near[4:], far[4:])
    d_ffn_input, d_arrived = sum_plane(wires, d_sums.get)

    hidden = jnp.concatenate([after(near[0], d_arrived[0]), near[1], *far[:2]])
    d_pre_low = jnp.concatenate([after(near[2], d_arrived[0]), near[3], *far[2:4]])
    d_out_rows = jnp.concatenate([rows for pair_of in d_out_chunks for rows in pair_of])
    ffn_rows = jnp.concatenate([rows for pair_of in ffn_chunks for rows in pair_of])
    down_partial = outer(hidden, d_out_rows).astype(LOW).reshape(deep, unit, model_width)
    up_partial = outer(ffn_rows, d_pre_low).astype(LOW)
    up_partial = up_partial.reshape(deep, 2 * flat * shard, hidden_units)
    ffn_partial = jnp.concatenate([down_partial, fold_up(up_partial, folds)], axis=1)
    ffn_terms = wires.swap_blocks(ffn_partial, wires.columns)

    d_ffn_input = after(d_ffn_input, ffn_partial)
    d_middle_norm, ff_gain_grad, ff_bias_grad = ffn_norm_back(d_ffn_input)
    d_middle = d_out + d_middle_norm

    down_full = after(ffn_blocks, d_middle)[:, :unit].reshape(hidden_units, model_width)
    results = rows_by(hidden, down_full)
    counts = [near[0].shape[0], far[0].shape[0]]
    cuts = [counts[0], 2 * counts[0], 2 * counts[0] + counts[1]]
    results = jnp.split(results, cuts)
    result_sums = collect_core(results[:2], results[2:])
    result_low = [result_sums[mask].astype(LOW) for mask in wires.masks]

    own_branch = d_middle.astype(LOW)
    d_branch = jnp.concatenate([own_branch, wires.send(own_branch, "core")], axis=0)
    out_partial = outer(mixed.reshape(-1, half_width), d_branch.reshape(-1, model_width))
    out_partial = out_partial.astype(LOW).reshape(deep, flat, shard, model_width)
    out_partial = jnp.stack([out_partial[..., :half_width], out_partial[..., half_width:]], axis=2)
    d_mixed = rows_back(after(d_branch, out_partial), out_full).astype(LOW)
    d_projected = attend_back(d_mixed, query, keyval, probs)

    source_rows = jnp.concatenate([after(own_sources, d_branch), far_sources]).reshape(-1, model_width)
    d_projected_rows = d_projected.reshape(-1, wide)
    plane_rows = 2 * flat * shard

    kept = {}

    def results_home(arrived):
        own_result, got = sum_plane(wires, result_sums.get, d_projected)
        kept["out"] = ((middle + own_result) * live_mask).astype(LOW)
        return got

    def sources_back(arrived):
        d_projected_now = after(d_projected, arrived)
        far_d = rows_back(d_projected_now[images:], qkv_full).astype(LOW)
        far_d = wires.send(far_d, "core").astype(WIDE)
        kept["rows"] = rows_back(d_projected_now[:images], qkv_full) + far_d
        return (kept["rows"],)

    def norms_back(arrived):
        d_rows = after(kept["rows"], arrived)
        d_latent_in, latent_gain_grad, latent_bias_grad = made["latent_norm_back"](d_rows[:, patches:, :])
        media_grad, media_gain_grad, media_bias_grad = made["media_norm_back"](d_rows[:, :patches, :])
        latent_grad = d_middle + d_latent_in
        table_part = jnp.dot(one_hot.T, jnp.sum(media_grad, axis=1), precision=HIGHEST)

        small_grads = jnp.concatenate(
            [table_part]
            + [
                v[None]
                for v in (
                    media_gain_grad,
                    media_bias_grad,
                    latent_gain_grad,
                    latent_bias_grad,
                    ff_gain_grad,
                    ff_bias_grad,
                )
            ],
            axis=0,
        )
        small_grads = small_grads.reshape(-1, count, shard).transpose(1, 0, 2)
        kept["media"], kept["latent"], kept["small"] = media_grad, latent_grad, small_grads
        return media_grad, latent_grad, small_grads

    def ffn_home(arrived):
        ffn_sum = jnp.sum(after(ffn_terms, arrived).astype(WIDE), axis=0)
        kept["down"] = ffn_sum[:unit]
        up_sum = unfold_up(ffn_sum[unit:].astype(LOW), folds)
        kept["up"] = up_sum.reshape(2 * flat, shard, hidden_units)
        small_grads = lax.all_to_all(after(kept["small"], ffn_terms), AXES, 0, 0, tiled=True)
        kept["small"] = jnp.sum(small_grads, axis=0)
        return kept["down"], kept["up"], small_grads

    def partial_rows(step, d_rows):
        at_plane = wires.plane(1 + step)
        rows = lax.dynamic_slice_in_dim(source_rows, at_plane * plane_rows, plane_rows, 1)
        block = outer(rows, d_rows).astype(LOW).reshape(2, flat, shard, wide)
        return block, at(out_partial, at_plane, 0)

    partials = {0: partial_rows(0, d_projected_rows)}

    def more_partials(arrived):
        d_rows = after(d_projected_rows, arrived)
        for step in range(1, deep):
            partials[step] = partial_rows(step, d_rows)
        return (partials[1][0], *results_home(arrived))

    def part(step, mask):
        block, out_block = partials[step]
        target = wires.f ^ mask
        return jnp.concatenate([at(block, target, 1), at(out_block, target, 0)], axis=-1)

    total = scatter_rows(
        wires,
        part,
        {
            0: lambda _: result_low,
            1: more_partials,
            2: sources_back,
            3: norms_back,
            4: ffn_home,
        },
    )
    qkv_sum = total[..., :wide]
    w_out_grad = jnp.concatenate([total[0, :, wide:], total[1, :, wide:]], axis=-1)
    media_grad, latent_grad = kept["media"], kept["latent"]
    w_down_grad = kept["down"]
    small_grads = kept["small"]
    latents_out = kept["out"]
    up_blocks = wires.swap_blocks(after(kept["up"], small_grads), wires.planes)
    w_up_grad = merge_units(up_blocks, unit)
    qkv_own = pick(qkv_sum, wires.c, 0)
    qkv_far = wires.send(pick(qkv_sum, 1 - wires.c, 0), "core", up_blocks)
    w_query_grad, w_keyval_grad = join_columns(
        wires.c, qkv_own, qkv_far, (model_width, 2 * model_width), group
    )
    return (
        latents_out,
        media_grad,
        latent_grad,
        small_grads[:table_rows],
        *[small_grads[table_rows + k] for k in range(6)],
        w_query_grad,
        w_keyval_grad,
        w_out_grad,
        w_up_grad,
        w_down_grad,
    )


def solution(mesh):
    lead = P(AXES)
    table = P(None, AXES)
    return jax.shard_map(
        functools.partial(on_device, Wires(mesh)),
        mesh=mesh,
        in_specs=(lead,) * 5 + (table,) + (lead,) * 11,
        out_specs=(lead,) * 3 + (table,) + (lead,) * 11,
        check_vma=False,
    )
```

```python
import functools
import math

import jax
import jax.numpy as jnp
from jax import lax
from jax.experimental import pallas as pl
from jax.experimental.pallas import tpu as pltpu
from jax.sharding import PartitionSpec as P

HEAD = 96
PACK = 4
AXES = ("dp", "fsdp")
LOW = jnp.bfloat16
WIDE = jnp.float32
HIGHEST = lax.Precision.HIGHEST
NORM_EPS = 1e-05
BRIEF = pl.CostEstimate(flops=1, bytes_accessed=1, transcendentals=0)


def norm_rows(inputs, gain, shift):
    row_mean = jnp.mean(inputs, axis=-1, keepdims=True)
    centered = inputs - row_mean
    variance = jnp.mean(centered * centered, axis=-1, keepdims=True)
    return centered * lax.rsqrt(variance + NORM_EPS) * gain + shift


def exact_gelu(inputs):
    return jax.nn.gelu(inputs, approximate=False)


def dot(left, right, contract):
    return lax.dot_general(left, right, (contract, ((), ())), preferred_element_type=WIDE)


def rows_by(left, right):
    return dot(left, right, ((left.ndim - 1,), (0,)))


def rows_back(left, right):
    return dot(left, right, ((left.ndim - 1,), (1,)))


def outer(left, right):
    return dot(left, right, ((0,), (0,)))


class Wires:
    def __init__(self, mesh):
        self.deep = mesh.shape["dp"] // 2
        self.flat = mesh.shape["fsdp"]
        self.count = 2 * self.deep * self.flat
        places = [
            (z, c, f) for z in range(self.deep) for c in range(2) for f in range(self.flat)
        ]

        def number(z, c, f):
            return (z * 2 + c) * self.flat + f

        def moves(target):
            return [(number(*place), number(*target(*place))) for place in places]

        self.bits = [1 << k for k in range(self.flat.bit_length() - 1)]
        self.masks = list(range(1, self.flat))
        self.moves = {
            "core": moves(lambda z, c, f: (z, 1 - c, f)),
        }
        self.moves["rise"] = moves(lambda z, c, f: ((z + 1) % self.deep, c, f))
        self.columns = [
            [number(z, c, f) for z in range(self.deep)] for c in range(2) for f in range(self.flat)
        ]
        self.planes = [
            [number(z, c, f) for c in range(2) for f in range(self.flat)] for z in range(self.deep)
        ]
        for mask in self.masks:
            self.moves[mask] = moves(lambda z, c, f, mask=mask: (z, c, f ^ mask))

    def place(self):
        outer_at = lax.axis_index("dp")
        self.z, self.c = outer_at // 2, outer_at % 2
        self.f = lax.axis_index("fsdp")
        self.queues = {}

    def send(self, block, kind, *ahead):
        if ahead:
            block = after(block, *ahead)
        return lax.ppermute(block, AXES, self.moves[kind])

    def swap_blocks(self, blocks, groups):
        return lax.all_to_all(blocks, AXES, 0, 0, tiled=True, axis_index_groups=groups)

    def plane(self, step):
        return lax.rem(self.z + 2 * self.deep - step, self.deep)


def after(block, *others):
    return lax.optimization_barrier((block, *others))[0]


def at(array, index, axis):
    return lax.dynamic_index_in_dim(array, index, axis, keepdims=False)


def pair(mine, other, side, axis):
    return jnp.where(
        side == 0, jnp.stack([mine, other], axis=axis), jnp.stack([other, mine], axis=axis)
    )


def pick(array, side, axis):
    return jnp.where(
        side == 0,
        lax.index_in_dim(array, 0, axis, keepdims=False),
        lax.index_in_dim(array, 1, axis, keepdims=False),
    )


def corner(mask):
    return mask & -mask, 1 << (mask.bit_length() - 1)


def gather_rows(wires, block, take, guest, hooks, before):
    rings, gathered, guests = [block], [], {0: guest}
    single = [mask for mask in wires.masks if not mask & (mask - 1)]
    multiple = sorted((m for m in wires.masks if m & (m - 1)), key=lambda m: bin(m).count("1"))
    steps = []
    for step in range(wires.deep + 1):
        now = []
        before = (*before, *(hooks[step](gathered[0]) if step in hooks else ()))
        if step < wires.deep:
            if step + 1 < wires.deep:
                rings.append(wires.send(rings[step], "rise", *before))
                now.append(rings[-1])
            mine = take(rings[step])
            got = {0: mine}
            for mask in single:
                got[mask] = wires.send(mine, mask, *before)
                now.append(got[mask])
            gathered.append(got)
        if step == 0:
            for mask in single:
                guests[mask] = wires.send(guest, mask, *before)
                now.append(guests[mask])
        if step:
            got = gathered[step - 1]
            for mask in multiple:
                low, high = corner(mask)
                got[mask] = (
                    wires.send(got[mask ^ high][0], high, *before),
                    wires.send(got[mask ^ low][1], low, *before),
                )
                now += got[mask]
        before = now
        steps.append(now)
    return rings, gathered, guests, steps


def scatter_rows(wires, part, pulls, riders, clocks):
    single = [mask for mask in wires.masks if not mask & (mask - 1)]
    multiple = sorted((m for m in wires.masks if m & (m - 1)), key=lambda m: -bin(m).count("1"))
    extra = [{} for _ in range(wires.deep)]
    before, total, clock = (), None, None
    for step in range(wires.deep + 2):
        now, ready = [], []
        ahead = (*(before if step else ()), *(pulls[step](clock) if step in pulls else ()))

        def term(block, mask, half=None):
            mine = part(block, mask)
            if half is not None:
                mine = mine[half]
            more = extra[block].get((mask, half), [])
            return sum([m.astype(WIDE) for m in more], mine).astype(LOW)

        block = step - 2
        if 0 <= block:
            total = (
                sum([m.astype(WIDE) for m in extra[block][0, None]], part(block, 0).astype(WIDE))
                + (0.0 if total is None else total)
            )
            if block == wires.deep - 1:
                return total
            arrived = wires.send(total.astype(LOW), "rise", *ahead)
            now.append(arrived)
            total = arrived.astype(WIDE)
        block = step - 1
        if 0 <= block < wires.deep:
            for mask in single:
                leaving = jnp.stack([term(block, mask, half) for half in range(2)])
                ready.append(leaving)
                arrived = wires.send(leaving, mask, *ahead)
                extra[block].setdefault((0, None), []).append(arrived)
                now.append(arrived)
        if step < wires.deep:
            for mask in multiple:
                low, high = corner(mask)
                for half, bit in ((0, high), (1, low)):
                    leaving = term(step, mask, half)
                    ready.append(leaving)
                    arrived = wires.send(leaving, bit, *ahead)
                    extra[step].setdefault((mask ^ bit, half), []).append(arrived)
                    now.append(arrived)
        clock = clocks[step](*ahead, *ready) if step in clocks else now[-1]
        for rider in riders.get(step, ()):
            now.append(rider(ahead))
        before = now


def spread_plane(wires, block, *ahead):
    got = {0: block}
    for mask in reversed(wires.masks):
        got[mask] = wires.send(block, mask, *ahead)
    return got


def sum_plane(wires, part, *ahead):
    arrived = [wires.send(part(mask).astype(LOW), mask, *ahead) for mask in reversed(wires.masks)]
    return sum([block.astype(WIDE) for block in arrived], part(0).astype(WIDE)), arrived


def lay(places, pieces, count):
    entry = pieces[0].shape[1:]
    views = [(k, i) for k, piece in enumerate(pieces) for i in range(piece.shape[0])]
    number = len(views)

    def kernel(places_ref, *refs):
        out_ref, held, sems = refs[-3:]
        loads = [
            pltpu.make_async_copy(refs[k].at[i], held.at[n], sems.at[0, n])
            for n, (k, i) in enumerate(views)
        ]
        stores = [
            pltpu.make_async_copy(held.at[n], out_ref.at[places_ref[n]], sems.at[1, n])
            for n in range(number)
        ]
        for load in loads:
            load.start()
        for load, store in zip(loads, stores, strict=True):
            load.wait()
            store.start()
        for store in stores:
            store.wait()

    anywhere = pl.BlockSpec(memory_space=pl.ANY)
    return pl.pallas_call(
        kernel,
        out_shape=jax.ShapeDtypeStruct((count,) + entry, pieces[0].dtype),
        in_specs=[pl.BlockSpec(memory_space=pltpu.SMEM)] + [anywhere] * len(pieces),
        out_specs=anywhere,
        scratch_shapes=[
            pltpu.VMEM((number,) + entry, pieces[0].dtype),
            pltpu.SemaphoreType.DMA((2, number)),
        ],
        compiler_params=pltpu.CompilerParams(vmem_limit_bytes=58 * 2**20),
    )(jnp.stack(places).astype(jnp.int32), *pieces)


def whole_tiles(rows):
    return rows % 16 == 0


def joined(places, pieces):
    shard = pieces[0].shape[-2]
    if whole_tiles(shard):
        return places, pieces
    rows = [row for piece in pieces for row in (piece if piece.ndim == 3 else (piece,))]
    full = jnp.zeros((len(rows), *rows[0].shape), rows[0].dtype)
    for place, row in zip(places, rows, strict=True):
        full = lax.dynamic_update_index_in_dim(full, row, place, 0)
    return [jnp.zeros((), jnp.int32)], [full.reshape(1, len(rows) * shard, -1)]


def on_chip(kernel, out_shape, side, *operands):
    whole = pl.BlockSpec(memory_space=pltpu.VMEM)
    return pl.pallas_call(
        kernel,
        out_shape=out_shape,
        in_specs=[pl.BlockSpec(memory_space=pltpu.SMEM)] + [whole] * len(operands),
        out_specs=jax.tree.map(lambda _: whole, out_shape),
    )(side.reshape(1).astype(jnp.int32), *operands)


def deal_columns(side, arrays, group):
    shard = arrays[0].shape[0]
    width = sum(array.shape[1] for array in arrays) // 2
    if not whole_tiles(shard):
        both = jnp.concatenate(arrays, axis=1).reshape(shard, -1, 2, group)
        return tuple(pick(both, s, 2).reshape(shard, width) for s in (side, 1 - side))

    def kernel(side_ref, *refs):
        *in_refs, own_ref, other_ref = refs
        first = side_ref[0] == 0
        base = 0
        for ref in in_refs:
            block = ref[...]
            count = block.shape[1] // (2 * group)
            hands = [
                jnp.concatenate(
                    [block[:, (2 * j + s) * group : (2 * j + s + 1) * group] for j in range(count)],
                    axis=1,
                )
                for s in range(2)
            ]
            own_ref[:, base : base + count * group] = jnp.where(first, hands[0], hands[1])
            other_ref[:, base : base + count * group] = jnp.where(first, hands[1], hands[0])
            base += count * group

    shape = jax.ShapeDtypeStruct((shard, width), arrays[0].dtype)
    return on_chip(kernel, (shape, shape), side, *arrays)


def join_columns(side, own, other, widths, group):
    shard = own.shape[0]
    if not whole_tiles(shard):
        halves = [part.reshape(shard, -1, group) for part in (own, other)]
        both = pair(halves[0], halves[1], side, 2).reshape(shard, -1)
        return tuple(jnp.split(both, [widths[0]], axis=1))

    def kernel(side_ref, own_ref, other_ref, *out_refs):
        first = side_ref[0] == 0
        hands = (
            jnp.where(first, own_ref[...], other_ref[...]),
            jnp.where(first, other_ref[...], own_ref[...]),
        )
        base = 0
        for ref in out_refs:
            parts = []
            for j in range(ref.shape[1] // (2 * group)):
                columns = slice(base + j * group, base + (j + 1) * group)
                parts += [hand[:, columns] for hand in hands]
            ref[...] = jnp.concatenate(parts, axis=1)
            base += ref.shape[1] // 2

    shapes = tuple(jax.ShapeDtypeStruct((own.shape[0], width), own.dtype) for width in widths)
    return on_chip(kernel, shapes, side, own, other)


def split_units(array, ways, unit):
    shard, width = array.shape
    deep = width // (ways * unit)
    if not whole_tiles(shard):
        blocks = array.reshape(shard, deep, ways, unit).transpose(2, 0, 1, 3)
        return blocks.reshape(ways, shard, deep * unit)

    def kernel(_, in_ref, out_ref):
        block = in_ref[...]
        for way in range(ways):
            parts = [
                block[:, (z * ways + way) * unit : (z * ways + way + 1) * unit] for z in range(deep)
            ]
            out_ref[way] = jnp.concatenate(parts, axis=1)

    shape = jax.ShapeDtypeStruct((ways, shard, deep * unit), array.dtype)
    return on_chip(kernel, shape, jnp.zeros((), jnp.int32), array)


def merge_units(blocks, unit):
    ways, shard, part = blocks.shape
    deep = part // unit
    if not whole_tiles(shard):
        blocks = blocks.reshape(ways, shard, deep, unit).transpose(1, 2, 0, 3)
        return blocks.reshape(shard, -1).astype(WIDE)

    def kernel(_, in_ref, out_ref):
        parts = []
        for z in range(deep):
            for way in range(ways):
                parts.append(in_ref[way][:, z * unit : (z + 1) * unit].astype(WIDE))
        out_ref[...] = jnp.concatenate(parts, axis=1)

    shape = jax.ShapeDtypeStruct((shard, deep * ways * unit), WIDE)
    return on_chip(kernel, shape, jnp.zeros((), jnp.int32), blocks)


def tile_heads(rows, mask):
    return jnp.concatenate([rows] * PACK, axis=0) * mask


def untile_heads(rows, mask):
    kept = rows * mask
    size = rows.shape[0] // PACK
    return sum(kept[k * size : (k + 1) * size] for k in range(PACK))


def head_mask(rows, dtype):
    row = lax.broadcasted_iota(jnp.int32, (PACK * rows, PACK * HEAD), 0) // rows
    column = lax.broadcasted_iota(jnp.int32, (PACK * rows, PACK * HEAD), 1) // HEAD
    return (row == column).astype(WIDE).astype(dtype)


def normed(rows, gain, shift):
    centered = rows - jnp.mean(rows, axis=-1, keepdims=True)
    inverse = lax.rsqrt(jnp.mean(centered * centered, axis=-1, keepdims=True) + NORM_EPS)
    unit = centered * inverse
    return unit * gain + shift, unit, inverse


def attend(places, pieces, own, far, time_rows, norm_rows_of, patches, half_width):
    images, key_rows, model_width = own.shape
    lat_rows = key_rows - patches
    slots = 2 * images
    width = 3 * half_width
    places, pieces = joined(places, pieces)
    chunk = PACK * HEAD
    groups = half_width // chunk
    scale = 1.0 / math.sqrt(HEAD)
    shard = pieces[0].shape[-2]
    views = []
    for k, piece in enumerate(pieces):
        views += [(k, None)] if piece.ndim == 2 else [(k, core) for core in range(piece.shape[0])]

    def kernel(places_ref, *refs):
        piece_refs = refs[: len(pieces)]
        (
            own_ref,
            far_ref,
            time_ref,
            params_ref,
            full_ref,
            sources_ref,
            query_ref,
            keyval_ref,
            probs_ref,
            mixed_ref,
            w_ref,
            sems,
        ) = refs[len(pieces) :]
        slot = pl.program_id(0)
        loads = []
        for i, (k, core) in enumerate(views):
            source = piece_refs[k] if core is None else piece_refs[k].at[core]
            start = pl.multiple_of(places_ref[i] * shard, shard)
            loads.append(pltpu.make_async_copy(source, w_ref.at[pl.ds(start, shard)], sems.at[i]))

        @pl.when(slot == 0)
        def _():
            for load in loads:
                load.start()

        def save():
            return pltpu.make_async_copy(w_ref, full_ref, sems.at[len(views)])

        raw = jnp.where(slot < images, own_ref[0], far_ref[0]).astype(WIDE)
        media = raw[:patches] + time_ref[0]
        sources_ref[0, :patches] = normed(media, params_ref[0:1], params_ref[1:2])[0].astype(LOW)
        lat = normed(raw[patches:], params_ref[2:3], params_ref[3:4])[0]
        sources_ref[0, patches:] = lat.astype(LOW)

        @pl.when(slot == 0)
        def _():
            for load in loads:
                load.wait()
            save().start()

        x = sources_ref[0]
        mask_low, mask_wide = head_mask(lat_rows, LOW), head_mask(lat_rows, WIDE)

        def project(rows, part):
            w = w_ref[:, part * chunk : (part + 1) * chunk]
            return jnp.dot(rows, w, preferred_element_type=WIDE).astype(LOW)

        for part in range(groups):
            columns = slice(part * chunk, (part + 1) * chunk)
            query = project(x[patches:], part)
            query_ref[0, :, columns] = query
            k = project(x, groups + part)
            keyval_ref[0, :, columns] = k
            v = project(x, 2 * groups + part)
            keyval_ref[0, :, half_width + part * chunk : half_width + (part + 1) * chunk] = v
            s = dot(tile_heads(query, mask_low), k, ((1,), (1,)))
            e = jnp.exp((s - jnp.max(s, axis=1, keepdims=True)) * scale)
            p = e * (1.0 / jnp.sum(e, axis=1, keepdims=True))
            probs_ref[0, part] = p
            m = jnp.dot(p.astype(LOW), v, preferred_element_type=WIDE)
            mixed_ref[0, :, columns] = untile_heads(m, mask_wide).astype(LOW)

        @pl.when(slot == slots - 1)
        def _():
            save().wait()

    anywhere = pl.BlockSpec(memory_space=pl.ANY)
    whole = pl.BlockSpec(memory_space=pltpu.VMEM)

    def slotted(*block):
        return pl.BlockSpec((1, *block), lambda i: (i,) + (0,) * len(block))

    def halved(first, *block):
        if first:
            return pl.BlockSpec((1, *block), lambda i: (jnp.minimum(i, images - 1), 0, 0))
        return pl.BlockSpec((1, *block), lambda i: (jnp.maximum(i - images, 0), 0, 0))

    return pl.pallas_call(
        kernel,
        grid=(slots,),
        out_shape=(
            jax.ShapeDtypeStruct((model_width, width), LOW),
            jax.ShapeDtypeStruct((slots, key_rows, model_width), LOW),
            jax.ShapeDtypeStruct((slots, lat_rows, half_width), LOW),
            jax.ShapeDtypeStruct((slots, key_rows, 2 * half_width), LOW),
            jax.ShapeDtypeStruct((slots, groups, PACK * lat_rows, key_rows), WIDE),
            jax.ShapeDtypeStruct((slots, lat_rows, half_width), LOW),
        ),
        in_specs=[pl.BlockSpec(memory_space=pltpu.SMEM)]
        + [anywhere] * len(pieces)
        + [
            halved(True, key_rows, model_width),
            halved(False, key_rows, model_width),
            slotted(1, model_width),
            whole,
        ],
        out_specs=(
            anywhere,
            slotted(key_rows, model_width),
            slotted(lat_rows, half_width),
            slotted(key_rows, 2 * half_width),
            slotted(groups, PACK * lat_rows, key_rows),
            slotted(lat_rows, half_width),
        ),
        scratch_shapes=[
            pltpu.VMEM((model_width, width), LOW),
            pltpu.SemaphoreType.DMA((len(views) + 1,)),
        ],
        compiler_params=pltpu.CompilerParams(vmem_limit_bytes=58 * 2**20),
        cost_estimate=BRIEF,
    )(jnp.stack(places).astype(jnp.int32), *pieces, own, far, time_rows[:, None], norm_rows_of)


def sources_back(d_projected, projections, far_part, own, time_rows, norm_rows_of, d_middle):
    images, key_rows, model_width = own.shape
    lat_rows = d_middle.shape[1]
    patches = key_rows - lat_rows
    width = d_projected.shape[-1]

    def kernel(d_ref, w_ref, far_ref, raw_ref, time_ref, params_ref, mid_ref, m_out, l_out, s_out):
        d = dot(d_ref[0], w_ref[...], ((1,), (1,))) + far_ref[0].astype(WIDE)

        def back(rows, d_rows, gain, shift):
            _, unit, inverse = normed(rows, gain, shift)
            scaled = d_rows * gain
            along = jnp.mean(scaled * unit, axis=-1, keepdims=True)
            inner = scaled - jnp.mean(scaled, axis=-1, keepdims=True) - unit * along
            sums = (
                jnp.sum(d_rows * unit, axis=0, keepdims=True),
                jnp.sum(d_rows, axis=0, keepdims=True),
            )
            return inverse * inner, sums

        rows = raw_ref[0, :patches].astype(WIDE) + time_ref[0]
        d_media, media_sums = back(rows, d[:patches], params_ref[0:1], params_ref[1:2])
        m_out[0] = d_media
        rows = raw_ref[0, patches:].astype(WIDE)
        d_lat, lat_sums = back(rows, d[patches:], params_ref[2:3], params_ref[3:4])
        l_out[0] = mid_ref[0] + d_lat
        total = jnp.sum(d_media, axis=0, keepdims=True)
        s_out[0] = jnp.concatenate(
            [total, *media_sums, *lat_sums, jnp.zeros((3, model_width), WIDE)], axis=0
        )

    whole = pl.BlockSpec(memory_space=pltpu.VMEM)

    def slotted(*block):
        return pl.BlockSpec((1, *block), lambda i: (i,) + (0,) * len(block))

    return pl.pallas_call(
        kernel,
        grid=(images,),
        out_shape=(
            jax.ShapeDtypeStruct((images, patches, model_width), WIDE),
            jax.ShapeDtypeStruct((images, lat_rows, model_width), WIDE),
            jax.ShapeDtypeStruct((images, 8, model_width), WIDE),
        ),
        in_specs=[
            slotted(key_rows, width),
            whole,
            slotted(key_rows, model_width),
            slotted(key_rows, model_width),
            slotted(1, model_width),
            whole,
            slotted(lat_rows, model_width),
        ],
        out_specs=(
            slotted(patches, model_width),
            slotted(lat_rows, model_width),
            slotted(8, model_width),
        ),
        compiler_params=pltpu.CompilerParams(vmem_limit_bytes=48 * 2**20),
        cost_estimate=BRIEF,
    )(d_projected, projections, far_part, own, time_rows[:, None], norm_rows_of, d_middle)


def project_out(places, pieces, mixed, model_width):
    slots, lat_rows, half_width = mixed.shape
    places, pieces = joined(places, pieces)
    shard = pieces[0].shape[-2]
    views = [(k, i) for k, piece in enumerate(pieces) for i in range(piece.shape[0])]
    chunk = PACK * HEAD

    def kernel(places_ref, *refs):
        piece_refs = refs[: len(pieces)]
        mixed_ref, full_ref, branch_ref, w_ref, sems = refs[len(pieces) :]
        loads = []
        for i, (k, entry) in enumerate(views):
            start = pl.multiple_of(places_ref[i] * shard, shard)
            loads.append(
                pltpu.make_async_copy(
                    piece_refs[k].at[entry], w_ref.at[pl.ds(start, shard)], sems.at[i]
                )
            )
        for load in loads:
            load.start()
        for load in loads:
            load.wait()
        save = pltpu.make_async_copy(w_ref, full_ref, sems.at[len(views)])
        save.start()
        rows = mixed_ref[...].reshape(slots * lat_rows, half_width)
        for part in range(model_width // chunk):
            columns = slice(part * chunk, (part + 1) * chunk)
            branch_ref[:, columns] = jnp.dot(
                rows, w_ref[:, columns], preferred_element_type=WIDE
            )
        save.wait()

    anywhere = pl.BlockSpec(memory_space=pl.ANY)
    whole = pl.BlockSpec(memory_space=pltpu.VMEM)
    full, branch = pl.pallas_call(
        kernel,
        out_shape=(
            jax.ShapeDtypeStruct((half_width, model_width), LOW),
            jax.ShapeDtypeStruct((slots * lat_rows, model_width), WIDE),
        ),
        in_specs=[pl.BlockSpec(memory_space=pltpu.SMEM)] + [anywhere] * len(pieces) + [whole],
        out_specs=(anywhere, whole),
        scratch_shapes=[
            pltpu.VMEM((half_width, model_width), LOW),
            pltpu.SemaphoreType.DMA((len(views) + 1,)),
        ],
        compiler_params=pltpu.CompilerParams(vmem_limit_bytes=16 * 2**20),
        cost_estimate=BRIEF,
    )(jnp.stack(places).astype(jnp.int32), *pieces, mixed)
    return full, branch.reshape(slots, lat_rows, model_width)


def normal_parts(x):
    density = jnp.exp(-0.5 * x * x)
    t = 1.0 / (1.0 + (0.3275911 * math.sqrt(0.5)) * jnp.abs(x))
    series = t * (
        0.254829592
        + t * (-0.284496736 + t * (1.421413741 + t * (-1.453152027 + t * 1.061405429)))
    )
    upper = 0.5 * series * density
    return jnp.where(x < 0, upper, 1.0 - upper), density * (1.0 / math.sqrt(2 * math.pi))


def fold_up(block, folds):
    return jnp.concatenate(jnp.split(block, folds, axis=-2), axis=-1)


def unfold_up(block, folds):
    return jnp.concatenate(jnp.split(block, folds, axis=-1), axis=-2)


def ffn_rows_back(ffn_blocks, xs, d_outs, unit):
    deep = ffn_blocks.shape[0]
    hidden_units = deep * unit
    rows, model_width = xs[0].shape
    folds = model_width // hidden_units
    block = 128
    direct = whole_tiles(unit) and hidden_units % 128 == 0
    if direct:
        weights = (ffn_blocks,)
    else:
        weights = (
            unfold_up(ffn_blocks[:, unit:], folds).reshape(model_width, hidden_units),
            ffn_blocks[:, :unit].reshape(hidden_units, model_width),
        )

    def copies(weight_refs, up_ref, down_ref, sems):
        if not direct:
            moves = list(zip(weight_refs, (up_ref, down_ref), strict=True))
        else:
            (ffn_ref,) = weight_refs
            moves = []
            for z in range(deep):
                moves.append((ffn_ref.at[z, pl.ds(0, unit)], down_ref.at[pl.ds(z * unit, unit)]))
                for fold in range(folds):
                    moves.append(
                        (
                            ffn_ref.at[z, pl.ds(unit, unit), pl.ds(fold * hidden_units, hidden_units)],
                            up_ref.at[pl.ds((z * folds + fold) * unit, unit)],
                        )
                    )
        return [pltpu.make_async_copy(*move, sems.at[i]) for i, move in enumerate(moves)]

    def kernel(x0, x1, d0, d1, *refs):
        weight_refs, (hidden0, hidden1, pre0, pre1, in0, in1, out0, out1, up_ref, down_ref, sems) = (
            refs[: len(weights)],
            refs[len(weights) :],
        )

        @pl.when(pl.program_id(0) == 0)
        def _():
            loads = copies(weight_refs, up_ref, down_ref, sems)
            for load in loads:
                load.start()
            for load in loads:
                load.wait()

        x = jnp.concatenate([x0[...], x1[...]])
        d_out = jnp.concatenate([d0[...], d1[...]])
        pre = jnp.dot(x, up_ref[...], preferred_element_type=WIDE)
        d_hidden = dot(d_out, down_ref[...], ((1,), (1,)))
        below, density = normal_parts(pre)
        hidden = (pre * below).astype(LOW)
        d_pre = (d_hidden * (below + pre * density)).astype(LOW)
        d_input = dot(d_pre, up_ref[...], ((1,), (1,)))
        out = jnp.dot(hidden, down_ref[...], preferred_element_type=WIDE)
        for side, (hidden_ref, pre_ref, in_ref, out_ref) in enumerate(
            ((hidden0, pre0, in0, out0), (hidden1, pre1, in1, out1))
        ):
            mine = slice(side * block, (side + 1) * block)
            hidden_ref[...] = hidden[mine]
            pre_ref[...] = d_pre[mine]
            in_ref[...] = d_input[mine].astype(in_ref.dtype)
            out_ref[...] = out[mine].astype(out_ref.dtype)

    wide = pl.BlockSpec((block, model_width), lambda i: (i, 0))
    narrow = pl.BlockSpec((block, hidden_units), lambda i: (i, 0))
    low = jax.ShapeDtypeStruct((rows, hidden_units), LOW)
    outs = pl.pallas_call(
        kernel,
        grid=(rows // block,),
        out_shape=(
            low,
            low,
            low,
            low,
            jax.ShapeDtypeStruct((rows, model_width), WIDE),
            jax.ShapeDtypeStruct((rows, model_width), LOW),
            jax.ShapeDtypeStruct((rows, model_width), WIDE),
            jax.ShapeDtypeStruct((rows, model_width), LOW),
        ),
        in_specs=[wide] * 4 + [pl.BlockSpec(memory_space=pl.ANY)] * len(weights),
        out_specs=(narrow,) * 4 + (wide,) * 4,
        scratch_shapes=[
            pltpu.VMEM((model_width, hidden_units), LOW),
            pltpu.VMEM((hidden_units, model_width), LOW),
            pltpu.SemaphoreType.DMA(((folds + 1) * deep,)),
        ],
        compiler_params=pltpu.CompilerParams(vmem_limit_bytes=32 * 2**20),
        cost_estimate=BRIEF,
    )(*xs, *d_outs, *weights)
    return outs[0:2], outs[2:4], outs[4:6], outs[6:8]


def ffn_outer(xs, d_outs, hidden, d_pre, deep, unit):
    model_width = xs[0].shape[1]
    hidden_units = deep * unit
    folds = model_width // hidden_units

    def kernel(x0, x1, d0, d1, h0, h1, p0, p1, out_ref):
        def both(left0, right0, left1, right1):
            total = dot(left0[...], right0[...], ((0,), (0,)))
            return (total + dot(left1[...], right1[...], ((0,), (0,)))).astype(LOW)

        down = both(h0, d0, h1, d1)
        for z in range(deep):
            out_ref[z, :unit] = down[z * unit : (z + 1) * unit]
        up = both(x0, p0, x1, p1)
        for z in range(deep):
            for fold in range(folds):
                rows = up[(z * folds + fold) * unit : (z * folds + fold + 1) * unit]
                out_ref[z, unit:, fold * hidden_units : (fold + 1) * hidden_units] = rows

    if not (whole_tiles(unit) and hidden_units % 128 == 0):
        pairs = ((hidden, d_outs), (xs, d_pre))
        down, up = (
            sum(outer(left, right) for left, right in zip(*pair_of, strict=True)).astype(LOW)
            for pair_of in pairs
        )
        down = down.reshape(deep, unit, model_width)
        return jnp.concatenate([down, fold_up(up.reshape(deep, -1, hidden_units), folds)], axis=1)
    whole = pl.BlockSpec(memory_space=pltpu.VMEM)
    return pl.pallas_call(
        kernel,
        out_shape=jax.ShapeDtypeStruct((deep, 2 * unit, model_width), LOW),
        in_specs=[whole] * 8,
        out_specs=whole,
        compiler_params=pltpu.CompilerParams(vmem_limit_bytes=56 * 2**20),
        cost_estimate=BRIEF,
    )(*xs, *d_outs, *hidden, *d_pre)


def attend_back(d_mixed, query, keyval, probs):
    slots, lat_rows, half_width = query.shape
    key_rows = keyval.shape[1]
    patches = key_rows - lat_rows
    chunk = PACK * HEAD
    groups = half_width // chunk
    scale = 1.0 / math.sqrt(HEAD)

    def kernel(d_ref, query_ref, keyval_ref, probs_ref, out_ref):
        mask_low, mask_wide = head_mask(lat_rows, LOW), head_mask(lat_rows, WIDE)
        out_ref[0, :patches, :half_width] = jnp.zeros((patches, half_width), LOW)
        for part in range(groups):
            columns = slice(part * chunk, (part + 1) * chunk)
            q = tile_heads(query_ref[0, :, columns], mask_low)
            d = tile_heads(d_ref[0, :, columns], mask_low)
            k = keyval_ref[0, :, columns]
            v = keyval_ref[0, :, half_width + part * chunk : half_width + (part + 1) * chunk]
            p = probs_ref[0, part]
            d_probs = dot(d, v, ((1,), (1,)))
            d_value = dot(p.astype(LOW), d, ((0,), (0,)))
            delta = jnp.sum(p * d_probs, axis=1, keepdims=True)
            d_scores = (p * (d_probs - delta)).astype(LOW)
            d_query = untile_heads(jnp.dot(d_scores, k, preferred_element_type=WIDE), mask_wide)
            d_key = dot(d_scores, q, ((0,), (0,)))
            out_ref[0, patches:, columns] = (d_query * scale).astype(LOW)
            out_ref[0, :, half_width + part * chunk : half_width + (part + 1) * chunk] = (
                d_key * scale
            ).astype(LOW)
            out_ref[0, :, 2 * half_width + part * chunk : 2 * half_width + (part + 1) * chunk] = (
                d_value.astype(LOW)
            )

    def slotted(*block):
        return pl.BlockSpec((1, *block), lambda i: (i,) + (0,) * len(block))

    return pl.pallas_call(
        kernel,
        grid=(slots,),
        out_shape=jax.ShapeDtypeStruct((slots, key_rows, 3 * half_width), LOW),
        in_specs=[
            slotted(lat_rows, half_width),
            slotted(lat_rows, half_width),
            slotted(key_rows, 2 * half_width),
            slotted(groups, PACK * lat_rows, key_rows),
        ],
        out_specs=slotted(key_rows, 3 * half_width),
        compiler_params=pltpu.CompilerParams(vmem_limit_bytes=32 * 2**20),
        cost_estimate=BRIEF,
    )(d_mixed, query, keyval, probs)


def on_device(
    wires,
    media,
    latents,
    upstream,
    time_index,
    live_count,
    time_table,
    media_gain,
    media_bias,
    latent_gain,
    latent_bias,
    ff_gain,
    ff_bias,
    w_query,
    w_keyval,
    w_out,
    w_up,
    w_down,
):
    wires.place()
    deep, flat, count = wires.deep, wires.flat, wires.count
    images, patches, model_width = media.shape
    lat_rows = latents.shape[1]
    key_rows = patches + lat_rows
    table_rows, shard = time_table.shape
    group = model_width // (2 * deep)
    half_width = model_width // 2
    slots = 2 * images

    qkv_mine, qkv_other = deal_columns(wires.c, (w_query, w_keyval), group)
    qkv_arrived = wires.send(qkv_other, "core")
    raw = jnp.concatenate([after(media, qkv_other), latents], axis=1)
    far_raw = wires.send(raw, "core")
    qkv_block = pair(qkv_mine, qkv_arrived, wires.c, 0)

    unit = w_down.shape[0]
    hidden_units = deep * unit
    tall, wide = 2 * shard, 3 * half_width
    folds = model_width // hidden_units
    ring_block = jnp.concatenate(
        [qkv_block.reshape(tall, wide), jnp.pad(w_out, ((0, 0), (0, wide - model_width)))]
    )
    smalls = jnp.concatenate(
        [time_table]
        + [v[None] for v in (media_gain, media_bias, latent_gain, latent_bias, ff_gain, ff_bias)],
        axis=0,
    )
    smalls = jnp.broadcast_to(smalls[None], (count, *smalls.shape))
    made = {}

    made["smalls"] = lax.all_to_all(smalls, AXES, 0, 0, tiled=True)

    def swap_up(first):
        shares = split_units(after(w_up, made["smalls"], first[wires.bits[-1]]), 2 * flat, unit)
        up_block = wires.swap_blocks(shares, wires.planes).reshape(-1, hidden_units)
        block = jnp.concatenate([w_down, fold_up(up_block, folds)])
        made["ffn"] = jnp.broadcast_to(block[None], (deep, *block.shape))
        return (made["ffn"],)

    d_out_low = after(upstream, qkv_other) * (jnp.arange(images) < live_count[0]).astype(LOW)[:, None, None]
    rings, gathered, d_out_got, steps = gather_rows(
        wires,
        ring_block,
        lambda block: block[:tall].reshape(2, shard, wide),
        after(d_out_low, made["smalls"]),
        {2: swap_up},
        (far_raw,),
    )
    places, pieces = [], []
    for step, got in enumerate(gathered):
        for mask, part in got.items():
            pieces += part if isinstance(part, tuple) else [part]
            for core in range(2):
                places.append((wires.plane(step) * 2 + core) * flat + (wires.f ^ mask))
    out_column = [ring[tall:, :model_width] for ring in rings]
    for mask in wires.masks:
        if mask not in d_out_got:
            d_out_got[mask] = wires.send(d_out_low, mask, *steps[-1])


    ffn_blocks = wires.swap_blocks(after(made["ffn"], rings[-1]), wires.columns)

    smalls = after(made["smalls"], *steps[-2][-1:])
    smalls = smalls.transpose(1, 0, 2).reshape(-1, model_width).astype(WIDE)
    norm_params = smalls[table_rows : table_rows + 4]
    ff_params = smalls[table_rows + 4 :]
    live_mask = (jnp.arange(images) < live_count[0]).astype(WIDE)[:, None, None]
    one_hot = (time_index[:, None] == jnp.arange(table_rows)[None, :]).astype(WIDE)
    time_rows = jnp.dot(one_hot, smalls[:table_rows], precision=HIGHEST)
    both_rows = jnp.concatenate([time_rows, wires.send(time_rows, "core")])

    out_places, out_pieces = [], []
    for mask, part in spread_plane(wires, jnp.stack(out_column), *steps[-1]).items():
        out_pieces.append(part)
        for step in range(deep):
            out_places.append(wires.plane(step) * flat + (wires.f ^ mask))


    qkv_full, sources, query, keyval, probs, mixed = attend(
        places,
        pieces,
        raw,
        far_raw,
        both_rows,
        norm_params,
        patches,
        half_width,
    )
    out_full, branch = project_out(
        out_places, out_pieces, after(mixed, *d_out_got.values()), model_width
    )
    branch = branch[:images] + wires.send(branch[images:], "core")
    middle = latents.astype(WIDE) + branch

    ffn_normed, ffn_norm_back = jax.vjp(norm_rows, middle, ff_params[0], ff_params[1])
    d_out = upstream.astype(WIDE) * live_mask

    def swapped(blocks, *ahead):
        mine = jnp.stack(blocks)
        far = wires.send(mine, "core", *ahead)
        return mine.reshape(-1, model_width), far.reshape(-1, model_width)

    ffn_low = ffn_normed.astype(LOW)
    ffn_got = spread_plane(wires, ffn_low)
    d_out_got = {mask: after(part, ffn_low) for mask, part in d_out_got.items()}
    order = [0, *wires.masks]
    d_out_rows = swapped([d_out_got[mask] for mask in order])
    ffn_rows = swapped([ffn_got[mask] for mask in order])
    hidden, d_pre, d_inputs, results = ffn_rows_back(
        ffn_blocks, ffn_rows, d_out_rows, unit
    )
    block_shape = (images, lat_rows, model_width)

    def collect_core(parts, *ahead):
        arrived = wires.send(parts[1], "core", *ahead)
        rows = (parts[0] + arrived.astype(WIDE)).reshape(len(order), *block_shape)
        return dict(zip(order, rows, strict=True)), arrived

    d_sums, d_swapped = collect_core(d_inputs)
    ffn_partial = ffn_outer(
        ffn_rows, d_out_rows, hidden, (after(d_pre[0], d_swapped), d_pre[1]), deep, unit
    )
    ffn_terms = wires.swap_blocks(ffn_partial, wires.columns)
    d_ffn_input, _ = sum_plane(wires, d_sums.get)
    d_ffn_input = after(d_ffn_input, ffn_partial)
    d_middle_norm, ff_gain_grad, ff_bias_grad = ffn_norm_back(d_ffn_input)
    d_middle = d_out + d_middle_norm

    own_branch = d_middle.astype(LOW)
    d_branch = jnp.concatenate([own_branch, wires.send(own_branch, "core")], axis=0)
    out_partial = outer(mixed.reshape(-1, half_width), d_branch.reshape(-1, model_width))
    out_partial = out_partial.astype(LOW).reshape(deep, flat, shard, model_width)
    out_partial = jnp.stack([out_partial[..., :half_width], out_partial[..., half_width:]], axis=2)
    d_mixed = rows_back(after(d_branch, out_partial), out_full).astype(LOW)
    d_projected = attend_back(d_mixed, query, keyval, probs)

    source_rows = sources.reshape(-1, model_width)
    d_projected_rows = d_projected.reshape(-1, wide)
    plane_rows = 2 * flat * shard

    kept = {}

    def results_clock(*ahead):
        result_sums, arrived = collect_core(results, *ahead)
        kept["own"] = result_sums[0]
        kept["low"] = {mask: rows.astype(LOW) for mask, rows in result_sums.items()}
        return arrived

    def far_back(_):
        kept["far"] = rows_back(d_projected[images:], qkv_full).astype(LOW)
        return (kept["far"], *kept["low"].values())

    def far_clock(*ahead):
        kept["far"] = wires.send(kept["far"], "core", *ahead)
        return kept["far"]

    def norms_back(arrived):
        media_grad, latent_grad, sums = sources_back(
            after(d_projected[:images], arrived),
            qkv_full,
            kept["far"],
            raw,
            time_rows,
            norm_params,
            d_middle,
        )
        table_part = jnp.dot(one_hot.T, sums[:, 0], precision=HIGHEST)
        small_grads = [table_part, jnp.sum(sums[:, 1:5], axis=0), ff_gain_grad[None], ff_bias_grad[None]]
        small_grads = jnp.concatenate(small_grads).reshape(-1, count, shard).transpose(1, 0, 2)
        kept["media"], kept["latent"], kept["small"] = media_grad, latent_grad, small_grads
        return media_grad, small_grads

    def last_pull(_):
        ffn_sum = jnp.sum(ffn_terms.astype(WIDE), axis=0)
        kept["down"] = ffn_sum[:unit]
        up_sum = unfold_up(ffn_sum[unit:].astype(LOW), folds)
        kept["up"] = up_sum.reshape(2 * flat, shard, hidden_units)
        return (kept["up"],)

    result_got = []

    def send_result(mask):
        def ride(ahead):
            result_got.append(wires.send(kept["low"][mask], mask, *ahead))
            return result_got[-1]

        return ride

    turning = [mask for mask in wires.masks if mask & (mask - 1)]
    riders = {
        1: [send_result(mask) for mask in turning],
        deep: [send_result(mask) for mask in wires.bits],
    }

    def partial_rows(step, d_rows):
        at_plane = wires.plane(1 + step)
        rows = lax.dynamic_slice_in_dim(source_rows, at_plane * plane_rows, plane_rows, 1)
        block = outer(rows, d_rows).astype(LOW).reshape(2, flat, shard, wide)
        return block, at(out_partial, at_plane, 0)

    partials = [partial_rows(step, d_projected_rows) for step in range(deep)]

    def part(step, mask):
        block, out_block = partials[step]
        target = wires.f ^ mask
        return jnp.concatenate([at(block, target, 1), at(out_block, target, 0)], axis=-1)

    total = scatter_rows(
        wires,
        part,
        {
            1: far_back,
            3: norms_back,
            4: last_pull,
        },
        riders,
        {0: results_clock, 2: far_clock},
    )
    qkv_sum = total[..., :wide]
    w_out_grad = jnp.concatenate([total[0, :, wide:], total[1, :, wide:]], axis=-1)
    media_grad, latent_grad = kept["media"], kept["latent"]
    w_down_grad = kept["down"]
    up_sum = wires.swap_blocks(kept["up"], wires.planes)
    w_up_grad = merge_units(up_sum, unit)
    small_grads = lax.all_to_all(after(kept["small"], up_sum), AXES, 0, 0, tiled=True)
    small_grads = jnp.sum(small_grads, axis=0)
    own_result = sum([rows.astype(WIDE) for rows in result_got], kept["own"])
    latents_out = ((middle + own_result) * live_mask).astype(LOW)
    qkv_own = pick(qkv_sum, wires.c, 0)
    qkv_far = wires.send(pick(qkv_sum, 1 - wires.c, 0), "core", small_grads)
    w_query_grad, w_keyval_grad = join_columns(
        wires.c, qkv_own, qkv_far, (model_width, 2 * model_width), group
    )
    return (
        latents_out,
        media_grad,
        latent_grad,
        small_grads[:table_rows],
        *[small_grads[table_rows + k] for k in range(6)],
        w_query_grad,
        w_keyval_grad,
        w_out_grad,
        w_up_grad,
        w_down_grad,
    )


def solution(mesh):
    lead = P(AXES)
    table = P(None, AXES)
    return jax.shard_map(
        functools.partial(on_device, Wires(mesh)),
        mesh=mesh,
        in_specs=(lead,) * 5 + (table,) + (lead,) * 11,
        out_specs=(lead,) * 3 + (table,) + (lead,) * 11,
        check_vma=False,
    )
```

```python
import functools
import math

import jax
import jax.numpy as jnp
from jax import lax
from jax.experimental import pallas as pl
from jax.experimental.pallas import tpu as pltpu
from jax.sharding import PartitionSpec as P

HEAD = 96
PACK = 4
AXES = ("dp", "fsdp")
LOW = jnp.bfloat16
WIDE = jnp.float32
HIGHEST = lax.Precision.HIGHEST
NORM_EPS = 1e-05
BRIEF = pl.CostEstimate(flops=1, bytes_accessed=1, transcendentals=0)


def norm_rows(inputs, gain, shift):
    row_mean = jnp.mean(inputs, axis=-1, keepdims=True)
    centered = inputs - row_mean
    variance = jnp.mean(centered * centered, axis=-1, keepdims=True)
    return centered * lax.rsqrt(variance + NORM_EPS) * gain + shift


def exact_gelu(inputs):
    return jax.nn.gelu(inputs, approximate=False)


def dot(left, right, contract):
    return lax.dot_general(left, right, (contract, ((), ())), preferred_element_type=WIDE)


def rows_by(left, right):
    return dot(left, right, ((left.ndim - 1,), (0,)))


def rows_back(left, right):
    return dot(left, right, ((left.ndim - 1,), (1,)))


def outer(left, right):
    return dot(left, right, ((0,), (0,)))


class Wires:
    def __init__(self, mesh):
        self.deep = mesh.shape["dp"] // 2
        self.flat = mesh.shape["fsdp"]
        self.count = 2 * self.deep * self.flat
        places = [
            (z, c, f) for z in range(self.deep) for c in range(2) for f in range(self.flat)
        ]

        def number(z, c, f):
            return (z * 2 + c) * self.flat + f

        def moves(target):
            return [(number(*place), number(*target(*place))) for place in places]

        self.bits = [1 << k for k in range(self.flat.bit_length() - 1)]
        self.masks = list(range(1, self.flat))
        self.moves = {
            "core": moves(lambda z, c, f: (z, 1 - c, f)),
        }
        self.moves["rise"] = moves(lambda z, c, f: ((z + 1) % self.deep, c, f))
        self.columns = [
            [number(z, c, f) for z in range(self.deep)] for c in range(2) for f in range(self.flat)
        ]
        self.planes = [
            [number(z, c, f) for c in range(2) for f in range(self.flat)] for z in range(self.deep)
        ]
        for mask in self.masks:
            self.moves[mask] = moves(lambda z, c, f, mask=mask: (z, c, f ^ mask))

    def place(self):
        outer_at = lax.axis_index("dp")
        self.z, self.c = outer_at // 2, outer_at % 2
        self.f = lax.axis_index("fsdp")
        self.queues = {}

    def send(self, block, kind, *ahead):
        if ahead:
            block = after(block, *ahead)
        return lax.ppermute(block, AXES, self.moves[kind])

    def swap_blocks(self, blocks, groups):
        return lax.all_to_all(blocks, AXES, 0, 0, tiled=True, axis_index_groups=groups)

    def plane(self, step):
        return lax.rem(self.z + 2 * self.deep - step, self.deep)


def after(block, *others):
    return lax.optimization_barrier((block, *others))[0]


def at(array, index, axis):
    return lax.dynamic_index_in_dim(array, index, axis, keepdims=False)


def pair(mine, other, side, axis):
    return jnp.where(
        side == 0, jnp.stack([mine, other], axis=axis), jnp.stack([other, mine], axis=axis)
    )


def pick(array, side, axis):
    return jnp.where(
        side == 0,
        lax.index_in_dim(array, 0, axis, keepdims=False),
        lax.index_in_dim(array, 1, axis, keepdims=False),
    )


def corner(mask):
    return mask & -mask, 1 << (mask.bit_length() - 1)


def gather_rows(wires, block, take, guest, hooks, before):
    rings, gathered, guests = [block], [], {0: guest}
    single = [mask for mask in wires.masks if not mask & (mask - 1)]
    multiple = sorted((m for m in wires.masks if m & (m - 1)), key=lambda m: bin(m).count("1"))
    steps = []
    for step in range(wires.deep + 1):
        now = []
        before = (*before, *(hooks[step](gathered[0]) if step in hooks else ()))
        if step < wires.deep:
            if step + 1 < wires.deep:
                rings.append(wires.send(rings[step], "rise", *before))
                now.append(rings[-1])
            mine = take(rings[step])
            got = {0: mine}
            for mask in single:
                got[mask] = wires.send(mine, mask, *before)
                now.append(got[mask])
            gathered.append(got)
        if step == 0:
            for mask in single:
                guests[mask] = wires.send(guest, mask, *before)
                now.append(guests[mask])
        if step:
            got = gathered[step - 1]
            for mask in multiple:
                low, high = corner(mask)
                got[mask] = (
                    wires.send(got[mask ^ high][0], high, *before),
                    wires.send(got[mask ^ low][1], low, *before),
                )
                now += got[mask]
        before = now
        steps.append(now)
    return rings, gathered, guests, steps


def scatter_rows(wires, part, pulls, riders, clocks):
    single = [mask for mask in wires.masks if not mask & (mask - 1)]
    multiple = sorted((m for m in wires.masks if m & (m - 1)), key=lambda m: -bin(m).count("1"))
    extra = [{} for _ in range(wires.deep)]
    before, total, clock = (), None, None
    for step in range(wires.deep + 3):
        now, ready = [], []
        ahead = (*(before if step else ()), *(pulls[step](clock) if step in pulls else ()))

        def term(block, mask, half=None):
            mine = part(block, mask)
            if half is not None:
                mine = mine[half]
            more = extra[block].get((mask, half), [])
            return sum([m.astype(WIDE) for m in more], mine).astype(LOW)

        block = step - 3
        if 0 <= block:
            total = (
                sum([m.astype(WIDE) for m in extra[block][0, None]], part(block, 0).astype(WIDE))
                + (0.0 if total is None else total)
            )
            if block == wires.deep - 1:
                return total
            arrived = wires.send(total.astype(LOW), "rise", *ahead)
            now.append(arrived)
            total = arrived.astype(WIDE)
        block = step - 1
        if 0 <= block < wires.deep:
            for mask in single:
                leaving = jnp.stack([term(block, mask, half) for half in range(2)])
                ready.append(leaving)
                arrived = wires.send(leaving, mask, *ahead)
                extra[block].setdefault((0, None), []).append(arrived)
                now.append(arrived)
        if step < wires.deep:
            for mask in multiple:
                low, high = corner(mask)
                for half, bit in ((0, high), (1, low)):
                    leaving = term(step, mask, half)
                    ready.append(leaving)
                    arrived = wires.send(leaving, bit, *ahead)
                    extra[step].setdefault((mask ^ bit, half), []).append(arrived)
                    now.append(arrived)
        clock = clocks[step](*ahead, *ready) if step in clocks else now[-1]
        for rider in riders.get(step, ()):
            now.append(rider(ahead))
        before = now


def spread_plane(wires, block, *ahead):
    got = {0: block}
    for mask in reversed(wires.masks):
        got[mask] = wires.send(block, mask, *ahead)
    return got


def sum_plane(wires, part, *ahead):
    arrived = [wires.send(part(mask).astype(LOW), mask, *ahead) for mask in reversed(wires.masks)]
    return sum([block.astype(WIDE) for block in arrived], part(0).astype(WIDE)), arrived


def lay(places, pieces, count):
    entry = pieces[0].shape[1:]
    views = [(k, i) for k, piece in enumerate(pieces) for i in range(piece.shape[0])]
    number = len(views)

    def kernel(places_ref, *refs):
        out_ref, held, sems = refs[-3:]
        loads = [
            pltpu.make_async_copy(refs[k].at[i], held.at[n], sems.at[0, n])
            for n, (k, i) in enumerate(views)
        ]
        stores = [
            pltpu.make_async_copy(held.at[n], out_ref.at[places_ref[n]], sems.at[1, n])
            for n in range(number)
        ]
        for load in loads:
            load.start()
        for load, store in zip(loads, stores, strict=True):
            load.wait()
            store.start()
        for store in stores:
            store.wait()

    anywhere = pl.BlockSpec(memory_space=pl.ANY)
    return pl.pallas_call(
        kernel,
        out_shape=jax.ShapeDtypeStruct((count,) + entry, pieces[0].dtype),
        in_specs=[pl.BlockSpec(memory_space=pltpu.SMEM)] + [anywhere] * len(pieces),
        out_specs=anywhere,
        scratch_shapes=[
            pltpu.VMEM((number,) + entry, pieces[0].dtype),
            pltpu.SemaphoreType.DMA((2, number)),
        ],
        compiler_params=pltpu.CompilerParams(vmem_limit_bytes=58 * 2**20),
    )(jnp.stack(places).astype(jnp.int32), *pieces)


def whole_tiles(rows):
    return rows % 16 == 0


def joined(places, pieces):
    shard = pieces[0].shape[-2]
    if whole_tiles(shard):
        return places, pieces
    rows = [row for piece in pieces for row in (piece if piece.ndim == 3 else (piece,))]
    full = jnp.zeros((len(rows), *rows[0].shape), rows[0].dtype)
    for place, row in zip(places, rows, strict=True):
        full = lax.dynamic_update_index_in_dim(full, row, place, 0)
    return [jnp.zeros((), jnp.int32)], [full.reshape(1, len(rows) * shard, -1)]


def on_chip(kernel, out_shape, side, *operands):
    whole = pl.BlockSpec(memory_space=pltpu.VMEM)
    return pl.pallas_call(
        kernel,
        out_shape=out_shape,
        in_specs=[pl.BlockSpec(memory_space=pltpu.SMEM)] + [whole] * len(operands),
        out_specs=jax.tree.map(lambda _: whole, out_shape),
    )(side.reshape(1).astype(jnp.int32), *operands)


def deal_columns(side, arrays, group):
    shard = arrays[0].shape[0]
    width = sum(array.shape[1] for array in arrays) // 2
    if not whole_tiles(shard):
        both = jnp.concatenate(arrays, axis=1).reshape(shard, -1, 2, group)
        return tuple(pick(both, s, 2).reshape(shard, width) for s in (side, 1 - side))

    def kernel(side_ref, *refs):
        *in_refs, own_ref, other_ref = refs
        first = side_ref[0] == 0
        base = 0
        for ref in in_refs:
            block = ref[...]
            count = block.shape[1] // (2 * group)
            hands = [
                jnp.concatenate(
                    [block[:, (2 * j + s) * group : (2 * j + s + 1) * group] for j in range(count)],
                    axis=1,
                )
                for s in range(2)
            ]
            own_ref[:, base : base + count * group] = jnp.where(first, hands[0], hands[1])
            other_ref[:, base : base + count * group] = jnp.where(first, hands[1], hands[0])
            base += count * group

    shape = jax.ShapeDtypeStruct((shard, width), arrays[0].dtype)
    return on_chip(kernel, (shape, shape), side, *arrays)


def join_columns(side, own, other, widths, group):
    shard = own.shape[0]
    if not whole_tiles(shard):
        halves = [part.reshape(shard, -1, group) for part in (own, other)]
        both = pair(halves[0], halves[1], side, 2).reshape(shard, -1)
        return tuple(jnp.split(both, [widths[0]], axis=1))

    def kernel(side_ref, own_ref, other_ref, *out_refs):
        first = side_ref[0] == 0
        hands = (
            jnp.where(first, own_ref[...], other_ref[...]),
            jnp.where(first, other_ref[...], own_ref[...]),
        )
        base = 0
        for ref in out_refs:
            parts = []
            for j in range(ref.shape[1] // (2 * group)):
                columns = slice(base + j * group, base + (j + 1) * group)
                parts += [hand[:, columns] for hand in hands]
            ref[...] = jnp.concatenate(parts, axis=1)
            base += ref.shape[1] // 2

    shapes = tuple(jax.ShapeDtypeStruct((own.shape[0], width), own.dtype) for width in widths)
    return on_chip(kernel, shapes, side, own, other)


def split_units(array, ways, unit):
    shard, width = array.shape
    deep = width // (ways * unit)
    if not whole_tiles(shard):
        blocks = array.reshape(shard, deep, ways, unit).transpose(2, 0, 1, 3)
        return blocks.reshape(ways, shard, deep * unit)

    def kernel(_, in_ref, out_ref):
        block = in_ref[...]
        for way in range(ways):
            parts = [
                block[:, (z * ways + way) * unit : (z * ways + way + 1) * unit] for z in range(deep)
            ]
            out_ref[way] = jnp.concatenate(parts, axis=1)

    shape = jax.ShapeDtypeStruct((ways, shard, deep * unit), array.dtype)
    return on_chip(kernel, shape, jnp.zeros((), jnp.int32), array)


def merge_units(blocks, unit):
    ways, shard, part = blocks.shape
    deep = part // unit
    if not whole_tiles(shard):
        blocks = blocks.reshape(ways, shard, deep, unit).transpose(1, 2, 0, 3)
        return blocks.reshape(shard, -1).astype(WIDE)

    def kernel(_, in_ref, out_ref):
        parts = []
        for z in range(deep):
            for way in range(ways):
                parts.append(in_ref[way][:, z * unit : (z + 1) * unit].astype(WIDE))
        out_ref[...] = jnp.concatenate(parts, axis=1)

    shape = jax.ShapeDtypeStruct((shard, deep * ways * unit), WIDE)
    return on_chip(kernel, shape, jnp.zeros((), jnp.int32), blocks)


def tile_heads(rows, mask):
    return jnp.concatenate([rows] * PACK, axis=0) * mask


def untile_heads(rows, mask):
    kept = rows * mask
    size = rows.shape[0] // PACK
    return sum(kept[k * size : (k + 1) * size] for k in range(PACK))


def head_mask(rows, dtype):
    row = lax.broadcasted_iota(jnp.int32, (PACK * rows, PACK * HEAD), 0) // rows
    column = lax.broadcasted_iota(jnp.int32, (PACK * rows, PACK * HEAD), 1) // HEAD
    return (row == column).astype(WIDE).astype(dtype)


def normed(rows, gain, shift):
    centered = rows - jnp.mean(rows, axis=-1, keepdims=True)
    inverse = lax.rsqrt(jnp.mean(centered * centered, axis=-1, keepdims=True) + NORM_EPS)
    unit = centered * inverse
    return unit * gain + shift, unit, inverse


def attend(places, pieces, own, far, time_rows, norm_rows_of, patches, half_width):
    images, key_rows, model_width = own.shape
    lat_rows = key_rows - patches
    slots = 2 * images
    width = 3 * half_width
    places, pieces = joined(places, pieces)
    chunk = PACK * HEAD
    groups = half_width // chunk
    scale = 1.0 / math.sqrt(HEAD)
    shard = pieces[0].shape[-2]
    views = []
    for k, piece in enumerate(pieces):
        views += [(k, None)] if piece.ndim == 2 else [(k, core) for core in range(piece.shape[0])]

    def kernel(places_ref, *refs):
        piece_refs = refs[: len(pieces)]
        (
            own_ref,
            far_ref,
            time_ref,
            params_ref,
            full_ref,
            sources_ref,
            query_ref,
            keyval_ref,
            probs_ref,
            mixed_ref,
            w_ref,
            sems,
        ) = refs[len(pieces) :]
        slot = pl.program_id(0)
        loads = []
        for i, (k, core) in enumerate(views):
            source = piece_refs[k] if core is None else piece_refs[k].at[core]
            start = pl.multiple_of(places_ref[i] * shard, shard)
            loads.append(pltpu.make_async_copy(source, w_ref.at[pl.ds(start, shard)], sems.at[i]))

        @pl.when(slot == 0)
        def _():
            for load in loads:
                load.start()

        def save():
            return pltpu.make_async_copy(w_ref, full_ref, sems.at[len(views)])

        raw = jnp.where(slot < images, own_ref[0], far_ref[0]).astype(WIDE)
        media = raw[:patches] + time_ref[0]
        sources_ref[0, :patches] = normed(media, params_ref[0:1], params_ref[1:2])[0].astype(LOW)
        lat = normed(raw[patches:], params_ref[2:3], params_ref[3:4])[0]
        sources_ref[0, patches:] = lat.astype(LOW)

        @pl.when(slot == 0)
        def _():
            for load in loads:
                load.wait()
            save().start()

        x = sources_ref[0]
        mask_low, mask_wide = head_mask(lat_rows, LOW), head_mask(lat_rows, WIDE)

        def project(rows, part):
            w = w_ref[:, part * chunk : (part + 1) * chunk]
            return jnp.dot(rows, w, preferred_element_type=WIDE).astype(LOW)

        for part in range(groups):
            columns = slice(part * chunk, (part + 1) * chunk)
            query = project(x[patches:], part)
            query_ref[0, :, columns] = query
            k = project(x, groups + part)
            keyval_ref[0, :, columns] = k
            v = project(x, 2 * groups + part)
            keyval_ref[0, :, half_width + part * chunk : half_width + (part + 1) * chunk] = v
            s = dot(tile_heads(query, mask_low), k, ((1,), (1,)))
            e = jnp.exp((s - jnp.max(s, axis=1, keepdims=True)) * scale)
            p = e * (1.0 / jnp.sum(e, axis=1, keepdims=True))
            probs_ref[0, part] = p
            m = jnp.dot(p.astype(LOW), v, preferred_element_type=WIDE)
            mixed_ref[0, :, columns] = untile_heads(m, mask_wide).astype(LOW)

        @pl.when(slot == slots - 1)
        def _():
            save().wait()

    anywhere = pl.BlockSpec(memory_space=pl.ANY)
    whole = pl.BlockSpec(memory_space=pltpu.VMEM)

    def slotted(*block):
        return pl.BlockSpec((1, *block), lambda i: (i,) + (0,) * len(block))

    def halved(first, *block):
        if first:
            return pl.BlockSpec((1, *block), lambda i: (jnp.minimum(i, images - 1), 0, 0))
        return pl.BlockSpec((1, *block), lambda i: (jnp.maximum(i - images, 0), 0, 0))

    return pl.pallas_call(
        kernel,
        grid=(slots,),
        out_shape=(
            jax.ShapeDtypeStruct((model_width, width), LOW),
            jax.ShapeDtypeStruct((slots, key_rows, model_width), LOW),
            jax.ShapeDtypeStruct((slots, lat_rows, half_width), LOW),
            jax.ShapeDtypeStruct((slots, key_rows, 2 * half_width), LOW),
            jax.ShapeDtypeStruct((slots, groups, PACK * lat_rows, key_rows), WIDE),
            jax.ShapeDtypeStruct((slots, lat_rows, half_width), LOW),
        ),
        in_specs=[pl.BlockSpec(memory_space=pltpu.SMEM)]
        + [anywhere] * len(pieces)
        + [
            halved(True, key_rows, model_width),
            halved(False, key_rows, model_width),
            slotted(1, model_width),
            whole,
        ],
        out_specs=(
            anywhere,
            slotted(key_rows, model_width),
            slotted(lat_rows, half_width),
            slotted(key_rows, 2 * half_width),
            slotted(groups, PACK * lat_rows, key_rows),
            slotted(lat_rows, half_width),
        ),
        scratch_shapes=[
            pltpu.VMEM((model_width, width), LOW),
            pltpu.SemaphoreType.DMA((len(views) + 1,)),
        ],
        compiler_params=pltpu.CompilerParams(vmem_limit_bytes=58 * 2**20),
        cost_estimate=BRIEF,
    )(jnp.stack(places).astype(jnp.int32), *pieces, own, far, time_rows[:, None], norm_rows_of)


def sources_back(d_projected, projections, far_part, own, time_rows, norm_rows_of, d_middle):
    images, key_rows, model_width = own.shape
    lat_rows = d_middle.shape[1]
    patches = key_rows - lat_rows
    width = d_projected.shape[-1]

    def kernel(d_ref, w_ref, far_ref, raw_ref, time_ref, params_ref, mid_ref, m_out, l_out, s_out):
        d = dot(d_ref[0], w_ref[...], ((1,), (1,))) + far_ref[0].astype(WIDE)

        def back(rows, d_rows, gain, shift):
            _, unit, inverse = normed(rows, gain, shift)
            scaled = d_rows * gain
            along = jnp.mean(scaled * unit, axis=-1, keepdims=True)
            inner = scaled - jnp.mean(scaled, axis=-1, keepdims=True) - unit * along
            sums = (
                jnp.sum(d_rows * unit, axis=0, keepdims=True),
                jnp.sum(d_rows, axis=0, keepdims=True),
            )
            return inverse * inner, sums

        rows = raw_ref[0, :patches].astype(WIDE) + time_ref[0]
        d_media, media_sums = back(rows, d[:patches], params_ref[0:1], params_ref[1:2])
        m_out[0] = d_media
        rows = raw_ref[0, patches:].astype(WIDE)
        d_lat, lat_sums = back(rows, d[patches:], params_ref[2:3], params_ref[3:4])
        l_out[0] = mid_ref[0] + d_lat
        total = jnp.sum(d_media, axis=0, keepdims=True)
        s_out[0] = jnp.concatenate(
            [total, *media_sums, *lat_sums, jnp.zeros((3, model_width), WIDE)], axis=0
        )

    whole = pl.BlockSpec(memory_space=pltpu.VMEM)

    def slotted(*block):
        return pl.BlockSpec((1, *block), lambda i: (i,) + (0,) * len(block))

    return pl.pallas_call(
        kernel,
        grid=(images,),
        out_shape=(
            jax.ShapeDtypeStruct((images, patches, model_width), WIDE),
            jax.ShapeDtypeStruct((images, lat_rows, model_width), WIDE),
            jax.ShapeDtypeStruct((images, 8, model_width), WIDE),
        ),
        in_specs=[
            slotted(key_rows, width),
            whole,
            slotted(key_rows, model_width),
            slotted(key_rows, model_width),
            slotted(1, model_width),
            whole,
            slotted(lat_rows, model_width),
        ],
        out_specs=(
            slotted(patches, model_width),
            slotted(lat_rows, model_width),
            slotted(8, model_width),
        ),
        compiler_params=pltpu.CompilerParams(vmem_limit_bytes=48 * 2**20),
        cost_estimate=BRIEF,
    )(d_projected, projections, far_part, own, time_rows[:, None], norm_rows_of, d_middle)


def project_out(places, pieces, mixed, model_width):
    slots, lat_rows, half_width = mixed.shape
    places, pieces = joined(places, pieces)
    shard = pieces[0].shape[-2]
    views = [(k, i) for k, piece in enumerate(pieces) for i in range(piece.shape[0])]
    chunk = PACK * HEAD

    def kernel(places_ref, *refs):
        piece_refs = refs[: len(pieces)]
        mixed_ref, full_ref, branch_ref, w_ref, sems = refs[len(pieces) :]
        loads = []
        for i, (k, entry) in enumerate(views):
            start = pl.multiple_of(places_ref[i] * shard, shard)
            loads.append(
                pltpu.make_async_copy(
                    piece_refs[k].at[entry], w_ref.at[pl.ds(start, shard)], sems.at[i]
                )
            )
        for load in loads:
            load.start()
        for load in loads:
            load.wait()
        save = pltpu.make_async_copy(w_ref, full_ref, sems.at[len(views)])
        save.start()
        rows = mixed_ref[...].reshape(slots * lat_rows, half_width)
        for part in range(model_width // chunk):
            columns = slice(part * chunk, (part + 1) * chunk)
            branch_ref[:, columns] = jnp.dot(
                rows, w_ref[:, columns], preferred_element_type=WIDE
            )
        save.wait()

    anywhere = pl.BlockSpec(memory_space=pl.ANY)
    whole = pl.BlockSpec(memory_space=pltpu.VMEM)
    full, branch = pl.pallas_call(
        kernel,
        out_shape=(
            jax.ShapeDtypeStruct((half_width, model_width), LOW),
            jax.ShapeDtypeStruct((slots * lat_rows, model_width), WIDE),
        ),
        in_specs=[pl.BlockSpec(memory_space=pltpu.SMEM)] + [anywhere] * len(pieces) + [whole],
        out_specs=(anywhere, whole),
        scratch_shapes=[
            pltpu.VMEM((half_width, model_width), LOW),
            pltpu.SemaphoreType.DMA((len(views) + 1,)),
        ],
        compiler_params=pltpu.CompilerParams(vmem_limit_bytes=16 * 2**20),
        cost_estimate=BRIEF,
    )(jnp.stack(places).astype(jnp.int32), *pieces, mixed)
    return full, branch.reshape(slots, lat_rows, model_width)


def normal_parts(x):
    density = jnp.exp(-0.5 * x * x)
    t = 1.0 / (1.0 + (0.3275911 * math.sqrt(0.5)) * jnp.abs(x))
    series = t * (
        0.254829592
        + t * (-0.284496736 + t * (1.421413741 + t * (-1.453152027 + t * 1.061405429)))
    )
    upper = 0.5 * series * density
    return jnp.where(x < 0, upper, 1.0 - upper), density * (1.0 / math.sqrt(2 * math.pi))


def fold_up(block, folds):
    return jnp.concatenate(jnp.split(block, folds, axis=-2), axis=-1)


def unfold_up(block, folds):
    return jnp.concatenate(jnp.split(block, folds, axis=-1), axis=-2)


def ffn_rows_back(ffn_blocks, xs, d_outs, unit):
    deep = ffn_blocks.shape[0]
    hidden_units = deep * unit
    rows, model_width = xs[0].shape
    folds = model_width // hidden_units
    block = 128
    direct = whole_tiles(unit) and hidden_units % 128 == 0
    if direct:
        weights = (ffn_blocks,)
    else:
        weights = (
            unfold_up(ffn_blocks[:, unit:], folds).reshape(model_width, hidden_units),
            ffn_blocks[:, :unit].reshape(hidden_units, model_width),
        )

    def copies(weight_refs, up_ref, down_ref, sems):
        if not direct:
            moves = list(zip(weight_refs, (up_ref, down_ref), strict=True))
        else:
            (ffn_ref,) = weight_refs
            moves = []
            for z in range(deep):
                moves.append((ffn_ref.at[z, pl.ds(0, unit)], down_ref.at[pl.ds(z * unit, unit)]))
                for fold in range(folds):
                    moves.append(
                        (
                            ffn_ref.at[z, pl.ds(unit, unit), pl.ds(fold * hidden_units, hidden_units)],
                            up_ref.at[pl.ds((z * folds + fold) * unit, unit)],
                        )
                    )
        return [pltpu.make_async_copy(*move, sems.at[i]) for i, move in enumerate(moves)]

    def kernel(x0, x1, d0, d1, *refs):
        weight_refs, (hidden0, hidden1, pre0, pre1, in0, in1, out0, out1, up_ref, down_ref, sems) = (
            refs[: len(weights)],
            refs[len(weights) :],
        )

        @pl.when(pl.program_id(0) == 0)
        def _():
            loads = copies(weight_refs, up_ref, down_ref, sems)
            for load in loads:
                load.start()
            for load in loads:
                load.wait()

        x = jnp.concatenate([x0[...], x1[...]])
        d_out = jnp.concatenate([d0[...], d1[...]])
        pre = jnp.dot(x, up_ref[...], preferred_element_type=WIDE)
        d_hidden = dot(d_out, down_ref[...], ((1,), (1,)))
        below, density = normal_parts(pre)
        hidden = (pre * below).astype(LOW)
        d_pre = (d_hidden * (below + pre * density)).astype(LOW)
        d_input = dot(d_pre, up_ref[...], ((1,), (1,)))
        out = jnp.dot(hidden, down_ref[...], preferred_element_type=WIDE)
        for side, (hidden_ref, pre_ref, in_ref, out_ref) in enumerate(
            ((hidden0, pre0, in0, out0), (hidden1, pre1, in1, out1))
        ):
            mine = slice(side * block, (side + 1) * block)
            hidden_ref[...] = hidden[mine]
            pre_ref[...] = d_pre[mine]
            in_ref[...] = d_input[mine].astype(in_ref.dtype)
            out_ref[...] = out[mine].astype(out_ref.dtype)

    wide = pl.BlockSpec((block, model_width), lambda i: (i, 0))
    narrow = pl.BlockSpec((block, hidden_units), lambda i: (i, 0))
    low = jax.ShapeDtypeStruct((rows, hidden_units), LOW)
    outs = pl.pallas_call(
        kernel,
        grid=(rows // block,),
        out_shape=(
            low,
            low,
            low,
            low,
            jax.ShapeDtypeStruct((rows, model_width), WIDE),
            jax.ShapeDtypeStruct((rows, model_width), LOW),
            jax.ShapeDtypeStruct((rows, model_width), WIDE),
            jax.ShapeDtypeStruct((rows, model_width), LOW),
        ),
        in_specs=[wide] * 4 + [pl.BlockSpec(memory_space=pl.ANY)] * len(weights),
        out_specs=(narrow,) * 4 + (wide,) * 4,
        scratch_shapes=[
            pltpu.VMEM((model_width, hidden_units), LOW),
            pltpu.VMEM((hidden_units, model_width), LOW),
            pltpu.SemaphoreType.DMA(((folds + 1) * deep,)),
        ],
        compiler_params=pltpu.CompilerParams(vmem_limit_bytes=32 * 2**20),
        cost_estimate=BRIEF,
    )(*xs, *d_outs, *weights)
    return outs[0:2], outs[2:4], outs[4:6], outs[6:8]


def ffn_outer(xs, d_outs, hidden, d_pre, deep, unit):
    model_width = xs[0].shape[1]
    hidden_units = deep * unit
    folds = model_width // hidden_units

    def kernel(x0, x1, d0, d1, h0, h1, p0, p1, out_ref):
        def both(left0, right0, left1, right1):
            total = dot(left0[...], right0[...], ((0,), (0,)))
            return (total + dot(left1[...], right1[...], ((0,), (0,)))).astype(LOW)

        down = both(h0, d0, h1, d1)
        for z in range(deep):
            out_ref[z, :unit] = down[z * unit : (z + 1) * unit]
        up = both(x0, p0, x1, p1)
        for z in range(deep):
            for fold in range(folds):
                rows = up[(z * folds + fold) * unit : (z * folds + fold + 1) * unit]
                out_ref[z, unit:, fold * hidden_units : (fold + 1) * hidden_units] = rows

    if not (whole_tiles(unit) and hidden_units % 128 == 0):
        pairs = ((hidden, d_outs), (xs, d_pre))
        down, up = (
            sum(outer(left, right) for left, right in zip(*pair_of, strict=True)).astype(LOW)
            for pair_of in pairs
        )
        down = down.reshape(deep, unit, model_width)
        return jnp.concatenate([down, fold_up(up.reshape(deep, -1, hidden_units), folds)], axis=1)
    whole = pl.BlockSpec(memory_space=pltpu.VMEM)
    return pl.pallas_call(
        kernel,
        out_shape=jax.ShapeDtypeStruct((deep, 2 * unit, model_width), LOW),
        in_specs=[whole] * 8,
        out_specs=whole,
        compiler_params=pltpu.CompilerParams(vmem_limit_bytes=56 * 2**20),
        cost_estimate=BRIEF,
    )(*xs, *d_outs, *hidden, *d_pre)


def attend_back(d_mixed, query, keyval, probs):
    slots, lat_rows, half_width = query.shape
    key_rows = keyval.shape[1]
    patches = key_rows - lat_rows
    chunk = PACK * HEAD
    groups = half_width // chunk
    scale = 1.0 / math.sqrt(HEAD)

    def kernel(d_ref, query_ref, keyval_ref, probs_ref, out_ref):
        mask_low, mask_wide = head_mask(lat_rows, LOW), head_mask(lat_rows, WIDE)
        out_ref[0, :patches, :half_width] = jnp.zeros((patches, half_width), LOW)
        for part in range(groups):
            columns = slice(part * chunk, (part + 1) * chunk)
            q = tile_heads(query_ref[0, :, columns], mask_low)
            d = tile_heads(d_ref[0, :, columns], mask_low)
            k = keyval_ref[0, :, columns]
            v = keyval_ref[0, :, half_width + part * chunk : half_width + (part + 1) * chunk]
            p = probs_ref[0, part]
            d_probs = dot(d, v, ((1,), (1,)))
            d_value = dot(p.astype(LOW), d, ((0,), (0,)))
            delta = jnp.sum(p * d_probs, axis=1, keepdims=True)
            d_scores = (p * (d_probs - delta)).astype(LOW)
            d_query = untile_heads(jnp.dot(d_scores, k, preferred_element_type=WIDE), mask_wide)
            d_key = dot(d_scores, q, ((0,), (0,)))
            out_ref[0, patches:, columns] = (d_query * scale).astype(LOW)
            out_ref[0, :, half_width + part * chunk : half_width + (part + 1) * chunk] = (
                d_key * scale
            ).astype(LOW)
            out_ref[0, :, 2 * half_width + part * chunk : 2 * half_width + (part + 1) * chunk] = (
                d_value.astype(LOW)
            )

    def slotted(*block):
        return pl.BlockSpec((1, *block), lambda i: (i,) + (0,) * len(block))

    return pl.pallas_call(
        kernel,
        grid=(slots,),
        out_shape=jax.ShapeDtypeStruct((slots, key_rows, 3 * half_width), LOW),
        in_specs=[
            slotted(lat_rows, half_width),
            slotted(lat_rows, half_width),
            slotted(key_rows, 2 * half_width),
            slotted(groups, PACK * lat_rows, key_rows),
        ],
        out_specs=slotted(key_rows, 3 * half_width),
        compiler_params=pltpu.CompilerParams(vmem_limit_bytes=32 * 2**20),
        cost_estimate=BRIEF,
    )(d_mixed, query, keyval, probs)


def on_device(
    wires,
    media,
    latents,
    upstream,
    time_index,
    live_count,
    time_table,
    media_gain,
    media_bias,
    latent_gain,
    latent_bias,
    ff_gain,
    ff_bias,
    w_query,
    w_keyval,
    w_out,
    w_up,
    w_down,
):
    wires.place()
    deep, flat, count = wires.deep, wires.flat, wires.count
    images, patches, model_width = media.shape
    lat_rows = latents.shape[1]
    key_rows = patches + lat_rows
    table_rows, shard = time_table.shape
    group = model_width // (2 * deep)
    half_width = model_width // 2
    slots = 2 * images

    qkv_mine, qkv_other = deal_columns(wires.c, (w_query, w_keyval), group)
    qkv_arrived = wires.send(qkv_other, "core")
    raw = jnp.concatenate([after(media, qkv_other), latents], axis=1)
    far_raw = wires.send(raw, "core")
    qkv_block = pair(qkv_mine, qkv_arrived, wires.c, 0)

    unit = w_down.shape[0]
    hidden_units = deep * unit
    tall, wide = 2 * shard, 3 * half_width
    folds = model_width // hidden_units
    ring_block = jnp.concatenate(
        [qkv_block.reshape(tall, wide), jnp.pad(w_out, ((0, 0), (0, wide - model_width)))]
    )
    smalls = jnp.concatenate(
        [time_table]
        + [v[None] for v in (media_gain, media_bias, latent_gain, latent_bias, ff_gain, ff_bias)],
        axis=0,
    )
    smalls = jnp.broadcast_to(smalls[None], (count, *smalls.shape))
    made = {}

    made["smalls"] = lax.all_to_all(smalls, AXES, 0, 0, tiled=True)

    def swap_up(first):
        shares = split_units(after(w_up, made["smalls"], first[wires.bits[-1]]), 2 * flat, unit)
        up_block = wires.swap_blocks(shares, wires.planes).reshape(-1, hidden_units)
        block = jnp.concatenate([w_down, fold_up(up_block, folds)])
        made["ffn"] = jnp.broadcast_to(block[None], (deep, *block.shape))
        return (made["ffn"],)

    d_out_low = after(upstream, qkv_other) * (jnp.arange(images) < live_count[0]).astype(LOW)[:, None, None]
    rings, gathered, d_out_got, steps = gather_rows(
        wires,
        ring_block,
        lambda block: block[:tall].reshape(2, shard, wide),
        after(d_out_low, made["smalls"]),
        {2: swap_up},
        (far_raw,),
    )
    places, pieces = [], []
    for step, got in enumerate(gathered):
        for mask, part in got.items():
            pieces += part if isinstance(part, tuple) else [part]
            for core in range(2):
                places.append((wires.plane(step) * 2 + core) * flat + (wires.f ^ mask))
    out_column = [ring[tall:, :model_width] for ring in rings]
    for mask in wires.masks:
        if mask not in d_out_got:
            d_out_got[mask] = wires.send(d_out_low, mask, *steps[-1])


    ffn_blocks = wires.swap_blocks(after(made["ffn"], rings[-1]), wires.columns)

    smalls = after(made["smalls"], *steps[-2][-1:])
    smalls = smalls.transpose(1, 0, 2).reshape(-1, model_width).astype(WIDE)
    norm_params = smalls[table_rows : table_rows + 4]
    ff_params = smalls[table_rows + 4 :]
    live_mask = (jnp.arange(images) < live_count[0]).astype(WIDE)[:, None, None]
    one_hot = (time_index[:, None] == jnp.arange(table_rows)[None, :]).astype(WIDE)
    time_rows = jnp.dot(one_hot, smalls[:table_rows], precision=HIGHEST)
    both_rows = jnp.concatenate([time_rows, wires.send(time_rows, "core")])

    out_places, out_pieces = [], []
    for mask, part in spread_plane(wires, jnp.stack(out_column), *steps[-1]).items():
        out_pieces.append(part)
        for step in range(deep):
            out_places.append(wires.plane(step) * flat + (wires.f ^ mask))


    qkv_full, sources, query, keyval, probs, mixed = attend(
        places,
        pieces,
        raw,
        far_raw,
        both_rows,
        norm_params,
        patches,
        half_width,
    )
    out_full, branch = project_out(
        out_places, out_pieces, after(mixed, *d_out_got.values()), model_width
    )
    branch = branch[:images] + wires.send(branch[images:], "core")
    middle = latents.astype(WIDE) + branch

    ffn_normed, ffn_norm_back = jax.vjp(norm_rows, middle, ff_params[0], ff_params[1])
    d_out = upstream.astype(WIDE) * live_mask

    def swapped(blocks, *ahead):
        mine = jnp.stack(blocks)
        far = wires.send(mine, "core", *ahead)
        return mine.reshape(-1, model_width), far.reshape(-1, model_width)

    ffn_low = ffn_normed.astype(LOW)
    ffn_got = spread_plane(wires, ffn_low)
    d_out_got = {mask: after(part, ffn_low) for mask, part in d_out_got.items()}
    order = [0, *wires.masks]
    d_out_rows = swapped([d_out_got[mask] for mask in order])
    ffn_rows = swapped([ffn_got[mask] for mask in order])
    hidden, d_pre, d_inputs, results = ffn_rows_back(
        ffn_blocks, ffn_rows, d_out_rows, unit
    )
    block_shape = (images, lat_rows, model_width)

    def collect_core(parts, *ahead):
        arrived = wires.send(parts[1], "core", *ahead)
        rows = (parts[0] + arrived.astype(WIDE)).reshape(len(order), *block_shape)
        return dict(zip(order, rows, strict=True)), arrived

    d_sums, d_swapped = collect_core(d_inputs)
    ffn_partial = ffn_outer(
        ffn_rows, d_out_rows, hidden, (after(d_pre[0], d_swapped), d_pre[1]), deep, unit
    )
    ffn_terms = wires.swap_blocks(ffn_partial, wires.columns)
    d_ffn_input, _ = sum_plane(wires, d_sums.get)
    d_ffn_input = after(d_ffn_input, ffn_partial)
    d_middle_norm, ff_gain_grad, ff_bias_grad = ffn_norm_back(d_ffn_input)
    d_middle = d_out + d_middle_norm

    own_branch = d_middle.astype(LOW)
    d_branch = jnp.concatenate([own_branch, wires.send(own_branch, "core")], axis=0)
    out_partial = outer(mixed.reshape(-1, half_width), d_branch.reshape(-1, model_width))
    out_partial = out_partial.astype(LOW).reshape(deep, flat, shard, model_width)
    out_partial = jnp.stack([out_partial[..., :half_width], out_partial[..., half_width:]], axis=2)
    d_mixed = rows_back(after(d_branch, out_partial), out_full).astype(LOW)
    d_projected = attend_back(d_mixed, query, keyval, probs)

    source_rows = sources.reshape(-1, model_width)
    d_projected_rows = d_projected.reshape(-1, wide)
    plane_rows = 2 * flat * shard

    kept = {}

    def results_clock(*ahead):
        result_sums, arrived = collect_core(results, *ahead)
        kept["own"] = result_sums[0]
        kept["low"] = {mask: rows.astype(LOW) for mask, rows in result_sums.items()}
        return arrived

    def far_back(_):
        kept["far"] = rows_back(d_projected[images:], qkv_full).astype(LOW)
        return (kept["far"], *kept["low"].values())

    def far_clock(*ahead):
        kept["far"] = wires.send(kept["far"], "core", *ahead)
        return kept["far"]

    def norms_back(arrived):
        media_grad, latent_grad, sums = sources_back(
            after(d_projected[:images], arrived),
            qkv_full,
            kept["far"],
            raw,
            time_rows,
            norm_params,
            d_middle,
        )
        table_part = jnp.dot(one_hot.T, sums[:, 0], precision=HIGHEST)
        small_grads = [table_part, jnp.sum(sums[:, 1:5], axis=0), ff_gain_grad[None], ff_bias_grad[None]]
        small_grads = jnp.concatenate(small_grads).reshape(-1, count, shard).transpose(1, 0, 2)
        kept["media"], kept["latent"], kept["small"] = media_grad, latent_grad, small_grads
        return media_grad, small_grads

    def last_pull(_):
        ffn_sum = jnp.sum(ffn_terms.astype(WIDE), axis=0)
        kept["down"] = ffn_sum[:unit]
        up_sum = unfold_up(ffn_sum[unit:].astype(LOW), folds)
        kept["up"] = up_sum.reshape(2 * flat, shard, hidden_units)
        return (kept["up"],)

    result_got = []

    def send_result(mask):
        def ride(ahead):
            result_got.append(wires.send(kept["low"][mask], mask, *ahead))
            return result_got[-1]

        return ride

    turning = [mask for mask in wires.masks if mask & (mask - 1)]
    riders = {
        deep + 1: [send_result(mask) for mask in (*wires.bits, *turning)],
    }

    def partial_rows(step, d_rows):
        at_plane = wires.plane(1 + step)
        rows = lax.dynamic_slice_in_dim(source_rows, at_plane * plane_rows, plane_rows, 1)
        block = outer(rows, d_rows).astype(LOW).reshape(2, flat, shard, wide)
        return block, at(out_partial, at_plane, 0)

    partials = [partial_rows(step, d_projected_rows) for step in range(deep)]

    def part(step, mask):
        block, out_block = partials[step]
        target = wires.f ^ mask
        return jnp.concatenate([at(block, target, 1), at(out_block, target, 0)], axis=-1)

    total = scatter_rows(
        wires,
        part,
        {
            1: far_back,
            3: norms_back,
            4: last_pull,
        },
        riders,
        {0: results_clock, 2: far_clock},
    )
    qkv_sum = total[..., :wide]
    w_out_grad = jnp.concatenate([total[0, :, wide:], total[1, :, wide:]], axis=-1)
    media_grad, latent_grad = kept["media"], kept["latent"]
    w_down_grad = kept["down"]
    up_sum = wires.swap_blocks(kept["up"], wires.planes)
    w_up_grad = merge_units(after(up_sum, result_got[0]), unit)
    small_grads = lax.all_to_all(after(kept["small"], up_sum, result_got[0]), AXES, 0, 0, tiled=True)
    small_grads = jnp.sum(small_grads, axis=0)
    own_result = sum([rows.astype(WIDE) for rows in result_got], kept["own"])
    latents_out = ((middle + own_result) * live_mask).astype(LOW)
    qkv_own = pick(qkv_sum, wires.c, 0)
    qkv_far = wires.send(pick(qkv_sum, 1 - wires.c, 0), "core", small_grads)
    w_query_grad, w_keyval_grad = join_columns(
        wires.c, qkv_own, qkv_far, (model_width, 2 * model_width), group
    )
    return (
        latents_out,
        media_grad,
        latent_grad,
        small_grads[:table_rows],
        *[small_grads[table_rows + k] for k in range(6)],
        w_query_grad,
        w_keyval_grad,
        w_out_grad,
        w_up_grad,
        w_down_grad,
    )


def solution(mesh):
    lead = P(AXES)
    table = P(None, AXES)
    return jax.shard_map(
        functools.partial(on_device, Wires(mesh)),
        mesh=mesh,
        in_specs=(lead,) * 5 + (table,) + (lead,) * 11,
        out_specs=(lead,) * 3 + (table,) + (lead,) * 11,
        check_vma=False,
    )
```

```python
import functools
import math

import jax
import jax.numpy as jnp
from jax import lax
from jax.experimental import pallas as pl
from jax.experimental.pallas import tpu as pltpu
from jax.sharding import PartitionSpec as P

HEAD = 96
PACK = 4
AXES = ("dp", "fsdp")
LOW = jnp.bfloat16
WIDE = jnp.float32
HIGHEST = lax.Precision.HIGHEST
NORM_EPS = 1e-05
BRIEF = pl.CostEstimate(flops=1, bytes_accessed=1, transcendentals=0)


def norm_rows(inputs, gain, shift):
    row_mean = jnp.mean(inputs, axis=-1, keepdims=True)
    centered = inputs - row_mean
    variance = jnp.mean(centered * centered, axis=-1, keepdims=True)
    return centered * lax.rsqrt(variance + NORM_EPS) * gain + shift


def exact_gelu(inputs):
    return jax.nn.gelu(inputs, approximate=False)


def dot(left, right, contract):
    return lax.dot_general(left, right, (contract, ((), ())), preferred_element_type=WIDE)


def rows_by(left, right):
    return dot(left, right, ((left.ndim - 1,), (0,)))


def rows_back(left, right):
    return dot(left, right, ((left.ndim - 1,), (1,)))


def outer(left, right):
    return dot(left, right, ((0,), (0,)))


class Wires:
    def __init__(self, mesh):
        self.deep = mesh.shape["dp"] // 2
        self.flat = mesh.shape["fsdp"]
        self.count = 2 * self.deep * self.flat
        places = [
            (z, c, f) for z in range(self.deep) for c in range(2) for f in range(self.flat)
        ]

        def number(z, c, f):
            return (z * 2 + c) * self.flat + f

        def moves(target):
            return [(number(*place), number(*target(*place))) for place in places]

        self.bits = [1 << k for k in range(self.flat.bit_length() - 1)]
        self.masks = list(range(1, self.flat))
        self.moves = {
            "core": moves(lambda z, c, f: (z, 1 - c, f)),
        }
        self.moves["rise"] = moves(lambda z, c, f: ((z + 1) % self.deep, c, f))
        self.columns = [
            [number(z, c, f) for z in range(self.deep)] for c in range(2) for f in range(self.flat)
        ]
        self.planes = [
            [number(z, c, f) for c in range(2) for f in range(self.flat)] for z in range(self.deep)
        ]
        for mask in self.masks:
            self.moves[mask] = moves(lambda z, c, f, mask=mask: (z, c, f ^ mask))

    def place(self):
        outer_at = lax.axis_index("dp")
        self.z, self.c = outer_at // 2, outer_at % 2
        self.f = lax.axis_index("fsdp")
        self.queues = {}

    def send(self, block, kind, *ahead):
        if ahead:
            block = after(block, *ahead)
        return lax.ppermute(block, AXES, self.moves[kind])

    def swap_blocks(self, blocks, groups):
        return lax.all_to_all(blocks, AXES, 0, 0, tiled=True, axis_index_groups=groups)

    def plane(self, step):
        return lax.rem(self.z + 2 * self.deep - step, self.deep)


def after(block, *others):
    return lax.optimization_barrier((block, *others))[0]


def at(array, index, axis):
    return lax.dynamic_index_in_dim(array, index, axis, keepdims=False)


def pair(mine, other, side, axis):
    return jnp.where(
        side == 0, jnp.stack([mine, other], axis=axis), jnp.stack([other, mine], axis=axis)
    )


def pick(array, side, axis):
    return jnp.where(
        side == 0,
        lax.index_in_dim(array, 0, axis, keepdims=False),
        lax.index_in_dim(array, 1, axis, keepdims=False),
    )


def corner(mask):
    return mask & -mask, 1 << (mask.bit_length() - 1)


def gather_rows(wires, block, take, guest, hooks, before):
    rings, gathered, guests = [block], [], {0: guest}
    single = [mask for mask in wires.masks if not mask & (mask - 1)]
    multiple = sorted((m for m in wires.masks if m & (m - 1)), key=lambda m: bin(m).count("1"))
    steps = []
    for step in range(wires.deep + 1):
        now = []
        before = (*before, *(hooks[step](gathered[0]) if step in hooks else ()))
        if step < wires.deep:
            if step + 1 < wires.deep:
                rings.append(wires.send(rings[step], "rise", *before))
                now.append(rings[-1])
            mine = take(rings[step])
            got = {0: mine}
            for mask in single:
                got[mask] = wires.send(mine, mask, *before)
                now.append(got[mask])
            gathered.append(got)
        if step == 0:
            for mask in single:
                guests[mask] = wires.send(guest, mask, *before)
                now.append(guests[mask])
        if step:
            got = gathered[step - 1]
            for mask in multiple:
                low, high = corner(mask)
                got[mask] = (
                    wires.send(got[mask ^ high][0], high, *before),
                    wires.send(got[mask ^ low][1], low, *before),
                )
                now += got[mask]
        before = now
        steps.append(now)
    return rings, gathered, guests, steps


def scatter_rows(wires, part, pulls, riders, clocks):
    single = [mask for mask in wires.masks if not mask & (mask - 1)]
    multiple = sorted((m for m in wires.masks if m & (m - 1)), key=lambda m: -bin(m).count("1"))
    extra = [{} for _ in range(wires.deep)]
    before, total, clock = (), None, None
    for step in range(wires.deep + 3):
        now, ready = [], []
        ahead = (*(before if step else ()), *(pulls[step](clock) if step in pulls else ()))

        def term(block, mask, half=None):
            mine = part(block, mask)
            if half is not None:
                mine = mine[half]
            more = extra[block].get((mask, half), [])
            return sum([m.astype(WIDE) for m in more], mine).astype(LOW)

        block = step - 3
        if 0 <= block:
            total = (
                sum([m.astype(WIDE) for m in extra[block][0, None]], part(block, 0).astype(WIDE))
                + (0.0 if total is None else total)
            )
            if block == wires.deep - 1:
                return total
            arrived = wires.send(total.astype(LOW), "rise", *ahead)
            now.append(arrived)
            total = arrived.astype(WIDE)
        block = step - 1
        if 0 <= block < wires.deep:
            for mask in single:
                leaving = jnp.stack([term(block, mask, half) for half in range(2)])
                ready.append(leaving)
                arrived = wires.send(leaving, mask, *ahead)
                extra[block].setdefault((0, None), []).append(arrived)
                now.append(arrived)
        if step < wires.deep:
            for mask in multiple:
                low, high = corner(mask)
                for half, bit in ((0, high), (1, low)):
                    leaving = term(step, mask, half)
                    ready.append(leaving)
                    arrived = wires.send(leaving, bit, *ahead)
                    extra[step].setdefault((mask ^ bit, half), []).append(arrived)
                    now.append(arrived)
        clock = clocks[step](*ahead, *ready) if step in clocks else now[-1]
        for rider in riders.get(step, ()):
            now.append(rider(ahead))
        before = now


def spread_plane(wires, block, *ahead):
    got = {0: block}
    for mask in reversed(wires.masks):
        got[mask] = wires.send(block, mask, *ahead)
    return got


def sum_plane(wires, part, *ahead):
    arrived = [wires.send(part(mask).astype(LOW), mask, *ahead) for mask in reversed(wires.masks)]
    return sum([block.astype(WIDE) for block in arrived], part(0).astype(WIDE)), arrived


def lay(places, pieces, count):
    entry = pieces[0].shape[1:]
    views = [(k, i) for k, piece in enumerate(pieces) for i in range(piece.shape[0])]
    number = len(views)

    def kernel(places_ref, *refs):
        out_ref, held, sems = refs[-3:]
        loads = [
            pltpu.make_async_copy(refs[k].at[i], held.at[n], sems.at[0, n])
            for n, (k, i) in enumerate(views)
        ]
        stores = [
            pltpu.make_async_copy(held.at[n], out_ref.at[places_ref[n]], sems.at[1, n])
            for n in range(number)
        ]
        for load in loads:
            load.start()
        for load, store in zip(loads, stores, strict=True):
            load.wait()
            store.start()
        for store in stores:
            store.wait()

    anywhere = pl.BlockSpec(memory_space=pl.ANY)
    return pl.pallas_call(
        kernel,
        out_shape=jax.ShapeDtypeStruct((count,) + entry, pieces[0].dtype),
        in_specs=[pl.BlockSpec(memory_space=pltpu.SMEM)] + [anywhere] * len(pieces),
        out_specs=anywhere,
        scratch_shapes=[
            pltpu.VMEM((number,) + entry, pieces[0].dtype),
            pltpu.SemaphoreType.DMA((2, number)),
        ],
        compiler_params=pltpu.CompilerParams(vmem_limit_bytes=58 * 2**20),
    )(jnp.stack(places).astype(jnp.int32), *pieces)


def whole_tiles(rows):
    return rows % 16 == 0


def joined(places, pieces):
    shard = pieces[0].shape[-2]
    if whole_tiles(shard):
        return places, pieces
    rows = [row for piece in pieces for row in (piece if piece.ndim == 3 else (piece,))]
    full = jnp.zeros((len(rows), *rows[0].shape), rows[0].dtype)
    for place, row in zip(places, rows, strict=True):
        full = lax.dynamic_update_index_in_dim(full, row, place, 0)
    return [jnp.zeros((), jnp.int32)], [full.reshape(1, len(rows) * shard, -1)]


def on_chip(kernel, out_shape, side, *operands):
    whole = pl.BlockSpec(memory_space=pltpu.VMEM)
    return pl.pallas_call(
        kernel,
        out_shape=out_shape,
        in_specs=[pl.BlockSpec(memory_space=pltpu.SMEM)] + [whole] * len(operands),
        out_specs=jax.tree.map(lambda _: whole, out_shape),
    )(side.reshape(1).astype(jnp.int32), *operands)


def deal_columns(side, arrays, group):
    shard = arrays[0].shape[0]
    width = sum(array.shape[1] for array in arrays) // 2
    if not whole_tiles(shard):
        both = jnp.concatenate(arrays, axis=1).reshape(shard, -1, 2, group)
        return tuple(pick(both, s, 2).reshape(shard, width) for s in (side, 1 - side))

    def kernel(side_ref, *refs):
        *in_refs, own_ref, other_ref = refs
        first = side_ref[0] == 0
        base = 0
        for ref in in_refs:
            block = ref[...]
            count = block.shape[1] // (2 * group)
            hands = [
                jnp.concatenate(
                    [block[:, (2 * j + s) * group : (2 * j + s + 1) * group] for j in range(count)],
                    axis=1,
                )
                for s in range(2)
            ]
            own_ref[:, base : base + count * group] = jnp.where(first, hands[0], hands[1])
            other_ref[:, base : base + count * group] = jnp.where(first, hands[1], hands[0])
            base += count * group

    shape = jax.ShapeDtypeStruct((shard, width), arrays[0].dtype)
    return on_chip(kernel, (shape, shape), side, *arrays)


def join_columns(side, own, other, widths, group):
    shard = own.shape[0]
    if not whole_tiles(shard):
        halves = [part.reshape(shard, -1, group) for part in (own, other)]
        both = pair(halves[0], halves[1], side, 2).reshape(shard, -1)
        return tuple(jnp.split(both, [widths[0]], axis=1))

    def kernel(side_ref, own_ref, other_ref, *out_refs):
        first = side_ref[0] == 0
        hands = (
            jnp.where(first, own_ref[...], other_ref[...]),
            jnp.where(first, other_ref[...], own_ref[...]),
        )
        base = 0
        for ref in out_refs:
            parts = []
            for j in range(ref.shape[1] // (2 * group)):
                columns = slice(base + j * group, base + (j + 1) * group)
                parts += [hand[:, columns] for hand in hands]
            ref[...] = jnp.concatenate(parts, axis=1)
            base += ref.shape[1] // 2

    shapes = tuple(jax.ShapeDtypeStruct((own.shape[0], width), own.dtype) for width in widths)
    return on_chip(kernel, shapes, side, own, other)


def split_units(array, ways, unit):
    shard, width = array.shape
    deep = width // (ways * unit)
    if not whole_tiles(shard):
        blocks = array.reshape(shard, deep, ways, unit).transpose(2, 0, 1, 3)
        return blocks.reshape(ways, shard, deep * unit)

    def kernel(_, in_ref, out_ref):
        block = in_ref[...]
        for way in range(ways):
            parts = [
                block[:, (z * ways + way) * unit : (z * ways + way + 1) * unit] for z in range(deep)
            ]
            out_ref[way] = jnp.concatenate(parts, axis=1)

    shape = jax.ShapeDtypeStruct((ways, shard, deep * unit), array.dtype)
    return on_chip(kernel, shape, jnp.zeros((), jnp.int32), array)


def merge_units(blocks, unit):
    ways, shard, part = blocks.shape
    deep = part // unit
    if not whole_tiles(shard):
        blocks = blocks.reshape(ways, shard, deep, unit).transpose(1, 2, 0, 3)
        return blocks.reshape(shard, -1).astype(WIDE)

    def kernel(_, in_ref, out_ref):
        parts = []
        for z in range(deep):
            for way in range(ways):
                parts.append(in_ref[way][:, z * unit : (z + 1) * unit].astype(WIDE))
        out_ref[...] = jnp.concatenate(parts, axis=1)

    shape = jax.ShapeDtypeStruct((shard, deep * ways * unit), WIDE)
    return on_chip(kernel, shape, jnp.zeros((), jnp.int32), blocks)


def tile_heads(rows, mask):
    return jnp.concatenate([rows] * PACK, axis=0) * mask


def untile_heads(rows, mask):
    kept = rows * mask
    size = rows.shape[0] // PACK
    return sum(kept[k * size : (k + 1) * size] for k in range(PACK))


def head_mask(rows, dtype):
    row = lax.broadcasted_iota(jnp.int32, (PACK * rows, PACK * HEAD), 0) // rows
    column = lax.broadcasted_iota(jnp.int32, (PACK * rows, PACK * HEAD), 1) // HEAD
    return (row == column).astype(WIDE).astype(dtype)


def normed(rows, gain, shift):
    centered = rows - jnp.mean(rows, axis=-1, keepdims=True)
    inverse = lax.rsqrt(jnp.mean(centered * centered, axis=-1, keepdims=True) + NORM_EPS)
    unit = centered * inverse
    return unit * gain + shift, unit, inverse


def attend(places, pieces, own, far, time_rows, norm_rows_of, patches, half_width):
    images, key_rows, model_width = own.shape
    lat_rows = key_rows - patches
    slots = 2 * images
    width = 3 * half_width
    places, pieces = joined(places, pieces)
    chunk = PACK * HEAD
    groups = half_width // chunk
    scale = 1.0 / math.sqrt(HEAD)
    shard = pieces[0].shape[-2]
    views = []
    for k, piece in enumerate(pieces):
        views += [(k, None)] if piece.ndim == 2 else [(k, core) for core in range(piece.shape[0])]

    def kernel(places_ref, *refs):
        piece_refs = refs[: len(pieces)]
        (
            own_ref,
            far_ref,
            time_ref,
            params_ref,
            full_ref,
            sources_ref,
            query_ref,
            keyval_ref,
            probs_ref,
            mixed_ref,
            w_ref,
            sems,
        ) = refs[len(pieces) :]
        slot = pl.program_id(0)
        loads = []
        for i, (k, core) in enumerate(views):
            source = piece_refs[k] if core is None else piece_refs[k].at[core]
            start = pl.multiple_of(places_ref[i] * shard, shard)
            loads.append(pltpu.make_async_copy(source, w_ref.at[pl.ds(start, shard)], sems.at[i]))

        @pl.when(slot == 0)
        def _():
            for load in loads:
                load.start()

        def save():
            return pltpu.make_async_copy(w_ref, full_ref, sems.at[len(views)])

        raw = jnp.where(slot < images, own_ref[0], far_ref[0]).astype(WIDE)
        media = raw[:patches] + time_ref[0]
        sources_ref[0, :patches] = normed(media, params_ref[0:1], params_ref[1:2])[0].astype(LOW)
        lat = normed(raw[patches:], params_ref[2:3], params_ref[3:4])[0]
        sources_ref[0, patches:] = lat.astype(LOW)

        @pl.when(slot == 0)
        def _():
            for load in loads:
                load.wait()
            save().start()

        x = sources_ref[0]
        mask_low, mask_wide = head_mask(lat_rows, LOW), head_mask(lat_rows, WIDE)

        def project(rows, part):
            w = w_ref[:, part * chunk : (part + 1) * chunk]
            return jnp.dot(rows, w, preferred_element_type=WIDE).astype(LOW)

        for part in range(groups):
            columns = slice(part * chunk, (part + 1) * chunk)
            query = project(x[patches:], part)
            query_ref[0, :, columns] = query
            k = project(x, groups + part)
            keyval_ref[0, :, columns] = k
            v = project(x, 2 * groups + part)
            keyval_ref[0, :, half_width + part * chunk : half_width + (part + 1) * chunk] = v
            s = dot(tile_heads(query, mask_low), k, ((1,), (1,)))
            e = jnp.exp((s - jnp.max(s, axis=1, keepdims=True)) * scale)
            p = e * (1.0 / jnp.sum(e, axis=1, keepdims=True))
            probs_ref[0, part] = p
            m = jnp.dot(p.astype(LOW), v, preferred_element_type=WIDE)
            mixed_ref[0, :, columns] = untile_heads(m, mask_wide).astype(LOW)

        @pl.when(slot == slots - 1)
        def _():
            save().wait()

    anywhere = pl.BlockSpec(memory_space=pl.ANY)
    whole = pl.BlockSpec(memory_space=pltpu.VMEM)

    def slotted(*block):
        return pl.BlockSpec((1, *block), lambda i: (i,) + (0,) * len(block))

    def halved(first, *block):
        if first:
            return pl.BlockSpec((1, *block), lambda i: (jnp.minimum(i, images - 1), 0, 0))
        return pl.BlockSpec((1, *block), lambda i: (jnp.maximum(i - images, 0), 0, 0))

    return pl.pallas_call(
        kernel,
        grid=(slots,),
        out_shape=(
            jax.ShapeDtypeStruct((model_width, width), LOW),
            jax.ShapeDtypeStruct((slots, key_rows, model_width), LOW),
            jax.ShapeDtypeStruct((slots, lat_rows, half_width), LOW),
            jax.ShapeDtypeStruct((slots, key_rows, 2 * half_width), LOW),
            jax.ShapeDtypeStruct((slots, groups, PACK * lat_rows, key_rows), WIDE),
            jax.ShapeDtypeStruct((slots, lat_rows, half_width), LOW),
        ),
        in_specs=[pl.BlockSpec(memory_space=pltpu.SMEM)]
        + [anywhere] * len(pieces)
        + [
            halved(True, key_rows, model_width),
            halved(False, key_rows, model_width),
            slotted(1, model_width),
            whole,
        ],
        out_specs=(
            anywhere,
            slotted(key_rows, model_width),
            slotted(lat_rows, half_width),
            slotted(key_rows, 2 * half_width),
            slotted(groups, PACK * lat_rows, key_rows),
            slotted(lat_rows, half_width),
        ),
        scratch_shapes=[
            pltpu.VMEM((model_width, width), LOW),
            pltpu.SemaphoreType.DMA((len(views) + 1,)),
        ],
        compiler_params=pltpu.CompilerParams(vmem_limit_bytes=58 * 2**20),
        cost_estimate=BRIEF,
    )(jnp.stack(places).astype(jnp.int32), *pieces, own, far, time_rows[:, None], norm_rows_of)


def sources_back(d_projected, projections, far_part, own, time_rows, norm_rows_of, d_middle):
    images, key_rows, model_width = own.shape
    lat_rows = d_middle.shape[1]
    patches = key_rows - lat_rows
    width = d_projected.shape[-1]

    def kernel(d_ref, w_ref, far_ref, raw_ref, time_ref, params_ref, mid_ref, m_out, l_out, s_out):
        d = dot(d_ref[0], w_ref[...], ((1,), (1,))) + far_ref[0].astype(WIDE)

        def back(rows, d_rows, gain, shift):
            _, unit, inverse = normed(rows, gain, shift)
            scaled = d_rows * gain
            along = jnp.mean(scaled * unit, axis=-1, keepdims=True)
            inner = scaled - jnp.mean(scaled, axis=-1, keepdims=True) - unit * along
            sums = (
                jnp.sum(d_rows * unit, axis=0, keepdims=True),
                jnp.sum(d_rows, axis=0, keepdims=True),
            )
            return inverse * inner, sums

        rows = raw_ref[0, :patches].astype(WIDE) + time_ref[0]
        d_media, media_sums = back(rows, d[:patches], params_ref[0:1], params_ref[1:2])
        m_out[0] = d_media
        rows = raw_ref[0, patches:].astype(WIDE)
        d_lat, lat_sums = back(rows, d[patches:], params_ref[2:3], params_ref[3:4])
        l_out[0] = mid_ref[0] + d_lat
        total = jnp.sum(d_media, axis=0, keepdims=True)
        s_out[0] = jnp.concatenate(
            [total, *media_sums, *lat_sums, jnp.zeros((3, model_width), WIDE)], axis=0
        )

    whole = pl.BlockSpec(memory_space=pltpu.VMEM)

    def slotted(*block):
        return pl.BlockSpec((1, *block), lambda i: (i,) + (0,) * len(block))

    return pl.pallas_call(
        kernel,
        grid=(images,),
        out_shape=(
            jax.ShapeDtypeStruct((images, patches, model_width), WIDE),
            jax.ShapeDtypeStruct((images, lat_rows, model_width), WIDE),
            jax.ShapeDtypeStruct((images, 8, model_width), WIDE),
        ),
        in_specs=[
            slotted(key_rows, width),
            whole,
            slotted(key_rows, model_width),
            slotted(key_rows, model_width),
            slotted(1, model_width),
            whole,
            slotted(lat_rows, model_width),
        ],
        out_specs=(
            slotted(patches, model_width),
            slotted(lat_rows, model_width),
            slotted(8, model_width),
        ),
        compiler_params=pltpu.CompilerParams(vmem_limit_bytes=48 * 2**20),
        cost_estimate=BRIEF,
    )(d_projected, projections, far_part, own, time_rows[:, None], norm_rows_of, d_middle)


def project_out(places, pieces, mixed, model_width):
    slots, lat_rows, half_width = mixed.shape
    places, pieces = joined(places, pieces)
    shard = pieces[0].shape[-2]
    views = [(k, i) for k, piece in enumerate(pieces) for i in range(piece.shape[0])]
    chunk = PACK * HEAD

    def kernel(places_ref, *refs):
        piece_refs = refs[: len(pieces)]
        mixed_ref, full_ref, branch_ref, w_ref, sems = refs[len(pieces) :]
        loads = []
        for i, (k, entry) in enumerate(views):
            start = pl.multiple_of(places_ref[i] * shard, shard)
            loads.append(
                pltpu.make_async_copy(
                    piece_refs[k].at[entry], w_ref.at[pl.ds(start, shard)], sems.at[i]
                )
            )
        for load in loads:
            load.start()
        for load in loads:
            load.wait()
        save = pltpu.make_async_copy(w_ref, full_ref, sems.at[len(views)])
        save.start()
        rows = mixed_ref[...].reshape(slots * lat_rows, half_width)
        for part in range(model_width // chunk):
            columns = slice(part * chunk, (part + 1) * chunk)
            branch_ref[:, columns] = jnp.dot(
                rows, w_ref[:, columns], preferred_element_type=WIDE
            )
        save.wait()

    anywhere = pl.BlockSpec(memory_space=pl.ANY)
    whole = pl.BlockSpec(memory_space=pltpu.VMEM)
    full, branch = pl.pallas_call(
        kernel,
        out_shape=(
            jax.ShapeDtypeStruct((half_width, model_width), LOW),
            jax.ShapeDtypeStruct((slots * lat_rows, model_width), WIDE),
        ),
        in_specs=[pl.BlockSpec(memory_space=pltpu.SMEM)] + [anywhere] * len(pieces) + [whole],
        out_specs=(anywhere, whole),
        scratch_shapes=[
            pltpu.VMEM((half_width, model_width), LOW),
            pltpu.SemaphoreType.DMA((len(views) + 1,)),
        ],
        compiler_params=pltpu.CompilerParams(vmem_limit_bytes=16 * 2**20),
        cost_estimate=BRIEF,
    )(jnp.stack(places).astype(jnp.int32), *pieces, mixed)
    return full, branch.reshape(slots, lat_rows, model_width)


def normal_parts(x):
    density = jnp.exp(-0.5 * x * x)
    t = 1.0 / (1.0 + (0.3275911 * math.sqrt(0.5)) * jnp.abs(x))
    series = t * (
        0.254829592
        + t * (-0.284496736 + t * (1.421413741 + t * (-1.453152027 + t * 1.061405429)))
    )
    upper = 0.5 * series * density
    return jnp.where(x < 0, upper, 1.0 - upper), density * (1.0 / math.sqrt(2 * math.pi))


def fold_up(block, folds):
    return jnp.concatenate(jnp.split(block, folds, axis=-2), axis=-1)


def unfold_up(block, folds):
    return jnp.concatenate(jnp.split(block, folds, axis=-1), axis=-2)


def ffn_rows_back(ffn_blocks, xs, d_outs, unit):
    deep = ffn_blocks.shape[0]
    hidden_units = deep * unit
    rows, model_width = xs[0].shape
    folds = model_width // hidden_units
    block = 128
    direct = whole_tiles(unit) and hidden_units % 128 == 0
    if direct:
        weights = (ffn_blocks,)
    else:
        weights = (
            unfold_up(ffn_blocks[:, unit:], folds).reshape(model_width, hidden_units),
            ffn_blocks[:, :unit].reshape(hidden_units, model_width),
        )

    def copies(weight_refs, up_ref, down_ref, sems):
        if not direct:
            moves = list(zip(weight_refs, (up_ref, down_ref), strict=True))
        else:
            (ffn_ref,) = weight_refs
            moves = []
            for z in range(deep):
                moves.append((ffn_ref.at[z, pl.ds(0, unit)], down_ref.at[pl.ds(z * unit, unit)]))
                for fold in range(folds):
                    moves.append(
                        (
                            ffn_ref.at[z, pl.ds(unit, unit), pl.ds(fold * hidden_units, hidden_units)],
                            up_ref.at[pl.ds((z * folds + fold) * unit, unit)],
                        )
                    )
        return [pltpu.make_async_copy(*move, sems.at[i]) for i, move in enumerate(moves)]

    def kernel(x0, x1, d0, d1, *refs):
        weight_refs, (hidden0, hidden1, pre0, pre1, in0, in1, out0, out1, up_ref, down_ref, sems) = (
            refs[: len(weights)],
            refs[len(weights) :],
        )

        @pl.when(pl.program_id(0) == 0)
        def _():
            loads = copies(weight_refs, up_ref, down_ref, sems)
            for load in loads:
                load.start()
            for load in loads:
                load.wait()

        x = jnp.concatenate([x0[...], x1[...]])
        d_out = jnp.concatenate([d0[...], d1[...]])
        pre = jnp.dot(x, up_ref[...], preferred_element_type=WIDE)
        d_hidden = dot(d_out, down_ref[...], ((1,), (1,)))
        below, density = normal_parts(pre)
        hidden = (pre * below).astype(LOW)
        d_pre = (d_hidden * (below + pre * density)).astype(LOW)
        d_input = dot(d_pre, up_ref[...], ((1,), (1,)))
        out = jnp.dot(hidden, down_ref[...], preferred_element_type=WIDE)
        for side, (hidden_ref, pre_ref, in_ref, out_ref) in enumerate(
            ((hidden0, pre0, in0, out0), (hidden1, pre1, in1, out1))
        ):
            mine = slice(side * block, (side + 1) * block)
            hidden_ref[...] = hidden[mine]
            pre_ref[...] = d_pre[mine]
            in_ref[...] = d_input[mine].astype(in_ref.dtype)
            out_ref[...] = out[mine].astype(out_ref.dtype)

    wide = pl.BlockSpec((block, model_width), lambda i: (i, 0))
    narrow = pl.BlockSpec((block, hidden_units), lambda i: (i, 0))
    low = jax.ShapeDtypeStruct((rows, hidden_units), LOW)
    outs = pl.pallas_call(
        kernel,
        grid=(rows // block,),
        out_shape=(
            low,
            low,
            low,
            low,
            jax.ShapeDtypeStruct((rows, model_width), WIDE),
            jax.ShapeDtypeStruct((rows, model_width), LOW),
            jax.ShapeDtypeStruct((rows, model_width), WIDE),
            jax.ShapeDtypeStruct((rows, model_width), LOW),
        ),
        in_specs=[wide] * 4 + [pl.BlockSpec(memory_space=pl.ANY)] * len(weights),
        out_specs=(narrow,) * 4 + (wide,) * 4,
        scratch_shapes=[
            pltpu.VMEM((model_width, hidden_units), LOW),
            pltpu.VMEM((hidden_units, model_width), LOW),
            pltpu.SemaphoreType.DMA(((folds + 1) * deep,)),
        ],
        compiler_params=pltpu.CompilerParams(vmem_limit_bytes=32 * 2**20),
        cost_estimate=BRIEF,
    )(*xs, *d_outs, *weights)
    return outs[0:2], outs[2:4], outs[4:6], outs[6:8]


def ffn_outer(xs, d_outs, hidden, d_pre, deep, unit):
    model_width = xs[0].shape[1]
    hidden_units = deep * unit
    folds = model_width // hidden_units

    def kernel(x0, x1, d0, d1, h0, h1, p0, p1, out_ref):
        def both(left0, right0, left1, right1):
            total = dot(left0[...], right0[...], ((0,), (0,)))
            return (total + dot(left1[...], right1[...], ((0,), (0,)))).astype(LOW)

        down = both(h0, d0, h1, d1)
        for z in range(deep):
            out_ref[z, :unit] = down[z * unit : (z + 1) * unit]
        up = both(x0, p0, x1, p1)
        for z in range(deep):
            for fold in range(folds):
                rows = up[(z * folds + fold) * unit : (z * folds + fold + 1) * unit]
                out_ref[z, unit:, fold * hidden_units : (fold + 1) * hidden_units] = rows

    if not (whole_tiles(unit) and hidden_units % 128 == 0):
        pairs = ((hidden, d_outs), (xs, d_pre))
        down, up = (
            sum(outer(left, right) for left, right in zip(*pair_of, strict=True)).astype(LOW)
            for pair_of in pairs
        )
        down = down.reshape(deep, unit, model_width)
        return jnp.concatenate([down, fold_up(up.reshape(deep, -1, hidden_units), folds)], axis=1)
    whole = pl.BlockSpec(memory_space=pltpu.VMEM)
    return pl.pallas_call(
        kernel,
        out_shape=jax.ShapeDtypeStruct((deep, 2 * unit, model_width), LOW),
        in_specs=[whole] * 8,
        out_specs=whole,
        compiler_params=pltpu.CompilerParams(vmem_limit_bytes=56 * 2**20),
        cost_estimate=BRIEF,
    )(*xs, *d_outs, *hidden, *d_pre)


def attend_back(d_mixed, query, keyval, probs):
    slots, lat_rows, half_width = query.shape
    key_rows = keyval.shape[1]
    patches = key_rows - lat_rows
    chunk = PACK * HEAD
    groups = half_width // chunk
    scale = 1.0 / math.sqrt(HEAD)

    def kernel(d_ref, query_ref, keyval_ref, probs_ref, out_ref):
        mask_low, mask_wide = head_mask(lat_rows, LOW), head_mask(lat_rows, WIDE)
        out_ref[0, :patches, :half_width] = jnp.zeros((patches, half_width), LOW)
        for part in range(groups):
            columns = slice(part * chunk, (part + 1) * chunk)
            q = tile_heads(query_ref[0, :, columns], mask_low)
            d = tile_heads(d_ref[0, :, columns], mask_low)
            k = keyval_ref[0, :, columns]
            v = keyval_ref[0, :, half_width + part * chunk : half_width + (part + 1) * chunk]
            p = probs_ref[0, part]
            d_probs = dot(d, v, ((1,), (1,)))
            d_value = dot(p.astype(LOW), d, ((0,), (0,)))
            delta = jnp.sum(p * d_probs, axis=1, keepdims=True)
            d_scores = (p * (d_probs - delta)).astype(LOW)
            d_query = untile_heads(jnp.dot(d_scores, k, preferred_element_type=WIDE), mask_wide)
            d_key = dot(d_scores, q, ((0,), (0,)))
            out_ref[0, patches:, columns] = (d_query * scale).astype(LOW)
            out_ref[0, :, half_width + part * chunk : half_width + (part + 1) * chunk] = (
                d_key * scale
            ).astype(LOW)
            out_ref[0, :, 2 * half_width + part * chunk : 2 * half_width + (part + 1) * chunk] = (
                d_value.astype(LOW)
            )

    def slotted(*block):
        return pl.BlockSpec((1, *block), lambda i: (i,) + (0,) * len(block))

    return pl.pallas_call(
        kernel,
        grid=(slots,),
        out_shape=jax.ShapeDtypeStruct((slots, key_rows, 3 * half_width), LOW),
        in_specs=[
            slotted(lat_rows, half_width),
            slotted(lat_rows, half_width),
            slotted(key_rows, 2 * half_width),
            slotted(groups, PACK * lat_rows, key_rows),
        ],
        out_specs=slotted(key_rows, 3 * half_width),
        compiler_params=pltpu.CompilerParams(vmem_limit_bytes=32 * 2**20),
        cost_estimate=BRIEF,
    )(d_mixed, query, keyval, probs)


def on_device(
    wires,
    media,
    latents,
    upstream,
    time_index,
    live_count,
    time_table,
    media_gain,
    media_bias,
    latent_gain,
    latent_bias,
    ff_gain,
    ff_bias,
    w_query,
    w_keyval,
    w_out,
    w_up,
    w_down,
):
    wires.place()
    deep, flat, count = wires.deep, wires.flat, wires.count
    images, patches, model_width = media.shape
    lat_rows = latents.shape[1]
    key_rows = patches + lat_rows
    table_rows, shard = time_table.shape
    group = model_width // (2 * deep)
    half_width = model_width // 2
    slots = 2 * images

    qkv_mine, qkv_other = deal_columns(wires.c, (w_query, w_keyval), group)
    qkv_arrived = wires.send(qkv_other, "core")
    raw = jnp.concatenate([after(media, qkv_other), latents], axis=1)
    far_raw = wires.send(raw, "core")
    qkv_block = pair(qkv_mine, qkv_arrived, wires.c, 0)

    unit = w_down.shape[0]
    hidden_units = deep * unit
    tall, wide = 2 * shard, 3 * half_width
    folds = model_width // hidden_units
    ring_block = jnp.concatenate(
        [qkv_block.reshape(tall, wide), jnp.pad(w_out, ((0, 0), (0, wide - model_width)))]
    )
    smalls = jnp.concatenate(
        [time_table]
        + [v[None] for v in (media_gain, media_bias, latent_gain, latent_bias, ff_gain, ff_bias)],
        axis=0,
    )
    smalls = jnp.broadcast_to(smalls[None], (count, *smalls.shape))
    made = {}

    made["smalls"] = lax.all_to_all(smalls, AXES, 0, 0, tiled=True)

    def swap_up(first):
        shares = split_units(after(w_up, made["smalls"], first[wires.bits[-1]]), 2 * flat, unit)
        up_block = wires.swap_blocks(shares, wires.planes).reshape(-1, hidden_units)
        block = jnp.concatenate([w_down, fold_up(up_block, folds)])
        made["ffn"] = jnp.broadcast_to(block[None], (deep, *block.shape))
        return (made["ffn"],)

    d_out_low = after(upstream, qkv_other) * (jnp.arange(images) < live_count[0]).astype(LOW)[:, None, None]
    rings, gathered, d_out_got, steps = gather_rows(
        wires,
        ring_block,
        lambda block: block[:tall].reshape(2, shard, wide),
        after(d_out_low, made["smalls"]),
        {2: swap_up},
        (far_raw,),
    )
    places, pieces = [], []
    for step, got in enumerate(gathered):
        for mask, part in got.items():
            pieces += part if isinstance(part, tuple) else [part]
            for core in range(2):
                places.append((wires.plane(step) * 2 + core) * flat + (wires.f ^ mask))
    out_column = [ring[tall:, :model_width] for ring in rings]
    for mask in wires.masks:
        if mask not in d_out_got:
            d_out_got[mask] = wires.send(d_out_low, mask, *steps[-1])


    ffn_blocks = wires.swap_blocks(after(made["ffn"], rings[-1]), wires.columns)

    smalls = after(made["smalls"], *steps[-2][-1:])
    smalls = smalls.transpose(1, 0, 2).reshape(-1, model_width).astype(WIDE)
    norm_params = smalls[table_rows : table_rows + 4]
    ff_params = smalls[table_rows + 4 :]
    live_mask = (jnp.arange(images) < live_count[0]).astype(WIDE)[:, None, None]
    one_hot = (time_index[:, None] == jnp.arange(table_rows)[None, :]).astype(WIDE)
    time_rows = jnp.dot(one_hot, smalls[:table_rows], precision=HIGHEST)
    both_rows = jnp.concatenate([time_rows, wires.send(time_rows, "core")])

    out_places, out_pieces = [], []
    for mask, part in spread_plane(wires, jnp.stack(out_column), *steps[-1]).items():
        out_pieces.append(part)
        for step in range(deep):
            out_places.append(wires.plane(step) * flat + (wires.f ^ mask))


    qkv_full, sources, query, keyval, probs, mixed = attend(
        places,
        pieces,
        raw,
        far_raw,
        both_rows,
        norm_params,
        patches,
        half_width,
    )
    out_full, branch = project_out(
        out_places, out_pieces, after(mixed, *d_out_got.values()), model_width
    )
    branch = branch[:images] + wires.send(branch[images:], "core")
    middle = latents.astype(WIDE) + branch

    ffn_normed, ffn_norm_back = jax.vjp(norm_rows, middle, ff_params[0], ff_params[1])
    d_out = upstream.astype(WIDE) * live_mask

    def swapped(blocks, *ahead):
        mine = jnp.stack(blocks)
        far = wires.send(mine, "core", *ahead)
        return mine.reshape(-1, model_width), far.reshape(-1, model_width)

    ffn_low = ffn_normed.astype(LOW)
    ffn_got = spread_plane(wires, ffn_low)
    d_out_got = {mask: after(part, ffn_low) for mask, part in d_out_got.items()}
    order = [0, *wires.masks]
    d_out_rows = swapped([d_out_got[mask] for mask in order])
    ffn_rows = swapped([ffn_got[mask] for mask in order])
    hidden, d_pre, d_inputs, results = ffn_rows_back(
        ffn_blocks, ffn_rows, d_out_rows, unit
    )
    block_shape = (images, lat_rows, model_width)

    def collect_core(parts, *ahead):
        arrived = wires.send(parts[1], "core", *ahead)
        rows = (parts[0] + arrived.astype(WIDE)).reshape(len(order), *block_shape)
        return dict(zip(order, rows, strict=True)), arrived

    d_sums, d_swapped = collect_core(d_inputs)
    ffn_partial = ffn_outer(
        ffn_rows, d_out_rows, hidden, (after(d_pre[0], d_swapped), d_pre[1]), deep, unit
    )
    ffn_terms = wires.swap_blocks(ffn_partial, wires.columns)
    d_ffn_input, _ = sum_plane(wires, d_sums.get)
    d_ffn_input = after(d_ffn_input, ffn_partial)
    d_middle_norm, ff_gain_grad, ff_bias_grad = ffn_norm_back(d_ffn_input)
    d_middle = d_out + d_middle_norm

    own_branch = d_middle.astype(LOW)
    d_branch = jnp.concatenate([own_branch, wires.send(own_branch, "core")], axis=0)
    out_partial = outer(mixed.reshape(-1, half_width), d_branch.reshape(-1, model_width))
    out_partial = out_partial.astype(LOW).reshape(deep, flat, shard, model_width)
    out_partial = jnp.stack([out_partial[..., :half_width], out_partial[..., half_width:]], axis=2)
    d_mixed = rows_back(after(d_branch, out_partial), out_full).astype(LOW)
    d_projected = attend_back(d_mixed, query, keyval, probs)

    source_rows = sources.reshape(-1, model_width)
    d_projected_rows = d_projected.reshape(-1, wide)
    plane_rows = 2 * flat * shard

    kept = {}

    def results_clock(*ahead):
        result_sums, arrived = collect_core(results, *ahead)
        kept["own"] = result_sums[0]
        kept["low"] = {mask: rows.astype(LOW) for mask, rows in result_sums.items()}
        return arrived

    def far_back(clock):
        kept["far"] = rows_back(after(d_projected, clock)[images:], qkv_full).astype(LOW)
        d_rows = after(d_projected_rows, clock)
        for step in range(1, deep):
            partials[step] = partial_rows(step, d_rows)
        return (kept["far"], partials[1][0], *kept["low"].values())

    def far_clock(*ahead):
        kept["far"] = wires.send(kept["far"], "core", *ahead)
        return kept["far"]

    def norms_back(arrived):
        media_grad, latent_grad, sums = sources_back(
            after(d_projected[:images], arrived),
            qkv_full,
            kept["far"],
            raw,
            time_rows,
            norm_params,
            d_middle,
        )
        table_part = jnp.dot(one_hot.T, sums[:, 0], precision=HIGHEST)
        small_grads = [table_part, jnp.sum(sums[:, 1:5], axis=0), ff_gain_grad[None], ff_bias_grad[None]]
        small_grads = jnp.concatenate(small_grads).reshape(-1, count, shard).transpose(1, 0, 2)
        kept["media"], kept["latent"], kept["small"] = media_grad, latent_grad, small_grads
        return media_grad, small_grads

    def last_pull(_):
        ffn_sum = jnp.sum(ffn_terms.astype(WIDE), axis=0)
        kept["down"] = ffn_sum[:unit]
        up_sum = unfold_up(ffn_sum[unit:].astype(LOW), folds)
        kept["up"] = up_sum.reshape(2 * flat, shard, hidden_units)
        return (kept["up"],)

    result_got = []

    def send_result(mask):
        def ride(ahead):
            result_got.append(wires.send(kept["low"][mask], mask, *ahead))
            return result_got[-1]

        return ride

    turning = [mask for mask in wires.masks if mask & (mask - 1)]
    riders = {
        deep + 1: [send_result(mask) for mask in (*wires.bits, *turning)],
    }

    def partial_rows(step, d_rows):
        at_plane = wires.plane(1 + step)
        rows = lax.dynamic_slice_in_dim(source_rows, at_plane * plane_rows, plane_rows, 1)
        block = outer(rows, d_rows).astype(LOW).reshape(2, flat, shard, wide)
        return block, at(out_partial, at_plane, 0)

    partials = {0: partial_rows(0, d_projected_rows)}

    def part(step, mask):
        block, out_block = partials[step]
        target = wires.f ^ mask
        return jnp.concatenate([at(block, target, 1), at(out_block, target, 0)], axis=-1)

    total = scatter_rows(
        wires,
        part,
        {
            1: far_back,
            3: norms_back,
            4: last_pull,
        },
        riders,
        {0: results_clock, 2: far_clock},
    )
    qkv_sum = total[..., :wide]
    w_out_grad = jnp.concatenate([total[0, :, wide:], total[1, :, wide:]], axis=-1)
    media_grad, latent_grad = kept["media"], kept["latent"]
    w_down_grad = kept["down"]
    up_sum = wires.swap_blocks(kept["up"], wires.planes)
    w_up_grad = merge_units(after(up_sum, result_got[0]), unit)
    small_grads = lax.all_to_all(after(kept["small"], up_sum, result_got[0]), AXES, 0, 0, tiled=True)
    small_grads = jnp.sum(small_grads, axis=0)
    own_result = sum([rows.astype(WIDE) for rows in result_got], kept["own"])
    latents_out = ((middle + own_result) * live_mask).astype(LOW)
    qkv_own = pick(qkv_sum, wires.c, 0)
    qkv_far = wires.send(pick(qkv_sum, 1 - wires.c, 0), "core", small_grads)
    w_query_grad, w_keyval_grad = join_columns(
        wires.c, qkv_own, qkv_far, (model_width, 2 * model_width), group
    )
    return (
        latents_out,
        media_grad,
        latent_grad,
        small_grads[:table_rows],
        *[small_grads[table_rows + k] for k in range(6)],
        w_query_grad,
        w_keyval_grad,
        w_out_grad,
        w_up_grad,
        w_down_grad,
    )


def solution(mesh):
    lead = P(AXES)
    table = P(None, AXES)
    return jax.shard_map(
        functools.partial(on_device, Wires(mesh)),
        mesh=mesh,
        in_specs=(lead,) * 5 + (table,) + (lead,) * 11,
        out_specs=(lead,) * 3 + (table,) + (lead,) * 11,
        check_vma=False,
    )
```
